32 devices in a mesh: ctx: 16 (over z, x, core), dp: 2 (over y).
Axes of the slice: x: 2, y: 2, z: 4, core: 2. Of those that a mesh axis runs over, the one named last changes fastest.
Arguments:
- queries: bfloat16 [4096, 4096], P(('dp', 'ctx')), parts along dimension 0, may hold values from -16 to 16
- key_rows: bfloat16 [4096, 4096], P(('dp', 'ctx')), parts along dimension 0, may hold values from -16 to 16
- value_rows: bfloat16 [4096, 4096], P(('dp', 'ctx')), parts along dimension 0, may hold values from -6 to 6
- lengths: int32 [20], P('dp'), parts along dimension 0, may hold values from 1 to 256, 2048 in all
- norm_gain: float32 [4096], replicated, may hold values from 0.1 to 1.9
- filters: bfloat16 [256, 128], replicated, may hold values from -0.5 to 0.5
- bypass: float32 [4096], replicated, may hold values from -4 to 4
Outputs:
- mixed: bfloat16 [4096, 4096], P(('dp', 'ctx')), parts along dimension 0
The draws below stay inside these ranges and needn't reach their ends.
There are 2 independent parts, one for each index of `dp`. The reference program is written for one: setup_inputs(seed, part) draws one part's arguments, and reference() takes and returns one part's arrays. A program takes and returns all parts, laid end to end along the dimension named above; an argument that names none is the same for every part. Nothing has to cross between parts.
Inputs may be any that keep to these rules, and one draw needn't show every extreme that they name: The lengths sum to 2048; one of them is exactly 256.
All inputs are finite; a program needn't handle non-finite values.
Results may differ from the reference program's by a relative error of at most 0.012.
Values may be sent and summed in bfloat16 or wider, within the bound.
No kernel may reach another device: no remote copies, remote signals or barrier semaphores. Data moves between devices by JAX's collectives and lax.ppermute only.
A program may use at most 64 MiB of HBM per device.

```python
import math
import jax
import jax.numpy as jnp
import numpy as np
from jax import lax

TOK_DEV = 128
HEADS = 32
HEAD_DIM = 128
TAPS = 128
CHANNELS = 4096
GROUPS = 256
DOC_MOST = 256
SEQ = 2048
NDOCS = 10


def draw_queries(key, part):
    drawn = jnp.clip(jax.random.normal(jax.random.fold_in(key, 1), (SEQ, HEADS * HEAD_DIM), jnp.float32), -6.0, 6.0)
    return drawn.astype(jnp.bfloat16)


def draw_key_rows(key, part):
    drawn = jnp.clip(jax.random.normal(jax.random.fold_in(key, 2), (SEQ, HEADS * HEAD_DIM), jnp.float32), -6.0, 6.0)
    return drawn.astype(jnp.bfloat16)


def shard_levels(rng, shape, cuts, low, top_value):
    factor_of = 1.0
    for dim, shards_of in cuts:
        steps = jax.random.uniform(jax.random.fold_in(jax.random.fold_in(rng, 6), dim), (shards_of,), jnp.float32, low / len(cuts), top_value / len(cuts))
        factor_of = factor_of * jnp.repeat(jnp.exp(steps), shape[dim] // shards_of).reshape((-1,) + (1,) * (len(shape) - 1 - dim))
    return factor_of


def length_profile(count, total, bound, skew):
    portions = [(1 << 20) // math.isqrt(grade ** skew) + 1 for grade in range(2, count + 1)]
    rest, holding = total - bound - (count - 1), [1] * (count - 1)
    while rest > 0:
        candidates = [i for i in range(count - 1) if holding[i] < bound]
        pool, budget = sum([portions[i] for i in candidates]), rest
        for i in candidates:
            more = min(bound - holding[i], max(1, budget * portions[i] // pool), rest)
            holding[i] = holding[i] + more
            rest = rest - more
    return np.array([bound] + holding)


def uneven_parts(key, number_of, total, most, lean):
    if number_of == 2:
        one = jax.random.randint(key, (), max(1, total - most), min(most, total - 1) + 1)
        return jnp.stack([one, total - one])
    sizes = jnp.asarray(length_profile(number_of, total, most, lean), jnp.int32)
    pairs = (number_of - 1) // 2
    donor, taker = sizes[1:1 + 2 * pairs:2], sizes[2:2 + 2 * pairs:2]
    slack = jnp.minimum(donor - 1, most - taker)
    moved = jax.random.randint(jax.random.fold_in(key, 1), (pairs,), 0, 1 << 20) % (slack + 1)
    sizes = sizes.at[1:1 + 2 * pairs:2].set(donor - moved).at[2:2 + 2 * pairs:2].set(taker + moved)
    return sizes[jax.random.permutation(jax.random.fold_in(key, 2), number_of)]


def normal_values(rng, dims, scale, reach, shards=(), kind=jnp.bfloat16):
    array = jax.random.normal(rng, dims, jnp.float32) * scale
    if len(shards) > 0:
        array = shard_levels(rng, dims, shards, -0.22, 0.18) * array
    return jnp.clip(array, min=-reach, max=reach).astype(kind)


def setup_inputs(seed: int = 0, part: int = 0) -> dict:
    arg_keys = jax.random.split(jax.random.key(seed), 8)
    part_splits = jax.random.split(jax.random.fold_in(arg_keys[7], part), 8)
    queries = draw_queries(jax.random.fold_in(jax.random.fold_in(arg_keys[7], part), 71), part)
    key_rows = draw_key_rows(jax.random.fold_in(jax.random.fold_in(arg_keys[7], part), 71), part)
    value_rows = normal_values(part_splits[2], (SEQ, CHANNELS), 1.0, 6.0, ((0, 16),))
    lengths = uneven_parts(part_splits[3], NDOCS, SEQ, DOC_MOST, 2).astype(jnp.int32)
    norm_gain = jnp.clip(1.0 + 0.18 * jax.random.normal(arg_keys[4], (CHANNELS,), jnp.float32), 0.1, 1.9)
    filters = normal_values(arg_keys[5], (GROUPS, TAPS), TAPS ** -0.5, 0.5)
    bypass = normal_values(arg_keys[6], (CHANNELS,), 1.0, 4.0, (), jnp.float32)
    return {"queries": queries, "key_rows": key_rows, "value_rows": value_rows, "lengths": lengths, "norm_gain": norm_gain, "filters": filters, "bypass": bypass}


def starts_of(lengths, count):
    ends = jnp.cumsum(lengths).astype(jnp.int32)
    position = jnp.arange(count, dtype=jnp.int32)
    passed = ends[None, :] <= position[:, None]
    return lax.optimization_barrier(jnp.sum(jnp.where(passed, lengths[None, :], 0), axis=1)).astype(jnp.int32)

def reference(queries, key_rows, value_rows, lengths, norm_gain, filters, bypass):
    seq_len = queries.shape[0]
    width = queries.shape[1]
    heads = width // HEAD_DIM
    starts = starts_of(lengths, seq_len)
    key_padded = jnp.concatenate([jnp.zeros((DOC_MOST, width), key_rows.dtype), key_rows], axis=0)
    value_padded = jnp.concatenate([jnp.zeros((DOC_MOST, width), value_rows.dtype), value_rows], axis=0)
    scale = 1.0 / math.sqrt(HEAD_DIM)

    def attend_block(block):
        begin = (block * TOK_DEV).astype(jnp.int32)
        query_part = lax.dynamic_slice_in_dim(queries, begin, TOK_DEV, 0).astype(jnp.float32)
        key_part = lax.dynamic_slice_in_dim(key_padded, begin, TOK_DEV + DOC_MOST, 0).astype(jnp.float32)
        value_part = lax.dynamic_slice_in_dim(value_padded, begin, TOK_DEV + DOC_MOST, 0).astype(jnp.float32)
        start_part = lax.dynamic_slice_in_dim(starts, begin, TOK_DEV, 0)
        query_heads = query_part.reshape(TOK_DEV, heads, HEAD_DIM)
        key_heads = key_part.reshape(TOK_DEV + DOC_MOST, heads, HEAD_DIM)
        value_heads = value_part.reshape(TOK_DEV + DOC_MOST, heads, HEAD_DIM)
        scores = jnp.einsum('thd,uhd->htu', query_heads, key_heads) * scale
        query_pos = begin + jnp.arange(TOK_DEV, dtype=jnp.int32)
        key_pos = begin - DOC_MOST + jnp.arange(TOK_DEV + DOC_MOST, dtype=jnp.int32)
        valid = (key_pos[None, :] >= start_part[:, None]) & (key_pos[None, :] <= query_pos[:, None])
        scores = jnp.where(valid[None], scores, jnp.float32(-1e+30))
        top = lax.optimization_barrier(jnp.max(scores, axis=2, keepdims=True))
        raised = jnp.where(valid[None], jnp.exp(scores - top), jnp.float32(0.0))
        weights = (raised / lax.optimization_barrier(jnp.sum(raised, axis=2, keepdims=True))).astype(jnp.bfloat16)
        result = jnp.einsum('htu,uhd->thd', weights.astype(jnp.float32), value_heads)
        return result.astype(jnp.bfloat16).reshape(TOK_DEV, width)
    blocks = seq_len // TOK_DEV
    attended = lax.map(attend_block, jnp.arange(blocks, dtype=jnp.int32)).reshape(seq_len, width)
    attended32 = attended.astype(jnp.float32)
    squares = lax.optimization_barrier(jnp.mean(attended32 * attended32, axis=1, keepdims=True))
    normed = (attended32 * lax.rsqrt(squares + 1e-06) * norm_gain[None, :]).astype(jnp.bfloat16)
    normed32 = normed.astype(jnp.float32)
    group_size = width // filters.shape[0]
    channel_filters = jnp.repeat(filters.astype(jnp.float32), group_size, axis=0).T
    normed_padded = jnp.concatenate([jnp.zeros((TAPS - 1, width), jnp.float32), normed32], axis=0)

    def conv_block(block):
        begin = (block * TOK_DEV).astype(jnp.int32)
        window = lax.dynamic_slice_in_dim(normed_padded, begin, TOK_DEV + TAPS - 1, 0)
        position = begin + jnp.arange(TOK_DEV, dtype=jnp.int32)
        start_part = lax.dynamic_slice_in_dim(starts, begin, TOK_DEV, 0)

        def add_tap(tap, total):
            tap = jnp.asarray(tap).astype(jnp.int32)
            offset = (TAPS - 1 - tap).astype(jnp.int32)
            piece = lax.dynamic_slice_in_dim(window, offset, TOK_DEV, 0)
            coeff = lax.dynamic_slice_in_dim(channel_filters, tap, 1, 0)
            allowed = (position - tap >= start_part)[:, None]
            return total + jnp.where(allowed, piece * coeff, jnp.float32(0.0))
        return lax.fori_loop(0, TAPS, add_tap, jnp.zeros((TOK_DEV, width), jnp.float32))
    convolved = lax.map(conv_block, jnp.arange(blocks, dtype=jnp.int32)).reshape(seq_len, width)
    return (convolved + bypass[None, :] * normed32).astype(jnp.bfloat16)
```

```python
import math

import jax
import jax.numpy as jnp
from jax import lax
from jax.experimental import pallas as pl
from jax.experimental.pallas import tpu as pltpu
from jax.sharding import PartitionSpec as P

HEAD_DIM = 128
LANES = 128
NEG = -1e30


def permuted(x, pairs):
    return lax.ppermute(x, "ctx", pairs)


def local_starts(lengths, first_row, count):
    ends = jnp.cumsum(lengths)
    position = first_row + jnp.arange(count, dtype=jnp.int32)
    passed = ends[None, :] <= position[:, None]
    return jnp.sum(jnp.where(passed, lengths[None, :], 0), axis=1) - first_row


def weights_kernel(heads, odd_ref, st_ref, qp_ref, q_ref, ka_ref, kb_ref, kn_ref, ko_ref, own_ref, prev_ref, bias_own, bias_prev):
    rows = q_ref.shape[0]

    @pl.when(pl.program_id(0) == 0)
    def _():
        st = st_ref[...]
        row = lax.broadcasted_iota(jnp.int32, (rows, 3 * rows), 0)
        key = lax.broadcasted_iota(jnp.int32, (rows, 3 * rows), 1) - 2 * rows
        bias_own[...] = jnp.where((key >= st) & (key <= row), 0.0, NEG)
        row = lax.broadcasted_iota(jnp.int32, (rows, 2 * rows), 0) - rows
        key = lax.broadcasted_iota(jnp.int32, (rows, 2 * rows), 1) - 2 * rows
        bias_prev[...] = jnp.where((key >= st[0:1, :]) & (key <= row), 0.0, NEG)

    odd = odd_ref[0] == 1
    factor = 1.0 / math.sqrt(HEAD_DIM) * math.log2(math.e)
    dims = (((1,), (1,)), ((), ()))
    for h in range(heads):
        cols = slice(h * HEAD_DIM, (h + 1) * HEAD_DIM)
        kf = jnp.where(odd, kb_ref[:, cols], ka_ref[:, cols])
        kfn = jnp.concatenate([kf, kn_ref[:, cols]], axis=0)
        kfno = jnp.concatenate([kfn, ko_ref[:, cols]], axis=0)
        s = lax.dot_general(q_ref[:, cols], kfno, dims, preferred_element_type=jnp.float32) + bias_own[...]
        s = (s - jnp.max(s, axis=1, keepdims=True)) * factor
        own_ref[h] = jnp.exp2(s).astype(jnp.bfloat16)
        s = lax.dot_general(qp_ref[:, cols], kfn, dims, preferred_element_type=jnp.float32) + bias_prev[...]
        s = (s - jnp.max(s, axis=1, keepdims=True)) * factor
        prev_ref[h] = jnp.exp2(s).astype(jnp.bfloat16)


def finish_kernel(heads, a_steps, odd_ref, st_ref, own_ref, prev_ref, va_ref, vb_ref, vn_ref, vo_ref, taps_ref, gain_ref, bypass_ref, out_ref, att, squares, scale, keep, lhs):
    rows = st_ref.shape[0]
    step = pl.program_id(0)
    all_heads = att.shape[0]
    width = all_heads * LANES

    @pl.when(step == 0)
    def _():
        squares[...] = jnp.zeros_like(squares)
        st = st_ref[...]
        row = lax.broadcasted_iota(jnp.int32, (rows, 2 * rows), 0)
        key = lax.broadcasted_iota(jnp.int32, (rows, 2 * rows), 1) - rows
        keep[...] = jnp.where((key >= st) & (key <= row) & (key > row - rows), 1.0, 0.0).astype(jnp.bfloat16)

    @pl.when(step < a_steps)
    def _():
        odd = odd_ref[0] == 1
        ones = jnp.ones((3 * rows, LANES), jnp.bfloat16)
        for h in range(heads):
            cols = slice(h * HEAD_DIM, (h + 1) * HEAD_DIM)
            vf = jnp.where(odd, vb_ref[:, cols], va_ref[:, cols])
            values = jnp.concatenate([vf, vn_ref[:, cols], vo_ref[:, cols]], axis=0)
            values = jnp.concatenate([values, ones], axis=1)
            o = jnp.dot(prev_ref[h], values[: 2 * rows], preferred_element_type=jnp.float32)
            a = (o[:, :LANES] / o[:, LANES:]).astype(jnp.bfloat16)
            att[step * heads + h, :rows] = a
            a = a.astype(jnp.float32)
            squares[:rows] += a * a
            o = jnp.dot(own_ref[h], values, preferred_element_type=jnp.float32)
            a = (o[:, :LANES] / o[:, LANES:]).astype(jnp.bfloat16)
            att[step * heads + h, rows:] = a
            a = a.astype(jnp.float32)
            squares[rows:] += a * a

    @pl.when(step == a_steps)
    def _():
        total = jnp.sum(squares[...], axis=1, keepdims=True)
        scale[...] = jnp.broadcast_to(lax.rsqrt(total * (1.0 / width) + 1e-06), scale.shape)

    @pl.when(step >= a_steps)
    def _():
        tiles = out_ref.shape[1] // LANES
        groups = taps_ref.shape[0] // tiles
        size = LANES // groups
        lane_group = lax.broadcasted_iota(jnp.int32, (rows, LANES), 1) // size
        first = (step - a_steps) * tiles
        for c in range(tiles):
            cols = slice(c * LANES, (c + 1) * LANES)
            x = att[first + c].astype(jnp.float32) * scale[...] * gain_ref[:, cols]
            x = x.astype(jnp.bfloat16)
            for g in range(groups):
                line = jnp.broadcast_to(taps_ref[c * groups + g : c * groups + g + 1, :], (rows, LANES))
                ring = pltpu.roll(line, 0, 1, stride=1, stride_axis=0).astype(jnp.bfloat16)
                lhs[c % 2, g * rows : (g + 1) * rows, :LANES] = ring * keep[:, :LANES]
                lhs[c % 2, g * rows : (g + 1) * rows, LANES:] = ring * keep[:, LANES:]
            y = jnp.dot(lhs[c % 2], x, preferred_element_type=jnp.float32)
            total = bypass_ref[:, cols] * x[rows:].astype(jnp.float32)
            picked = y[:rows]
            for g in range(1, groups):
                picked = jnp.where(lane_group == g, y[g * rows : (g + 1) * rows], picked)
            out_ref[:, cols] = (total + picked).astype(jnp.bfloat16)


def shards(queries, key_rows, value_rows, lengths, norm_gain, filters, bypass):
    rows, width = queries.shape
    heads = width // HEAD_DIM
    groups, taps = filters.shape
    n = lax.axis_size("ctx")
    me = lax.axis_index("ctx")
    odd = (me % 2).astype(jnp.int32).reshape(1)
    st = local_starts(lengths, me * rows, rows).astype(jnp.int32).reshape(rows, 1)

    ahead = [(i, i + 1) for i in range(n - 1)]
    skip = [(i, i + 2) for i in range(0, n - 2, 2)]
    within = [(i, i + 1) for i in range(0, n - 1, 2)]

    key_near = permuted(key_rows, ahead)
    key_skip = permuted(key_rows, skip)
    query_near = permuted(queries, ahead)
    key_within = permuted(key_near, within)
    value_near = permuted(value_rows, ahead)
    value_skip = permuted(value_rows, skip)
    value_within = permuted(value_near, within)

    hb = 4
    cols = hb * HEAD_DIM
    rowspec = pl.BlockSpec((rows, cols), lambda i: (0, i))
    smem = pl.BlockSpec(memory_space=pltpu.SMEM)
    stspec = pl.BlockSpec((rows, 1), lambda i: (0, 0))
    own, prev = pl.pallas_call(
        lambda *refs: weights_kernel(hb, *refs),
        grid=(heads // hb,),
        out_shape=(
            jax.ShapeDtypeStruct((heads, rows, 3 * rows), jnp.bfloat16),
            jax.ShapeDtypeStruct((heads, rows, 2 * rows), jnp.bfloat16),
        ),
        in_specs=[smem, stspec] + [rowspec] * 6,
        out_specs=(
            pl.BlockSpec((hb, rows, 3 * rows), lambda i: (i, 0, 0)),
            pl.BlockSpec((hb, rows, 2 * rows), lambda i: (i, 0, 0)),
        ),
        scratch_shapes=[pltpu.VMEM((rows, 3 * rows), jnp.float32), pltpu.VMEM((rows, 2 * rows), jnp.float32)],
        compiler_params=pltpu.CompilerParams(vmem_limit_bytes=40 * 2**20),
        cost_estimate=pl.CostEstimate(flops=2 * 5 * rows * rows * width, bytes_accessed=16 * 2**20, transcendentals=0),
        name="weights",
    )(odd, st, query_near, queries, key_skip, key_within, key_near, key_rows)

    mirrored = jnp.roll(filters[:, ::-1], 1, axis=1).astype(jnp.float32)
    ab = 8
    a_steps = heads // ab
    bt = 4
    b_steps = width // (bt * LANES)
    per_tile = groups // (width // LANES)
    clamp_a = lambda i: jnp.minimum(i, a_steps - 1)
    clamp_b = lambda i: jnp.maximum(i - a_steps, 0)
    vspec = pl.BlockSpec((rows, ab * HEAD_DIM), lambda i: (0, clamp_a(i)))
    lane = pl.BlockSpec((1, bt * LANES), lambda i: (0, clamp_b(i)))
    return pl.pallas_call(
        lambda *refs: finish_kernel(ab, a_steps, *refs),
        grid=(a_steps + b_steps,),
        out_shape=jax.ShapeDtypeStruct((rows, width), jnp.bfloat16),
        in_specs=[
            smem,
            stspec,
            pl.BlockSpec((ab, rows, 3 * rows), lambda i: (clamp_a(i), 0, 0)),
            pl.BlockSpec((ab, rows, 2 * rows), lambda i: (clamp_a(i), 0, 0)),
            vspec,
            vspec,
            vspec,
            vspec,
            pl.BlockSpec((bt * per_tile, taps), lambda i: (clamp_b(i), 0)),
            lane,
            lane,
        ],
        out_specs=pl.BlockSpec((rows, bt * LANES), lambda i: (0, clamp_b(i))),
        scratch_shapes=[
            pltpu.VMEM((width // LANES, 2 * rows, LANES), jnp.bfloat16),
            pltpu.VMEM((2 * rows, LANES), jnp.float32),
            pltpu.VMEM((2 * rows, LANES), jnp.float32),
            pltpu.VMEM((rows, 2 * rows), jnp.bfloat16),
            pltpu.VMEM((2, per_tile * rows, 2 * rows), jnp.bfloat16),
        ],
        compiler_params=pltpu.CompilerParams(vmem_limit_bytes=40 * 2**20),
        cost_estimate=pl.CostEstimate(flops=2 * 5 * rows * rows * width, bytes_accessed=16 * 2**20, transcendentals=0),
        name="finish",
    )(odd, st, own, prev, value_skip, value_within, value_near, value_rows, mirrored, norm_gain.reshape(1, width), bypass.reshape(1, width))


def solution(mesh):
    rows = P(("dp", "ctx"), None)
    in_specs = (rows, rows, rows, P("dp"), P(), P(), P())
    return jax.shard_map(shards, mesh=mesh, in_specs=in_specs, out_specs=rows, check_vma=False)
```

```python
import math

import jax
import jax.numpy as jnp
from jax import lax
from jax.experimental import pallas as pl
from jax.experimental.pallas import tpu as pltpu
from jax.sharding import PartitionSpec as P

HEAD_DIM = 128
LANES = 128
NEG = -1e30
FACTOR = 1.0 / math.sqrt(HEAD_DIM) * math.log2(math.e)
CONTRACT_LAST = (((1,), (1,)), ((), ()))
VMEM_BYTES = 40 * 2**20

ODD, BEFORE, NEXT_BEFORE, NEXT_AFTER = range(4)


def permuted(x, pairs):
    return lax.ppermute(x, "ctx", pairs)


def after(x, *others):
    return lax.optimization_barrier((x, *others))[0]


def places(lengths, first_row, count):
    ends = jnp.cumsum(lengths)
    position = first_row + jnp.arange(count + 1, dtype=jnp.int32)
    passed = ends[None, :] <= position[:, None]
    starts = jnp.sum(jnp.where(passed, lengths[None, :], 0), axis=1) - first_row
    past = jnp.min(jnp.where(passed[count], jnp.int32(2**30), ends)) - first_row - count
    odd = (first_row // count) % 2
    facts = jnp.stack([odd, -starts[0], count - starts[count], past]).astype(jnp.int32)
    return starts[:count].astype(jnp.int32).reshape(count, 1), facts


def bias_of(rows, columns, row_first, key_first, start):
    row = lax.broadcasted_iota(jnp.int32, (rows, columns), 0) + row_first
    key = lax.broadcasted_iota(jnp.int32, (rows, columns), 1) + key_first
    return jnp.where((key >= start) & (key <= row), 0.0, NEG)


def scored(query, key, bias):
    s = lax.dot_general(query, key, CONTRACT_LAST, preferred_element_type=jnp.float32) + bias
    top = jnp.max(s, axis=1, keepdims=True)
    return jnp.exp2((s - top) * FACTOR).astype(jnp.bfloat16), top


def summed(weights, value):
    ones = jnp.ones(value.shape, jnp.bfloat16)
    o = jnp.dot(weights, jnp.concatenate([value, ones], axis=1), preferred_element_type=jnp.float32)
    return o[:, :LANES], o[:, LANES:]


def share_kernel(heads, facts_ref, qb_ref, q_ref, kn_ref, ko_ref, vn_ref, vo_ref, b_ref, stat_ref, c_ref, bias):
    rows = q_ref.shape[0]
    step = pl.program_id(0)
    before = facts_ref[NEXT_BEFORE]
    past = facts_ref[NEXT_AFTER]
    odd = facts_ref[ODD] == 1

    @pl.when(odd & (before <= rows))
    def _():
        b_ref[...] = vo_ref[...]
        c_ref[...] = q_ref[...]

    @pl.when(odd & (before > rows))
    def _():
        @pl.when(step == 0)
        def _():
            bias[:rows] = bias_of(rows, 2 * rows, rows, -rows, rows - before)
            bias[rows:] = bias_of(rows, 2 * rows, 0, -rows, rows - before)

        lane = lax.broadcasted_iota(jnp.int32, (rows, LANES), 1)
        ours = lax.broadcasted_iota(jnp.int32, (rows, LANES), 0) < past
        stat = stat_ref[...]
        for h in range(heads):
            cols = slice(h * HEAD_DIM, (h + 1) * HEAD_DIM)
            key = jnp.concatenate([kn_ref[:, cols], ko_ref[:, cols]], axis=0)
            value = jnp.concatenate([vn_ref[:, cols], vo_ref[:, cols]], axis=0)
            query = jnp.concatenate([qb_ref[:, cols], q_ref[:, cols]], axis=0)
            weights, top = scored(query, key, bias[...])
            o, l = summed(weights, value)
            o = (o / l).astype(jnp.bfloat16)
            b_ref[:, cols] = o[:rows]
            c_ref[:, cols] = o[rows:]
            lse = jnp.where(ours, top[:rows] * FACTOR + jnp.log2(l[:rows]), NEG)
            stat = jnp.where(lane == step * heads + h, lse, stat)
        stat_ref[...] = stat


def weights_kernel(heads, facts_ref, st_ref, q_ref, ko_ref, kp_ref, kf_ref, kn_ref, qn_ref, own_ref, prev_ref, top_ref, bias_own, bias_prev):
    rows = q_ref.shape[0]
    step = pl.program_id(0)
    odd = facts_ref[ODD] == 1

    @pl.when(step == 0)
    def _():
        low = jnp.where((facts_ref[ODD] == 0) & (facts_ref[BEFORE] > rows), 0, -(2**20))
        st = jnp.maximum(st_ref[...], low)
        bias_own[...] = bias_of(rows, 3 * rows, 0, -2 * rows, st)
        bias_prev[...] = bias_of(rows, 2 * rows, -rows, -2 * rows, st_ref[0:1, :])

    @pl.when(odd)
    def _():
        for h in range(heads):
            cols = slice(h * HEAD_DIM, (h + 1) * HEAD_DIM)
            key = jnp.concatenate([kf_ref[:, cols], kn_ref[:, cols], ko_ref[:, cols]], axis=0)
            own_ref[h] = scored(q_ref[:, cols], key, bias_own[...])[0]
            prev_ref[h] = scored(qn_ref[:, cols], key[: 2 * rows], bias_prev[...])[0]

    @pl.when(jnp.logical_not(odd))
    def _():
        lane = lax.broadcasted_iota(jnp.int32, (rows, LANES), 1)
        tops = top_ref[...]
        for h in range(heads):
            cols = slice(h * HEAD_DIM, (h + 1) * HEAD_DIM)
            key = jnp.concatenate([kp_ref[:, cols], ko_ref[:, cols]], axis=0)
            weights, top = scored(q_ref[:, cols], key, bias_own[:, rows:])
            own_ref[h, :, rows:] = weights
            tops = jnp.where(lane == step * heads + h, top * FACTOR, tops)
        top_ref[...] = tops


def values_kernel(heads, facts_ref, own_ref, prev_ref, top_ref, stat_ref, vp_ref, vf_ref, vn_ref, vo_ref, att_ref, near_ref, sq_ref, sq_near_ref):
    rows = vo_ref.shape[0]
    step = pl.program_id(0)
    odd = facts_ref[ODD] == 1

    @pl.when(step == 0)
    def _():
        sq_ref[...] = jnp.zeros_like(sq_ref)
        sq_near_ref[...] = jnp.zeros_like(sq_near_ref)

    @pl.when(odd)
    def _():
        for h in range(heads):
            cols = slice(h * HEAD_DIM, (h + 1) * HEAD_DIM)
            value = jnp.concatenate([vf_ref[:, cols], vn_ref[:, cols], vo_ref[:, cols]], axis=0)
            o, l = summed(own_ref[h], value)
            a = (o / l).astype(jnp.bfloat16)
            att_ref[h] = a
            a = a.astype(jnp.float32)
            sq_ref[...] += a * a
            o, l = summed(prev_ref[h], value[: 2 * rows])
            a = (o / l).astype(jnp.bfloat16)
            near_ref[h] = a
            a = a.astype(jnp.float32)
            sq_near_ref[...] += a * a

    @pl.when(jnp.logical_not(odd))
    def _():
        lane = lax.broadcasted_iota(jnp.int32, (rows, LANES), 1)
        shared = facts_ref[BEFORE] > rows
        for h in range(heads):
            cols = slice(h * HEAD_DIM, (h + 1) * HEAD_DIM)
            value = jnp.concatenate([vp_ref[:, cols], vo_ref[:, cols]], axis=0)
            o, l = summed(own_ref[h, :, rows:], value)
            mine = lane == step * heads + h
            top = jnp.sum(jnp.where(mine, top_ref[...], 0.0), axis=1, keepdims=True)
            lse = jnp.sum(jnp.where(mine, stat_ref[...], 0.0), axis=1, keepdims=True)
            lse = jnp.where(shared, lse, NEG)
            high = jnp.maximum(top, lse)
            here = jnp.exp2(top - high)
            there = jnp.exp2(lse - high)
            o = o * here + vp_ref[:, cols].astype(jnp.float32) * there
            a = (o / (l * here + there)).astype(jnp.bfloat16)
            att_ref[h] = a
            a = a.astype(jnp.float32)
            sq_ref[...] += a * a


def finish_kernel(heads, a_steps, facts_ref, st_ref, kp_ref, vp_ref, c_ref, near_ref, sq_ref, sq_near_ref, att_ref, taps_ref, gain_ref, bypass_ref, out_ref, prev, squares, scale, keep, lhs, bias):
    rows = st_ref.shape[0]
    step = pl.program_id(0)
    width = prev.shape[0] * LANES
    odd = facts_ref[ODD] == 1
    shared = facts_ref[BEFORE] > rows

    @pl.when(step == 0)
    def _():
        squares[...] = sq_near_ref[...]
        st = st_ref[...]
        row = lax.broadcasted_iota(jnp.int32, (rows, 2 * rows), 0)
        key = lax.broadcasted_iota(jnp.int32, (rows, 2 * rows), 1) - rows
        keep[...] = jnp.where((key >= st) & (key <= row) & (key > row - rows), 1.0, 0.0).astype(jnp.bfloat16)
        bias[...] = bias_of(rows, rows, -rows, -rows, st[0:1, :])

    @pl.when((step < a_steps) & odd)
    def _():
        for h in range(heads):
            prev[step * heads + h] = near_ref[h]

    @pl.when((step < a_steps) & jnp.logical_not(odd) & shared)
    def _():
        for h in range(heads):
            a = c_ref[:, h * HEAD_DIM : (h + 1) * HEAD_DIM]
            prev[step * heads + h] = a
            a = a.astype(jnp.float32)
            squares[...] += a * a

    @pl.when((step < a_steps) & jnp.logical_not(odd) & jnp.logical_not(shared))
    def _():
        for h in range(heads):
            cols = slice(h * HEAD_DIM, (h + 1) * HEAD_DIM)
            weights, _ = scored(c_ref[:, cols], kp_ref[:, cols], bias[...])
            o, l = summed(weights, vp_ref[:, cols])
            a = (o / l).astype(jnp.bfloat16)
            prev[step * heads + h] = a
            a = a.astype(jnp.float32)
            squares[...] += a * a

    @pl.when(step == a_steps)
    def _():
        total = jnp.sum(squares[...], axis=1, keepdims=True)
        scale[:rows] = jnp.broadcast_to(lax.rsqrt(total * (1.0 / width) + 1e-06), squares.shape)
        total = jnp.sum(sq_ref[...], axis=1, keepdims=True)
        scale[rows:] = jnp.broadcast_to(lax.rsqrt(total * (1.0 / width) + 1e-06), squares.shape)

    @pl.when(step >= a_steps)
    def _():
        tiles = out_ref.shape[1] // LANES
        groups = taps_ref.shape[0] // tiles
        size = LANES // groups
        lane_group = lax.broadcasted_iota(jnp.int32, (rows, LANES), 1) // size
        first = (step - a_steps) * tiles
        for c in range(tiles):
            cols = slice(c * LANES, (c + 1) * LANES)
            x = jnp.concatenate([prev[first + c], att_ref[c]], axis=0)
            x = (x.astype(jnp.float32) * scale[...] * gain_ref[:, cols]).astype(jnp.bfloat16)
            for g in range(groups):
                line = jnp.broadcast_to(taps_ref[c * groups + g : c * groups + g + 1, :], (rows, LANES))
                ring = pltpu.roll(line, 0, 1, stride=1, stride_axis=0).astype(jnp.bfloat16)
                lhs[c % 2, g * rows : (g + 1) * rows, :LANES] = ring * keep[:, :LANES]
                lhs[c % 2, g * rows : (g + 1) * rows, LANES:] = ring * keep[:, LANES:]
            y = jnp.dot(lhs[c % 2], x, preferred_element_type=jnp.float32)
            total = bypass_ref[:, cols] * x[rows:].astype(jnp.float32)
            picked = y[:rows]
            for g in range(1, groups):
                picked = jnp.where(lane_group == g, y[g * rows : (g + 1) * rows], picked)
            out_ref[:, cols] = (total + picked).astype(jnp.bfloat16)


def params():
    return pltpu.CompilerParams(vmem_limit_bytes=VMEM_BYTES)


def shards(queries, key_rows, value_rows, lengths, norm_gain, filters, bypass):
    rows, width = queries.shape
    heads = width // HEAD_DIM
    groups, taps = filters.shape
    n = lax.axis_size("ctx")
    st, facts = places(lengths, lax.axis_index("ctx") * rows, rows)

    back = [(i, i - 1) for i in range(2, n, 2)]
    within = [(i, i + 1) for i in range(0, n - 1, 2)]
    across = [(i, i + 1) for i in range(1, n - 1, 2)]

    smem = pl.BlockSpec(memory_space=pltpu.SMEM)
    wide = jax.ShapeDtypeStruct((rows, width), jnp.bfloat16)
    stats = jax.ShapeDtypeStruct((rows, LANES), jnp.float32)
    whole = lambda shape: pl.BlockSpec(shape, lambda i: (0,) * len(shape))
    starts = whole((rows, 1))
    square = whole((rows, LANES))
    wide_bytes = rows * width * 2
    tile_flops = 4 * rows * rows * width

    query_back = permuted(queries, back)
    key_near = permuted(key_rows, within)
    value_near = permuted(value_rows, within)
    query_near = permuted(queries, within)
    key_across = permuted(after(key_rows, query_back), across)

    hb = 4
    block = pl.BlockSpec((rows, hb * HEAD_DIM), lambda i: (0, i))
    slot_b, stat, slot_c = pl.pallas_call(
        lambda *refs: share_kernel(hb, *refs),
        grid=(heads // hb,),
        out_shape=(wide, stats, wide),
        in_specs=[smem] + [block] * 6,
        out_specs=(block, square, block),
        scratch_shapes=[pltpu.VMEM((2 * rows, 2 * rows), jnp.float32)],
        compiler_params=params(),
        cost_estimate=pl.CostEstimate(flops=4 * tile_flops, bytes_accessed=8 * wide_bytes, transcendentals=0),
        name="share",
    )(facts, query_back, queries, key_near, key_rows, value_near, value_rows)

    stat_across = permuted(stat, across)
    b_across = permuted(slot_b, across)
    c_across = permuted(after(slot_c, key_across), across)
    key_far = permuted(key_across, within)

    own_spec = lambda size: pl.BlockSpec((size, rows, 3 * rows), lambda i: (i, 0, 0))
    prev_spec = lambda size: pl.BlockSpec((size, rows, 2 * rows), lambda i: (i, 0, 0))
    own, prev, tops = pl.pallas_call(
        lambda *refs: weights_kernel(hb, *refs),
        grid=(heads // hb,),
        out_shape=(
            jax.ShapeDtypeStruct((heads, rows, 3 * rows), jnp.bfloat16),
            jax.ShapeDtypeStruct((heads, rows, 2 * rows), jnp.bfloat16),
            stats,
        ),
        in_specs=[smem, starts] + [block] * 6,
        out_specs=(own_spec(hb), prev_spec(hb), square),
        scratch_shapes=[pltpu.VMEM((rows, 3 * rows), jnp.float32), pltpu.VMEM((rows, 2 * rows), jnp.float32)],
        compiler_params=params(),
        cost_estimate=pl.CostEstimate(flops=5 * tile_flops, bytes_accessed=11 * wide_bytes, transcendentals=0),
        name="weights",
    )(facts, st, queries, key_rows, key_across, key_far, key_near, query_near)

    value_far = permuted(after(b_across, own), within)

    att_shape = jax.ShapeDtypeStruct((heads, rows, HEAD_DIM), jnp.bfloat16)
    att_block = pl.BlockSpec((hb, rows, HEAD_DIM), lambda i: (i, 0, 0))
    att, near, squares, near_squares = pl.pallas_call(
        lambda *refs: values_kernel(hb, *refs),
        grid=(heads // hb,),
        out_shape=(att_shape, att_shape, stats, stats),
        in_specs=[smem, own_spec(hb), prev_spec(hb), square, square] + [block] * 4,
        out_specs=(att_block, att_block, square, square),
        compiler_params=params(),
        cost_estimate=pl.CostEstimate(flops=5 * tile_flops, bytes_accessed=11 * wide_bytes, transcendentals=0),
        name="values",
    )(facts, own, prev, tops, stat_across, b_across, value_far, value_near, value_rows)

    mirrored = jnp.roll(filters[:, ::-1], 1, axis=1).astype(jnp.float32)
    ab = 8
    a_steps = heads // ab
    bt = 4
    b_steps = width // (bt * LANES)
    per_tile = groups // (width // LANES)
    clamp_a = lambda i: jnp.minimum(i, a_steps - 1)
    clamp_b = lambda i: jnp.maximum(i - a_steps, 0)
    early = pl.BlockSpec((rows, ab * HEAD_DIM), lambda i: (0, clamp_a(i)))
    lane = pl.BlockSpec((1, bt * LANES), lambda i: (0, clamp_b(i)))
    return pl.pallas_call(
        lambda *refs: finish_kernel(ab, a_steps, *refs),
        grid=(a_steps + b_steps,),
        out_shape=wide,
        in_specs=[
            smem,
            starts,
            early,
            early,
            early,
            pl.BlockSpec((ab, rows, HEAD_DIM), lambda i: (clamp_a(i), 0, 0)),
            square,
            square,
            pl.BlockSpec((bt, rows, HEAD_DIM), lambda i: (clamp_b(i), 0, 0)),
            pl.BlockSpec((bt * per_tile, taps), lambda i: (clamp_b(i), 0)),
            lane,
            lane,
        ],
        out_specs=pl.BlockSpec((rows, bt * LANES), lambda i: (0, clamp_b(i))),
        scratch_shapes=[
            pltpu.VMEM((width // LANES, rows, LANES), jnp.bfloat16),
            pltpu.VMEM((rows, LANES), jnp.float32),
            pltpu.VMEM((2 * rows, LANES), jnp.float32),
            pltpu.VMEM((rows, 2 * rows), jnp.bfloat16),
            pltpu.VMEM((2, per_tile * rows, 2 * rows), jnp.bfloat16),
            pltpu.VMEM((rows, rows), jnp.float32),
        ],
        compiler_params=params(),
        cost_estimate=pl.CostEstimate(flops=4 * tile_flops, bytes_accessed=6 * wide_bytes, transcendentals=0),
        name="finish",
    )(
        facts,
        st,
        key_across,
        b_across,
        c_across,
        near,
        squares,
        near_squares,
        att,
        mirrored,
        norm_gain.reshape(1, width),
        bypass.reshape(1, width),
    )


def solution(mesh):
    rows = P(("dp", "ctx"), None)
    in_specs = (rows, rows, rows, P("dp"), P(), P(), P())
    return jax.shard_map(shards, mesh=mesh, in_specs=in_specs, out_specs=rows, check_vma=False)
```

```python
import math

import jax
import jax.numpy as jnp
from jax import lax
from jax.experimental import pallas as pl
from jax.experimental.pallas import tpu as pltpu
from jax.sharding import PartitionSpec as P

HEAD_DIM = 128
LANES = 128
NEG = -1e30
FACTOR = 1.0 / math.sqrt(HEAD_DIM) * math.log2(math.e)
CONTRACT_LAST = (((1,), (1,)), ((), ()))
VMEM_BYTES = 20 * 2**20

ODD, BEFORE, NEXT_BEFORE, NEXT_AFTER = range(4)


def permuted(x, pairs):
    return lax.ppermute(x, "ctx", pairs)


def after(x, *others):
    return lax.optimization_barrier((x, *others))[0]


def places(lengths, first_row, count):
    ends = jnp.cumsum(lengths)
    position = first_row + jnp.arange(count + 1, dtype=jnp.int32)
    passed = ends[None, :] <= position[:, None]
    starts = jnp.sum(jnp.where(passed, lengths[None, :], 0), axis=1) - first_row
    past = jnp.min(jnp.where(passed[count], jnp.int32(2**30), ends)) - first_row - count
    odd = (first_row // count) % 2
    facts = jnp.stack([odd, -starts[0], count - starts[count], past]).astype(jnp.int32)
    return starts[:count].astype(jnp.int32).reshape(count, 1), facts


def bias_of(rows, columns, row_first, key_first, start):
    row = lax.broadcasted_iota(jnp.int32, (rows, columns), 0) + row_first
    key = lax.broadcasted_iota(jnp.int32, (rows, columns), 1) + key_first
    return jnp.where((key >= start) & (key <= row), 0.0, NEG)


def scores_of(query, key):
    return lax.dot_general(query, key, CONTRACT_LAST, preferred_element_type=jnp.float32)


def raised(scores, bias):
    s = scores + bias
    top = jnp.max(s, axis=1, keepdims=True)
    return jnp.exp2((s - top) * FACTOR).astype(jnp.bfloat16), top


def summed(weights, value):
    ones = jnp.ones(value.shape, jnp.bfloat16)
    o = jnp.dot(weights, jnp.concatenate([value, ones], axis=1), preferred_element_type=jnp.float32)
    return o[:, :LANES], o[:, LANES:]


def columns(head):
    return slice(head * HEAD_DIM, (head + 1) * HEAD_DIM)


def attend(heads, query, key, value, bias, use):
    ahead = scores_of(query(0), key(0))
    held = None
    for h in range(heads):
        now = ahead
        if h + 1 < heads:
            ahead = scores_of(query(h + 1), key(h + 1))
        weights, top = raised(now, bias)
        if held is not None:
            use(h - 1, *summed(held[0], value(h - 1)), held[1])
        held = weights, top
    use(heads - 1, *summed(held[0], value(heads - 1)), held[1])


def taps_kernel(facts_ref, st_ref, filters_ref, far_ref, near_ref, keep):
    rows = st_ref.shape[0]

    @pl.when(pl.program_id(0) == 0)
    def _():
        st = st_ref[...]
        row = lax.broadcasted_iota(jnp.int32, (rows, 2 * rows), 0)
        key = lax.broadcasted_iota(jnp.int32, (rows, 2 * rows), 1) - rows
        keep[...] = jnp.where((key >= st) & (key <= row) & (key > row - rows), 1.0, 0.0).astype(jnp.bfloat16)

    tap = lax.broadcasted_iota(jnp.int32, (rows, rows), 0)
    place = lax.broadcasted_iota(jnp.int32, (rows, rows), 1)
    turn = jnp.where((tap + place == 0) | (tap + place == rows), 1.0, 0.0).astype(jnp.bfloat16)
    lines = jnp.dot(filters_ref[...], turn, preferred_element_type=jnp.float32)
    tiles = far_ref.shape[0]
    groups = filters_ref.shape[0] // tiles
    for c in range(tiles):
        for g in range(groups):
            line = jnp.broadcast_to(lines[c * groups + g : c * groups + g + 1], (rows, rows))
            ring = pltpu.roll(line, 0, 1, stride=1, stride_axis=0).astype(jnp.bfloat16)
            cols = slice(g * rows, (g + 1) * rows)
            far_ref[c, :, cols] = ring * keep[:, :rows]
            near_ref[c, :, cols] = ring * keep[:, rows:]


def share_kernel(heads, facts_ref, qb_ref, q_ref, kn_ref, ko_ref, vn_ref, vo_ref, b_ref, stat_ref, c_ref, bias):
    rows = q_ref.shape[0]
    step = pl.program_id(0)
    before = facts_ref[NEXT_BEFORE]
    past = facts_ref[NEXT_AFTER]
    odd = facts_ref[ODD] == 1

    @pl.when(odd & (before <= rows))
    def _():
        b_ref[...] = vo_ref[...]
        c_ref[...] = q_ref[...]

    @pl.when(odd & (before > rows))
    def _():
        @pl.when(step == 0)
        def _():
            bias[:rows] = bias_of(rows, 2 * rows, rows, -rows, rows - before)
            bias[rows:] = bias_of(rows, 2 * rows, 0, -rows, rows - before)

        lane = lax.broadcasted_iota(jnp.int32, (rows, LANES), 1)
        ours = lax.broadcasted_iota(jnp.int32, (rows, LANES), 0) < past
        stat = [stat_ref[...]]

        def use(h, o, l, top):
            o = (o / l).astype(jnp.bfloat16)
            b_ref[:, columns(h)] = o[:rows]
            c_ref[:, columns(h)] = o[rows:]
            lse = jnp.where(ours, top[:rows] * FACTOR + jnp.log2(l[:rows]), NEG)
            stat[0] = jnp.where(lane == step * heads + h, lse, stat[0])

        attend(
            heads,
            lambda h: jnp.concatenate([qb_ref[:, columns(h)], q_ref[:, columns(h)]], axis=0),
            lambda h: jnp.concatenate([kn_ref[:, columns(h)], ko_ref[:, columns(h)]], axis=0),
            lambda h: jnp.concatenate([vn_ref[:, columns(h)], vo_ref[:, columns(h)]], axis=0),
            bias[...],
            use,
        )
        stat_ref[...] = stat[0]


def weights_kernel(heads, facts_ref, st_ref, q_ref, ko_ref, kp_ref, kf_ref, kn_ref, qn_ref, three_ref, two_ref, top_ref, bias_own, bias_prev):
    rows = q_ref.shape[0]
    step = pl.program_id(0)
    odd = facts_ref[ODD] == 1

    @pl.when(step == 0)
    def _():
        low = jnp.where((facts_ref[ODD] == 0) & (facts_ref[BEFORE] > rows), 0, -(2**20))
        st = jnp.maximum(st_ref[...], low)
        bias_own[...] = bias_of(rows, 3 * rows, 0, -2 * rows, st)
        bias_prev[...] = bias_of(rows, 2 * rows, -rows, -2 * rows, st_ref[0:1, :])

    @pl.when(odd)
    def _():
        def scores(h):
            key = jnp.concatenate([kf_ref[:, columns(h)], kn_ref[:, columns(h)], ko_ref[:, columns(h)]], axis=0)
            return scores_of(q_ref[:, columns(h)], key), scores_of(qn_ref[:, columns(h)], key[: 2 * rows])

        ahead = scores(0)
        for h in range(heads):
            now = ahead
            if h + 1 < heads:
                ahead = scores(h + 1)
            three_ref[h] = raised(now[0], bias_own[...])[0]
            two_ref[h] = raised(now[1], bias_prev[...])[0]

    @pl.when(jnp.logical_not(odd))
    def _():
        lane = lax.broadcasted_iota(jnp.int32, (rows, LANES), 1)
        tops = top_ref[...]

        def scores(h):
            key = jnp.concatenate([kp_ref[:, columns(h)], ko_ref[:, columns(h)]], axis=0)
            return scores_of(q_ref[:, columns(h)], key)

        ahead = scores(0)
        for h in range(heads):
            now = ahead
            if h + 1 < heads:
                ahead = scores(h + 1)
            weights, top = raised(now, bias_own[:, rows:])
            two_ref[h] = weights
            tops = jnp.where(lane == step * heads + h, top * FACTOR, tops)
        top_ref[...] = tops


def values_kernel(heads, facts_ref, three_ref, two_ref, top_ref, stat_ref, vp_ref, vf_ref, vn_ref, vo_ref, att_ref, near_ref, sq_ref, sq_near_ref):
    rows = vo_ref.shape[0]
    step = pl.program_id(0)
    odd = facts_ref[ODD] == 1

    @pl.when(step == 0)
    def _():
        sq_ref[...] = jnp.zeros_like(sq_ref)
        sq_near_ref[...] = jnp.zeros_like(sq_near_ref)

    @pl.when(odd)
    def _():
        squares = sq_ref[...]
        squares_near = sq_near_ref[...]
        for h in range(heads):
            value = jnp.concatenate([vf_ref[:, columns(h)], vn_ref[:, columns(h)], vo_ref[:, columns(h)]], axis=0)
            o, l = summed(three_ref[h], value)
            a = (o / l).astype(jnp.bfloat16)
            att_ref[h] = a
            a = a.astype(jnp.float32)
            squares += a * a
            o, l = summed(two_ref[h], value[: 2 * rows])
            a = (o / l).astype(jnp.bfloat16)
            near_ref[h] = a
            a = a.astype(jnp.float32)
            squares_near += a * a
        sq_ref[...] = squares
        sq_near_ref[...] = squares_near

    @pl.when(jnp.logical_not(odd))
    def _():
        lane = lax.broadcasted_iota(jnp.int32, (rows, LANES), 1)
        shared = facts_ref[BEFORE] > rows
        stat = jnp.where(shared, stat_ref[...], NEG)
        tops = top_ref[...]
        squares = sq_ref[...]
        high = jnp.maximum(tops, stat)
        here_all = jnp.exp2(tops - high)
        there_all = jnp.exp2(stat - high)
        for h in range(heads):
            value = jnp.concatenate([vp_ref[:, columns(h)], vo_ref[:, columns(h)]], axis=0)
            o, l = summed(two_ref[h], value)
            mine = lane == step * heads + h
            here = jnp.sum(jnp.where(mine, here_all, 0.0), axis=1, keepdims=True)
            there = jnp.sum(jnp.where(mine, there_all, 0.0), axis=1, keepdims=True)
            o = o * here + vp_ref[:, columns(h)].astype(jnp.float32) * there
            a = (o / (l * here + there)).astype(jnp.bfloat16)
            att_ref[h] = a
            a = a.astype(jnp.float32)
            squares += a * a
        sq_ref[...] = squares


def scale_of(squares, width):
    total = jnp.sum(squares, axis=1, keepdims=True)
    return jnp.broadcast_to(lax.rsqrt(total * (1.0 / width) + 1e-06), squares.shape)


def spread(x, groups):
    size = LANES // groups
    lane_group = lax.broadcasted_iota(jnp.int32, x.shape, 1) // size
    return jnp.concatenate([jnp.where(lane_group == g, x, jnp.zeros_like(x)) for g in range(groups)], axis=0)


def own_kernel(width, facts_ref, att_ref, sq_ref, taps_ref, gain_ref, bypass_ref, out_ref, scale):
    tiles, rows, _ = att_ref.shape

    @pl.when(pl.program_id(0) == 0)
    def _():
        scale[...] = scale_of(sq_ref[...], width)

    for c in range(tiles):
        cols = columns(c)
        x = (att_ref[c].astype(jnp.float32) * scale[...] * gain_ref[:, cols]).astype(jnp.bfloat16)
        y = jnp.dot(taps_ref[c], spread(x, taps_ref.shape[2] // rows), preferred_element_type=jnp.float32)
        out_ref[:, cols] = y + bypass_ref[:, cols] * x.astype(jnp.float32)


def finish_kernel(heads, a_steps, facts_ref, st_ref, kp_ref, vp_ref, c_ref, near_ref, sq_near_ref, part_ref, taps_ref, gain_ref, out_ref, prev, squares, scale, bias):
    rows = st_ref.shape[0]
    step = pl.program_id(0)
    width = prev.shape[0] * LANES
    odd = facts_ref[ODD] == 1
    shared = facts_ref[BEFORE] > rows

    @pl.when(step == 0)
    def _():
        squares[...] = jnp.where(odd, sq_near_ref[...], 0.0)
        bias[...] = bias_of(rows, rows, -rows, -rows, st_ref[0:1, :])

    @pl.when((step < a_steps) & odd)
    def _():
        for h in range(heads):
            prev[step * heads + h] = near_ref[h]

    @pl.when((step < a_steps) & jnp.logical_not(odd) & shared)
    def _():
        total = squares[...]
        for h in range(heads):
            a = c_ref[:, columns(h)]
            prev[step * heads + h] = a
            a = a.astype(jnp.float32)
            total += a * a
        squares[...] = total

    @pl.when((step < a_steps) & jnp.logical_not(odd) & jnp.logical_not(shared))
    def _():
        total = [squares[...]]

        def use(h, o, l, top):
            a = (o / l).astype(jnp.bfloat16)
            prev[step * heads + h] = a
            a = a.astype(jnp.float32)
            total[0] += a * a

        attend(heads, lambda h: c_ref[:, columns(h)], lambda h: kp_ref[:, columns(h)], lambda h: vp_ref[:, columns(h)], bias[...], use)
        squares[...] = total[0]

    @pl.when(step == a_steps)
    def _():
        scale[...] = scale_of(squares[...], width)

    @pl.when(step >= a_steps)
    def _():
        tiles = taps_ref.shape[0]
        first = (step - a_steps) * tiles
        for c in range(tiles):
            cols = columns(c)
            x = (prev[first + c].astype(jnp.float32) * scale[...] * gain_ref[:, cols]).astype(jnp.bfloat16)
            y = jnp.dot(taps_ref[c], spread(x, taps_ref.shape[2] // rows), preferred_element_type=jnp.float32)
            out_ref[:, cols] = (y + part_ref[:, cols]).astype(jnp.bfloat16)


def run(kernel, name, steps, facts, out_shape, in_specs, out_specs, scratch, args):
    return pl.pallas_call(
        kernel,
        out_shape=out_shape,
        grid_spec=pltpu.PrefetchScalarGridSpec(
            num_scalar_prefetch=1, grid=(steps,), in_specs=in_specs, out_specs=out_specs, scratch_shapes=scratch
        ),
        compiler_params=pltpu.CompilerParams(vmem_limit_bytes=VMEM_BYTES),
        cost_estimate=pl.CostEstimate(flops=2**20, bytes_accessed=2**16, transcendentals=0),
        name=name,
    )(facts, *args)


def shards(queries, key_rows, value_rows, lengths, norm_gain, filters, bypass):
    rows, width = queries.shape
    heads = width // HEAD_DIM
    groups, taps = filters.shape
    n = lax.axis_size("ctx")
    st, facts = places(lengths, lax.axis_index("ctx") * rows, rows)

    back = [(i, i - 1) for i in range(2, n, 2)]
    within = [(i, i + 1) for i in range(0, n - 1, 2)]
    across = [(i, i + 1) for i in range(1, n - 1, 2)]

    wide = jax.ShapeDtypeStruct((rows, width), jnp.bfloat16)
    stats = jax.ShapeDtypeStruct((rows, LANES), jnp.float32)
    always = lambda i, facts: i
    if_odd = lambda i, facts: jnp.where(facts[ODD] == 1, i, 0)
    if_even = lambda i, facts: jnp.where(facts[ODD] == 0, i, 0)
    whole = lambda shape: pl.BlockSpec(shape, lambda i, facts: (0,) * len(shape))
    starts = whole((rows, 1))
    square = whole((rows, LANES))

    def strip(size, when=always):
        return pl.BlockSpec((rows, size * LANES), lambda i, facts: (0, when(i, facts)))

    def stack(size, depth, when=always):
        return pl.BlockSpec((size, rows, depth), lambda i, facts: (when(i, facts), 0, 0))

    query_back = permuted(queries, back)
    key_near = permuted(key_rows, within)
    value_near = permuted(value_rows, within)
    query_near = permuted(queries, within)

    tiles = width // LANES
    per_tile = groups // tiles
    tb = 4
    taps_shape = jax.ShapeDtypeStruct((tiles, rows, per_tile * rows), jnp.bfloat16)
    taps_far, taps_near = run(
        taps_kernel,
        "taps",
        tiles // tb,
        facts,
        (taps_shape, taps_shape),
        [starts, pl.BlockSpec((tb * per_tile, taps), lambda i, facts: (i, 0))],
        (stack(tb, per_tile * rows), stack(tb, per_tile * rows)),
        [pltpu.VMEM((rows, 2 * rows), jnp.bfloat16)],
        (st, filters),
    )

    key_across = permuted(after(key_rows, query_back, taps_far), across)

    hb = 8
    both = lambda i, facts: jnp.where((facts[ODD] == 1) & (facts[NEXT_BEFORE] > rows), i, 0)
    slot_b, stat, slot_c = run(
        lambda *refs: share_kernel(hb, *refs),
        "share",
        heads // hb,
        facts,
        (wide, stats, wide),
        [strip(hb, both), strip(hb, if_odd), strip(hb, both), strip(hb, both), strip(hb, both), strip(hb, if_odd)],
        (strip(hb, if_odd), square, strip(hb, if_odd)),
        [pltpu.VMEM((2 * rows, 2 * rows), jnp.float32)],
        (query_back, queries, key_near, key_rows, value_near, value_rows),
    )
    b_across = permuted(slot_b, across)
    stat_across = permuted(stat, across)
    c_across = permuted(slot_c, across)
    key_far = permuted(after(key_across, slot_b), within)

    three = jax.ShapeDtypeStruct((heads, rows, 3 * rows), jnp.bfloat16)
    two = jax.ShapeDtypeStruct((heads, rows, 2 * rows), jnp.bfloat16)
    weights_three, weights_two, tops = run(
        lambda *refs: weights_kernel(hb, *refs),
        "weights",
        heads // hb,
        facts,
        (three, two, stats),
        [starts, strip(hb), strip(hb), strip(hb, if_even)] + [strip(hb, if_odd)] * 3,
        (stack(hb, 3 * rows, if_odd), stack(hb, 2 * rows), square),
        [pltpu.VMEM((rows, 3 * rows), jnp.float32), pltpu.VMEM((rows, 2 * rows), jnp.float32)],
        (st, queries, key_rows, key_across, key_far, key_near, query_near),
    )
    value_far = permuted(after(b_across, weights_two), within)

    att_shape = jax.ShapeDtypeStruct((heads, rows, HEAD_DIM), jnp.bfloat16)
    att, near, squares, near_squares = run(
        lambda *refs: values_kernel(hb, *refs),
        "values",
        heads // hb,
        facts,
        (att_shape, att_shape, stats, stats),
        [stack(hb, 3 * rows, if_odd), stack(hb, 2 * rows), square, square, strip(hb, if_even), strip(hb, if_odd), strip(hb, if_odd), strip(hb)],
        (stack(hb, HEAD_DIM), stack(hb, HEAD_DIM, if_odd), square, square),
        [],
        (weights_three, weights_two, tops, stat_across, b_across, value_far, value_near, value_rows),
    )

    gain = norm_gain.reshape(1, width)
    lane = pl.BlockSpec((1, tb * LANES), lambda i, facts: (0, i))
    part = run(
        lambda *refs: own_kernel(width, *refs),
        "own",
        tiles // tb,
        facts,
        jax.ShapeDtypeStruct((rows, width), jnp.float32),
        [stack(tb, HEAD_DIM), square, stack(tb, per_tile * rows), lane, lane],
        strip(tb),
        [pltpu.VMEM((rows, LANES), jnp.float32)],
        (att, squares, taps_near, gain, bypass.reshape(1, width)),
    )

    a_steps = heads // hb
    early = lambda when: lambda i, facts: jnp.where(when(facts), jnp.minimum(i, a_steps - 1), 0)
    late = lambda i, facts: jnp.maximum(i - a_steps, 0)
    alone = early(lambda facts: (facts[ODD] == 0) & (facts[BEFORE] <= rows))
    return run(
        lambda *refs: finish_kernel(hb, a_steps, *refs),
        "finish",
        a_steps + tiles // tb,
        facts,
        wide,
        [
            starts,
            strip(hb, alone),
            strip(hb, alone),
            strip(hb, early(lambda facts: facts[ODD] == 0)),
            stack(hb, HEAD_DIM, early(lambda facts: facts[ODD] == 1)),
            square,
            strip(tb, late),
            stack(tb, per_tile * rows, late),
            pl.BlockSpec((1, tb * LANES), lambda i, facts: (0, late(i, facts))),
        ],
        strip(tb, late),
        [
            pltpu.VMEM((tiles, rows, LANES), jnp.bfloat16),
            pltpu.VMEM((rows, LANES), jnp.float32),
            pltpu.VMEM((rows, LANES), jnp.float32),
            pltpu.VMEM((rows, rows), jnp.float32),
        ],
        (st, key_across, b_across, after(c_across, part), near, near_squares, part, taps_far, gain),
    )


def solution(mesh):
    rows = P(("dp", "ctx"), None)
    in_specs = (rows, rows, rows, P("dp"), P(), P(), P())
    return jax.shard_map(shards, mesh=mesh, in_specs=in_specs, out_specs=rows, check_vma=False)
```

```python
import math

import jax
import jax.numpy as jnp
from jax import lax
from jax.experimental import pallas as pl
from jax.experimental.pallas import tpu as pltpu
from jax.sharding import PartitionSpec as P

HEAD_DIM = 128
LANES = 128
NEG = -1e30
FACTOR = 1.0 / math.sqrt(HEAD_DIM) * math.log2(math.e)
CONTRACT_LAST = (((1,), (1,)), ((), ()))
VMEM_BYTES = 20 * 2**20

ODD, BEFORE, NEXT_BEFORE, NEXT_AFTER = range(4)


def permuted(x, pairs):
    return lax.ppermute(x, "ctx", pairs)


def after(x, *others):
    return lax.optimization_barrier((x, *others))[0]


def places(lengths, first_row, count):
    ends = jnp.cumsum(lengths)
    position = first_row + jnp.arange(count + 1, dtype=jnp.int32)
    passed = ends[None, :] <= position[:, None]
    starts = jnp.sum(jnp.where(passed, lengths[None, :], 0), axis=1) - first_row
    past = jnp.min(jnp.where(passed[count], jnp.int32(2**30), ends)) - first_row - count
    odd = (first_row // count) % 2
    facts = jnp.stack([odd, -starts[0], count - starts[count], past]).astype(jnp.int32)
    return starts[:count].astype(jnp.int32).reshape(count, 1), facts


def bias_of(rows, columns, row_first, key_first, start):
    row = lax.broadcasted_iota(jnp.int32, (rows, columns), 0) + row_first
    key = lax.broadcasted_iota(jnp.int32, (rows, columns), 1) + key_first
    return jnp.where((key >= start) & (key <= row), 0.0, NEG)


def scores_of(query, key):
    return lax.dot_general(query, key, CONTRACT_LAST, preferred_element_type=jnp.float32)


def raised(scores, bias):
    s = scores + bias
    top = jnp.max(s, axis=1, keepdims=True)
    return jnp.exp2((s - top) * FACTOR).astype(jnp.bfloat16), top


def summed(weights, value):
    ones = jnp.ones(value.shape, jnp.bfloat16)
    o = jnp.dot(weights, jnp.concatenate([value, ones], axis=1), preferred_element_type=jnp.float32)
    return o[:, :LANES], o[:, LANES:]


def columns(head):
    return slice(head * HEAD_DIM, (head + 1) * HEAD_DIM)


def attend(heads, query, key, value, bias, use):
    ahead = scores_of(query(0), key(0))
    held = None
    for h in range(heads):
        now = ahead
        if h + 1 < heads:
            ahead = scores_of(query(h + 1), key(h + 1))
        weights, top = raised(now, bias)
        if held is not None:
            use(h - 1, *summed(held[0], value(h - 1)), held[1])
        held = weights, top
    use(heads - 1, *summed(held[0], value(heads - 1)), held[1])


def taps_kernel(facts_ref, st_ref, filters_ref, far_ref, near_ref, keep):
    rows = st_ref.shape[0]

    @pl.when(pl.program_id(0) == 0)
    def _():
        st = st_ref[...]
        row = lax.broadcasted_iota(jnp.int32, (rows, 2 * rows), 0)
        key = lax.broadcasted_iota(jnp.int32, (rows, 2 * rows), 1) - rows
        keep[...] = jnp.where((key >= st) & (key <= row) & (key > row - rows), 1.0, 0.0).astype(jnp.bfloat16)

    tap = lax.broadcasted_iota(jnp.int32, (rows, rows), 0)
    place = lax.broadcasted_iota(jnp.int32, (rows, rows), 1)
    turn = jnp.where((tap + place == 0) | (tap + place == rows), 1.0, 0.0).astype(jnp.bfloat16)
    lines = jnp.dot(filters_ref[...], turn, preferred_element_type=jnp.float32)
    tiles = far_ref.shape[0]
    groups = filters_ref.shape[0] // tiles
    for c in range(tiles):
        for g in range(groups):
            line = jnp.broadcast_to(lines[c * groups + g : c * groups + g + 1], (rows, rows))
            ring = pltpu.roll(line, 0, 1, stride=1, stride_axis=0).astype(jnp.bfloat16)
            cols = slice(g * rows, (g + 1) * rows)
            far_ref[c, :, cols] = ring * keep[:, :rows]
            near_ref[c, :, cols] = ring * keep[:, rows:]


def share_kernel(heads, facts_ref, qb_ref, q_ref, kn_ref, ko_ref, vn_ref, vo_ref, *rest):
    b_ref, c_ref, bias, stat_ref = rest[-4:]
    rows = q_ref.shape[0]
    step = pl.program_id(0)
    before = facts_ref[NEXT_BEFORE]
    past = facts_ref[NEXT_AFTER]
    odd = facts_ref[ODD] == 1
    last = b_ref.shape[0] - 1

    @pl.when(odd & (before <= rows))
    def _():
        for h in range(heads):
            b_ref[step * heads + h] = vo_ref[:, columns(h)]
        c_ref[...] = q_ref[...]

    @pl.when(odd & (before > rows))
    def _():
        @pl.when(step == 0)
        def _():
            bias[:rows] = bias_of(rows, 2 * rows, rows, -rows, rows - before)
            bias[rows:] = bias_of(rows, 2 * rows, 0, -rows, rows - before)
            stat_ref[...] = jnp.zeros_like(stat_ref)

        lane = lax.broadcasted_iota(jnp.int32, (rows, LANES), 1)
        ours = lax.broadcasted_iota(jnp.int32, (rows, LANES), 0) < past
        stat = [stat_ref[...]]

        def use(h, o, l, top):
            o = (o / l).astype(jnp.bfloat16)
            b_ref[step * heads + h] = o[:rows]
            c_ref[:, columns(h)] = o[rows:]
            lse = jnp.where(ours, top[:rows] * FACTOR + jnp.log2(l[:rows]), NEG)
            stat[0] = jnp.where(lane == step * heads + h, lse, stat[0])

        attend(
            heads,
            lambda h: jnp.concatenate([qb_ref[:, columns(h)], q_ref[:, columns(h)]], axis=0),
            lambda h: jnp.concatenate([kn_ref[:, columns(h)], ko_ref[:, columns(h)]], axis=0),
            lambda h: jnp.concatenate([vn_ref[:, columns(h)], vo_ref[:, columns(h)]], axis=0),
            bias[...],
            use,
        )
        stat_ref[...] = stat[0]

        @pl.when(step == pl.num_programs(0) - 1)
        def _():
            total = stat[0]
            high = total.astype(jnp.bfloat16).astype(jnp.float32)
            middle = (total - high).astype(jnp.bfloat16).astype(jnp.float32)
            low = total - high - middle
            packed = high + pltpu.roll(middle, last, 1) + pltpu.roll(low, 2 * last, 1)
            b_ref[last] = packed.astype(jnp.bfloat16)


def attention_kernel(heads, facts_ref, st_ref, q_ref, ko_ref, vo_ref, kp_ref, vp0_ref, vp1_ref, stat0_ref, stat1_ref, qn_ref, kn_ref, vn_ref, kf_ref, vf0_ref, vf1_ref, att_ref, near_ref, sq_ref, sq_near_ref, bias_own, bias_prev):
    rows = q_ref.shape[0]
    step = pl.program_id(0)
    odd = facts_ref[ODD] == 1
    half = pl.num_programs(0) // 2
    vp = lambda h: jnp.where(step < half, vp0_ref[h], vp1_ref[h])
    vf = lambda h: jnp.where(step < half, vf0_ref[h], vf1_ref[h])

    @pl.when(step == 0)
    def _():
        low = jnp.where((facts_ref[ODD] == 0) & (facts_ref[BEFORE] > rows), 0, -(2**20))
        st = jnp.maximum(st_ref[...], low)
        bias_own[...] = bias_of(rows, 3 * rows, 0, -2 * rows, st)
        bias_prev[...] = bias_of(rows, 2 * rows, -rows, -2 * rows, st_ref[0:1, :])
        sq_ref[...] = jnp.zeros_like(sq_ref)
        sq_near_ref[...] = jnp.zeros_like(sq_near_ref)

    @pl.when(odd)
    def _():
        squares = [sq_ref[...], sq_near_ref[...]]

        def use_own(h, o, l, top):
            a = (o / l).astype(jnp.bfloat16)
            att_ref[h] = a
            a = a.astype(jnp.float32)
            squares[0] += a * a

        def use_near(h, o, l, top):
            a = (o / l).astype(jnp.bfloat16)
            near_ref[h] = a
            a = a.astype(jnp.float32)
            squares[1] += a * a

        attend(
            heads,
            lambda h: q_ref[:, columns(h)],
            lambda h: jnp.concatenate([kf_ref[:, columns(h)], kn_ref[:, columns(h)], ko_ref[:, columns(h)]], axis=0),
            lambda h: jnp.concatenate([vf(h), vn_ref[:, columns(h)], vo_ref[:, columns(h)]], axis=0),
            bias_own[...],
            use_own,
        )
        attend(
            heads,
            lambda h: qn_ref[:, columns(h)],
            lambda h: jnp.concatenate([kf_ref[:, columns(h)], kn_ref[:, columns(h)]], axis=0),
            lambda h: jnp.concatenate([vf(h), vn_ref[:, columns(h)]], axis=0),
            bias_prev[...],
            use_near,
        )
        sq_ref[...] = squares[0]
        sq_near_ref[...] = squares[1]

    @pl.when(jnp.logical_not(odd))
    def _():
        lane = lax.broadcasted_iota(jnp.int32, (rows, LANES), 1)
        slot_heads = half * heads
        first = lax.rem(step, half) * heads
        packed = jnp.where(step < half, stat0_ref[0], stat1_ref[0]).astype(jnp.float32)
        stat = packed + pltpu.roll(packed, LANES - slot_heads, 1) + pltpu.roll(packed, LANES - 2 * slot_heads, 1)
        stat = jnp.where(facts_ref[BEFORE] > rows, stat, NEG)
        squares = [sq_ref[...]]

        def use(h, o, l, top):
            lse = jnp.sum(jnp.where(lane == first + h, stat, 0.0), axis=1, keepdims=True)
            top = top * FACTOR
            high = jnp.maximum(top, lse)
            here = jnp.exp2(top - high)
            there = jnp.exp2(lse - high)
            o = o * here + vp(h).astype(jnp.float32) * there
            a = (o / (l * here + there)).astype(jnp.bfloat16)
            att_ref[h] = a
            a = a.astype(jnp.float32)
            squares[0] += a * a

        attend(
            heads,
            lambda h: q_ref[:, columns(h)],
            lambda h: jnp.concatenate([kp_ref[:, columns(h)], ko_ref[:, columns(h)]], axis=0),
            lambda h: jnp.concatenate([vp(h), vo_ref[:, columns(h)]], axis=0),
            bias_own[:, rows:],
            use,
        )
        sq_ref[...] = squares[0]


def scale_of(squares, width):
    total = jnp.sum(squares, axis=1, keepdims=True)
    return jnp.broadcast_to(lax.rsqrt(total * (1.0 / width) + 1e-06), squares.shape)


def spread(x, groups):
    size = LANES // groups
    lane_group = lax.broadcasted_iota(jnp.int32, x.shape, 1) // size
    return jnp.concatenate([jnp.where(lane_group == g, x, jnp.zeros_like(x)) for g in range(groups)], axis=0)


def own_kernel(width, facts_ref, att_ref, sq_ref, taps_ref, gain_ref, bypass_ref, out_ref, scale):
    tiles, rows, _ = att_ref.shape

    @pl.when(pl.program_id(0) == 0)
    def _():
        scale[...] = scale_of(sq_ref[...], width)

    for c in range(tiles):
        cols = columns(c)
        x = (att_ref[c].astype(jnp.float32) * scale[...] * gain_ref[:, cols]).astype(jnp.bfloat16)
        y = jnp.dot(taps_ref[c], spread(x, taps_ref.shape[2] // rows), preferred_element_type=jnp.float32)
        out_ref[:, cols] = y + bypass_ref[:, cols] * x.astype(jnp.float32)


def finish_kernel(heads, a_steps, facts_ref, st_ref, kp_ref, vp0_ref, vp1_ref, c_ref, near_ref, sq_near_ref, part_ref, taps_ref, gain_ref, out_ref, prev, squares, scale, bias):
    rows = st_ref.shape[0]
    step = pl.program_id(0)
    width = prev.shape[0] * LANES
    odd = facts_ref[ODD] == 1
    shared = facts_ref[BEFORE] > rows
    half = a_steps // 2
    vp = lambda h: jnp.where(step < half, vp0_ref[h], vp1_ref[h])
    slot = lambda h: c_ref[:, columns(h)]

    @pl.when(step == 0)
    def _():
        squares[...] = jnp.where(odd, sq_near_ref[...], 0.0)
        bias[...] = bias_of(rows, rows, -rows, -rows, st_ref[0:1, :])

    @pl.when((step < a_steps) & odd)
    def _():
        for h in range(heads):
            prev[step * heads + h] = near_ref[h]

    @pl.when((step < a_steps) & jnp.logical_not(odd) & shared)
    def _():
        total = squares[...]
        for h in range(heads):
            a = slot(h)
            prev[step * heads + h] = a
            a = a.astype(jnp.float32)
            total += a * a
        squares[...] = total

    @pl.when((step < a_steps) & jnp.logical_not(odd) & jnp.logical_not(shared))
    def _():
        total = [squares[...]]

        def use(h, o, l, top):
            a = (o / l).astype(jnp.bfloat16)
            prev[step * heads + h] = a
            a = a.astype(jnp.float32)
            total[0] += a * a

        attend(heads, slot, lambda h: kp_ref[:, columns(h)], vp, bias[...], use)
        squares[...] = total[0]

    @pl.when(step == a_steps)
    def _():
        scale[...] = scale_of(squares[...], width)

    @pl.when(step >= a_steps)
    def _():
        tiles = taps_ref.shape[0]
        first = (step - a_steps) * tiles
        for c in range(tiles):
            cols = columns(c)
            x = (prev[first + c].astype(jnp.float32) * scale[...] * gain_ref[:, cols]).astype(jnp.bfloat16)
            y = jnp.dot(taps_ref[c], spread(x, taps_ref.shape[2] // rows), preferred_element_type=jnp.float32)
            out_ref[:, cols] = (y + part_ref[:, cols]).astype(jnp.bfloat16)


def run(kernel, name, steps, facts, out_shape, in_specs, out_specs, scratch, args, aliases={}):
    return pl.pallas_call(
        kernel,
        out_shape=out_shape,
        grid_spec=pltpu.PrefetchScalarGridSpec(
            num_scalar_prefetch=1, grid=(steps,), in_specs=in_specs, out_specs=out_specs, scratch_shapes=scratch
        ),
        compiler_params=pltpu.CompilerParams(vmem_limit_bytes=VMEM_BYTES),
        cost_estimate=pl.CostEstimate(flops=2**20, bytes_accessed=2**16, transcendentals=0),
        input_output_aliases=aliases,
        name=name,
    )(facts, *args)


def shards(queries, key_rows, value_rows, lengths, norm_gain, filters, bypass):
    rows, width = queries.shape
    heads = width // HEAD_DIM
    groups, taps = filters.shape
    n = lax.axis_size("ctx")
    st, facts = places(lengths, lax.axis_index("ctx") * rows, rows)

    back = [(i, i - 1) for i in range(2, n, 2)]
    within = [(i, i + 1) for i in range(0, n - 1, 2)]
    across = [(i, i + 1) for i in range(1, n - 1, 2)]

    wide = jax.ShapeDtypeStruct((rows, width), jnp.bfloat16)
    stats = jax.ShapeDtypeStruct((rows, LANES), jnp.float32)
    always = lambda i, facts: i
    if_odd = lambda i, facts: jnp.where(facts[ODD] == 1, i, 0)
    if_even = lambda i, facts: jnp.where(facts[ODD] == 0, i, 0)
    whole = lambda shape: pl.BlockSpec(shape, lambda i, facts: (0,) * len(shape))
    starts = whole((rows, 1))
    square = whole((rows, LANES))

    def strip(size, when=always):
        return pl.BlockSpec((rows, size * LANES), lambda i, facts: (0, when(i, facts)))

    def stack(size, depth, when=always):
        return pl.BlockSpec((size, rows, depth), lambda i, facts: (when(i, facts), 0, 0))

    query_back = permuted(queries, back)
    key_near = permuted(key_rows, within)
    value_near = permuted(value_rows, within)
    query_near = permuted(queries, within)

    tiles = width // LANES
    per_tile = groups // tiles
    tb = 4
    taps_shape = jax.ShapeDtypeStruct((tiles, rows, per_tile * rows), jnp.bfloat16)
    taps_far, taps_near = run(
        taps_kernel,
        "taps",
        tiles // tb,
        facts,
        (taps_shape, taps_shape),
        [starts, pl.BlockSpec((tb * per_tile, taps), lambda i, facts: (i, 0))],
        (stack(tb, per_tile * rows), stack(tb, per_tile * rows)),
        [pltpu.VMEM((rows, 2 * rows), jnp.bfloat16)],
        (st, filters),
    )

    key_across = permuted(after(key_rows, query_back, taps_far), across)

    hb = 8
    both = lambda i, facts: jnp.where((facts[ODD] == 1) & (facts[NEXT_BEFORE] > rows), i, 0)
    half_heads = heads // 2
    half_steps = half_heads // hb
    slots = jax.ShapeDtypeStruct((half_heads + 1, rows, HEAD_DIM), jnp.bfloat16)

    def share(part, *filled):
        offset = part * half_steps
        on_odd = lambda i, facts: jnp.where(facts[ODD] == 1, i + offset, offset)
        on_both = lambda i, facts: jnp.where((facts[ODD] == 1) & (facts[NEXT_BEFORE] > rows), i + offset, offset)
        return run(
            lambda *refs: share_kernel(hb, *refs),
            "share",
            half_steps,
            facts,
            (slots, wide),
            [strip(hb, on_both), strip(hb, on_odd), strip(hb, on_both), strip(hb, on_both), strip(hb, on_both), strip(hb, on_odd)]
            + [pl.BlockSpec(memory_space=pl.ANY)] * len(filled),
            (whole((half_heads + 1, rows, HEAD_DIM)), strip(hb, on_odd)),
            [pltpu.VMEM((2 * rows, 2 * rows), jnp.float32), pltpu.VMEM((rows, LANES), jnp.float32)],
            (query_back, queries, key_near, key_rows, value_near, value_rows, *filled),
            {7: 1} if filled else {},
        )

    slot_b0, slot_c = share(0)
    slot_b1, slot_c = share(1, slot_c)
    slots_b = slot_b0, slot_b1
    b_across = [permuted(x, across) for x in slots_b]
    c_across = permuted(slot_c, across)
    key_far = permuted(after(key_across, *slots_b), within)
    value_far = [permuted(x, within) for x in b_across]

    att_shape = jax.ShapeDtypeStruct((heads, rows, HEAD_DIM), jnp.bfloat16)
    att, near, squares, near_squares = run(
        lambda *refs: attention_kernel(hb, *refs),
        "attention",
        heads // hb,
        facts,
        (att_shape, att_shape, stats, stats),
        [
            starts,
            strip(hb),
            strip(hb),
            strip(hb),
            strip(hb, if_even),
            stack(hb, HEAD_DIM, lambda i, facts: if_even(jnp.minimum(i, half_steps - 1), facts)),
            stack(hb, HEAD_DIM, lambda i, facts: if_even(jnp.maximum(i - half_steps, 0), facts)),
            stack(1, HEAD_DIM, lambda i, facts: half_heads),
            stack(1, HEAD_DIM, lambda i, facts: half_heads),
            strip(hb, if_odd),
            strip(hb, if_odd),
            strip(hb, if_odd),
            strip(hb, if_odd),
            stack(hb, HEAD_DIM, lambda i, facts: if_odd(jnp.minimum(i, half_steps - 1), facts)),
            stack(hb, HEAD_DIM, lambda i, facts: if_odd(jnp.maximum(i - half_steps, 0), facts)),
        ],
        (stack(hb, HEAD_DIM), stack(hb, HEAD_DIM, if_odd), square, square),
        [pltpu.VMEM((rows, 3 * rows), jnp.float32), pltpu.VMEM((rows, 2 * rows), jnp.float32)],
        (st, queries, key_rows, value_rows, key_across, *b_across, *b_across, query_near, key_near, value_near, key_far, *value_far),
    )

    gain = norm_gain.reshape(1, width)
    lane = pl.BlockSpec((1, tb * LANES), lambda i, facts: (0, i))
    part = run(
        lambda *refs: own_kernel(width, *refs),
        "own",
        tiles // tb,
        facts,
        jax.ShapeDtypeStruct((rows, width), jnp.float32),
        [stack(tb, HEAD_DIM), square, stack(tb, per_tile * rows), lane, lane],
        strip(tb),
        [pltpu.VMEM((rows, LANES), jnp.float32)],
        (att, squares, taps_near, gain, bypass.reshape(1, width)),
    )

    a_steps = heads // hb

    def early(when, low=0, high=a_steps - 1):
        return lambda i, facts: jnp.where(when(facts), jnp.clip(i - low, 0, high - low), 0)

    late = lambda i, facts: jnp.maximum(i - a_steps, 0)
    even = lambda facts: facts[ODD] == 0
    alone = lambda facts: even(facts) & (facts[BEFORE] <= rows)
    return run(
        lambda *refs: finish_kernel(hb, a_steps, *refs),
        "finish",
        a_steps + tiles // tb,
        facts,
        wide,
        [
            starts,
            strip(hb, early(alone)),
            stack(hb, HEAD_DIM, early(alone, 0, half_steps - 1)),
            stack(hb, HEAD_DIM, early(alone, half_steps)),
            strip(hb, early(even)),
            stack(hb, HEAD_DIM, early(lambda facts: facts[ODD] == 1)),
            square,
            strip(tb, late),
            stack(tb, per_tile * rows, late),
            pl.BlockSpec((1, tb * LANES), lambda i, facts: (0, late(i, facts))),
        ],
        strip(tb, late),
        [
            pltpu.VMEM((tiles, rows, LANES), jnp.bfloat16),
            pltpu.VMEM((rows, LANES), jnp.float32),
            pltpu.VMEM((rows, LANES), jnp.float32),
            pltpu.VMEM((rows, rows), jnp.float32),
        ],
        (st, key_across, *b_across, c_across, near, near_squares, part, taps_far, gain),
    )


def solution(mesh):
    rows = P(("dp", "ctx"), None)
    in_specs = (rows, rows, rows, P("dp"), P(), P(), P())
    return jax.shard_map(shards, mesh=mesh, in_specs=in_specs, out_specs=rows, check_vma=False)
```

```python
import math

import jax
import jax.numpy as jnp
from jax import lax
from jax.experimental import pallas as pl
from jax.experimental.pallas import tpu as pltpu
from jax.sharding import PartitionSpec as P

HEAD_DIM = 128
LANES = 128
NEG = -1e30
FACTOR = 1.0 / math.sqrt(HEAD_DIM) * math.log2(math.e)
CONTRACT_LAST = (((1,), (1,)), ((), ()))
VMEM_BYTES = 16 * 2**20
UNROLL = 8

ODD, BEFORE, NEXT_BEFORE, NEXT_AFTER = range(4)


def permuted(x, pairs):
    return lax.ppermute(x, "ctx", pairs)


def after(x, *others):
    return lax.optimization_barrier((x, *others))[0]


def places(lengths, first_row, count):
    ends = jnp.cumsum(lengths)
    position = first_row + jnp.arange(count + 1, dtype=jnp.int32)
    passed = ends[None, :] <= position[:, None]
    starts = jnp.sum(jnp.where(passed, lengths[None, :], 0), axis=1) - first_row
    past = jnp.min(jnp.where(passed[count], jnp.int32(2**30), ends)) - first_row - count
    odd = (first_row // count) % 2
    facts = jnp.stack([odd, -starts[0], count - starts[count], past]).astype(jnp.int32)
    return starts[:count].astype(jnp.int32).reshape(count, 1), facts


def bias_of(rows, columns, row_first, key_first, start):
    row = lax.broadcasted_iota(jnp.int32, (rows, columns), 0) + row_first
    key = lax.broadcasted_iota(jnp.int32, (rows, columns), 1) + key_first
    return jnp.where((key >= start) & (key <= row), 0.0, NEG)


def scores_of(query, key):
    return lax.dot_general(query, key, CONTRACT_LAST, preferred_element_type=jnp.float32)


def raised(scores, bias):
    s = scores + bias
    top = jnp.max(s, axis=1, keepdims=True)
    return jnp.exp2((s - top) * FACTOR).astype(jnp.bfloat16), top


def summed(weights, value):
    ones = jnp.ones(value.shape, jnp.bfloat16)
    o = jnp.dot(weights, jnp.concatenate([value, ones], axis=1), preferred_element_type=jnp.float32)
    return o[:, :LANES], o[:, LANES:]


def columns(head):
    if isinstance(head, int):
        return slice(head * HEAD_DIM, (head + 1) * HEAD_DIM)
    return pl.ds(pl.multiple_of(head * HEAD_DIM, HEAD_DIM), HEAD_DIM)


def attend(heads, query, key, value, bias, use):
    ahead = scores_of(query(0), key(0))
    held = None
    for h in range(heads):
        now = ahead
        if h + 1 < heads:
            ahead = scores_of(query(h + 1), key(h + 1))
        weights, top = raised(now, bias)
        if held is not None:
            use(h - 1, *summed(held[0], value(h - 1)), held[1])
        held = weights, top
    use(heads - 1, *summed(held[0], value(heads - 1)), held[1])


def each(count, body):
    @pl.loop(0, count // UNROLL)
    def _(step):
        body(step * UNROLL)


def taps_kernel(facts_ref, st_ref, filters_ref, far_ref, near_ref, keep, lines):
    rows = st_ref.shape[0]
    tiles = far_ref.shape[0]
    groups = filters_ref.shape[0] // tiles
    st = st_ref[...]
    row = lax.broadcasted_iota(jnp.int32, (rows, 2 * rows), 0)
    key = lax.broadcasted_iota(jnp.int32, (rows, 2 * rows), 1) - rows
    keep[...] = jnp.where((key >= st) & (key <= row) & (key > row - rows), 1.0, 0.0).astype(jnp.bfloat16)
    tap = lax.broadcasted_iota(jnp.int32, (rows, rows), 0)
    place = lax.broadcasted_iota(jnp.int32, (rows, rows), 1)
    turn = jnp.where((tap + place == 0) | (tap + place == rows), 1.0, 0.0).astype(jnp.bfloat16)
    lines[...] = jnp.dot(filters_ref[...], turn, preferred_element_type=jnp.float32).reshape(lines.shape)

    @pl.loop(0, tiles)
    def _(c):
        some = lines[c]
        for g in range(groups):
            line = jnp.broadcast_to(some[g : g + 1], (rows, rows))
            ring = pltpu.roll(line, 0, 1, stride=1, stride_axis=0).astype(jnp.bfloat16)
            cols = slice(g * rows, (g + 1) * rows)
            far_ref[c, :, cols] = ring * keep[:, :rows]
            near_ref[c, :, cols] = ring * keep[:, rows:]


def share_kernel(facts_ref, qb_ref, q_ref, kn_ref, ko_ref, vn_ref, vo_ref, b0_ref, b1_ref, c_ref, bias, stat_ref):
    rows = q_ref.shape[0]
    before = facts_ref[NEXT_BEFORE]
    past = facts_ref[NEXT_AFTER]
    odd = facts_ref[ODD] == 1
    half = b0_ref.shape[0] - 1

    @pl.when(odd & (before <= rows))
    def _():
        c_ref[...] = q_ref[...]
        for part, b_ref in enumerate((b0_ref, b1_ref)):

            @pl.loop(0, half)
            def _(h):
                b_ref[h] = vo_ref[:, columns(part * half + h)]

    @pl.when(odd & (before > rows))
    def _():
        bias[:rows] = bias_of(rows, 2 * rows, rows, -rows, rows - before)
        bias[rows:] = bias_of(rows, 2 * rows, 0, -rows, rows - before)
        lane = lax.broadcasted_iota(jnp.int32, (rows, LANES), 1)
        ours = lax.broadcasted_iota(jnp.int32, (rows, LANES), 0) < past
        for part, b_ref in enumerate((b0_ref, b1_ref)):
            stat_ref[...] = jnp.zeros_like(stat_ref)

            def heads(first):
                at = lambda h: columns(part * half + first + h)
                stat = [stat_ref[...]]

                def use(h, o, l, top):
                    o = (o / l).astype(jnp.bfloat16)
                    b_ref[first + h] = o[:rows]
                    c_ref[:, at(h)] = o[rows:]
                    lse = jnp.where(ours, top[:rows] * FACTOR + jnp.log2(l[:rows]), NEG)
                    stat[0] = jnp.where(lane == first + h, lse, stat[0])

                attend(
                    UNROLL,
                    lambda h: jnp.concatenate([qb_ref[:, at(h)], q_ref[:, at(h)]], axis=0),
                    lambda h: jnp.concatenate([kn_ref[:, at(h)], ko_ref[:, at(h)]], axis=0),
                    lambda h: jnp.concatenate([vn_ref[:, at(h)], vo_ref[:, at(h)]], axis=0),
                    bias[...],
                    use,
                )
                stat_ref[...] = stat[0]

            each(half, heads)
            total = stat_ref[...]
            high = total.astype(jnp.bfloat16).astype(jnp.float32)
            middle = (total - high).astype(jnp.bfloat16).astype(jnp.float32)
            low = total - high - middle
            packed = high + pltpu.roll(middle, half, 1) + pltpu.roll(low, 2 * half, 1)
            b_ref[half] = packed.astype(jnp.bfloat16)


def attention_kernel(part, facts_ref, st_ref, q_ref, ko_ref, vo_ref, kp_ref, vp_ref, qn_ref, kn_ref, vn_ref, kf_ref, vf_ref, att_ref, near_ref, sq_ref, sq_near_ref, bias_own, bias_prev):
    rows = q_ref.shape[0]
    odd = facts_ref[ODD] == 1
    half = att_ref.shape[0]
    low = jnp.where((facts_ref[ODD] == 0) & (facts_ref[BEFORE] > rows), 0, -(2**20))
    bias_own[...] = bias_of(rows, 3 * rows, 0, -2 * rows, jnp.maximum(st_ref[...], low))
    sq_ref[...] = jnp.zeros_like(sq_ref)
    sq_near_ref[...] = jnp.zeros_like(sq_near_ref)

    @pl.when(odd)
    def _():
        bias_prev[...] = bias_of(rows, 2 * rows, -rows, -2 * rows, st_ref[0:1, :])

        def heads(first):
            at = lambda h: columns(part * half + first + h)
            squares = [sq_ref[...], sq_near_ref[...]]

            def use_own(h, o, l, top):
                a = (o / l).astype(jnp.bfloat16)
                att_ref[first + h] = a
                a = a.astype(jnp.float32)
                squares[0] += a * a

            def use_near(h, o, l, top):
                a = (o / l).astype(jnp.bfloat16)
                near_ref[first + h] = a
                a = a.astype(jnp.float32)
                squares[1] += a * a

            attend(
                UNROLL,
                lambda h: q_ref[:, at(h)],
                lambda h: jnp.concatenate([kf_ref[:, at(h)], kn_ref[:, at(h)], ko_ref[:, at(h)]], axis=0),
                lambda h: jnp.concatenate([vf_ref[first + h], vn_ref[:, at(h)], vo_ref[:, at(h)]], axis=0),
                bias_own[...],
                use_own,
            )
            attend(
                UNROLL,
                lambda h: qn_ref[:, at(h)],
                lambda h: jnp.concatenate([kf_ref[:, at(h)], kn_ref[:, at(h)]], axis=0),
                lambda h: jnp.concatenate([vf_ref[first + h], vn_ref[:, at(h)]], axis=0),
                bias_prev[...],
                use_near,
            )
            sq_ref[...] = squares[0]
            sq_near_ref[...] = squares[1]

        each(half, heads)

    @pl.when(jnp.logical_not(odd))
    def _():
        lane = lax.broadcasted_iota(jnp.int32, (rows, LANES), 1)

        def heads(first):
            at = lambda h: columns(part * half + first + h)
            packed = vp_ref[half].astype(jnp.float32)
            stat = packed + pltpu.roll(packed, LANES - half, 1) + pltpu.roll(packed, LANES - 2 * half, 1)
            stat = jnp.where(facts_ref[BEFORE] > rows, stat, NEG)
            squares = [sq_ref[...]]

            def use(h, o, l, top):
                lse = jnp.sum(jnp.where(lane == first + h, stat, 0.0), axis=1, keepdims=True)
                top = top * FACTOR
                high = jnp.maximum(top, lse)
                here = jnp.exp2(top - high)
                there = jnp.exp2(lse - high)
                o = o * here + vp_ref[first + h].astype(jnp.float32) * there
                a = (o / (l * here + there)).astype(jnp.bfloat16)
                att_ref[first + h] = a
                a = a.astype(jnp.float32)
                squares[0] += a * a

            attend(
                UNROLL,
                lambda h: q_ref[:, at(h)],
                lambda h: jnp.concatenate([kp_ref[:, at(h)], ko_ref[:, at(h)]], axis=0),
                lambda h: jnp.concatenate([vp_ref[first + h], vo_ref[:, at(h)]], axis=0),
                bias_own[:, rows:],
                use,
            )
            sq_ref[...] = squares[0]

        each(half, heads)


def scale_of(squares, width):
    total = jnp.sum(squares, axis=1, keepdims=True)
    return jnp.broadcast_to(lax.rsqrt(total * (1.0 / width) + 1e-06), squares.shape)


def spread(x, groups):
    size = LANES // groups
    lane_group = lax.broadcasted_iota(jnp.int32, x.shape, 1) // size
    return jnp.concatenate([jnp.where(lane_group == g, x, jnp.zeros_like(x)) for g in range(groups)], axis=0)


def own_kernel(facts_ref, att0_ref, att1_ref, sq0_ref, sq1_ref, taps_ref, gain_ref, bypass_ref, out_ref, scale):
    half, rows, _ = att0_ref.shape
    scale[...] = scale_of(sq0_ref[...] + sq1_ref[...], 2 * half * LANES)
    for part, att_ref in enumerate((att0_ref, att1_ref)):

        def tiles(first):
            for c in range(UNROLL):
                tile = part * half + first + c
                cols = columns(tile)
                x = (att_ref[first + c].astype(jnp.float32) * scale[...] * gain_ref[:, cols]).astype(jnp.bfloat16)
                y = jnp.dot(taps_ref[tile], spread(x, taps_ref.shape[2] // rows), preferred_element_type=jnp.float32)
                out_ref[:, cols] = y + bypass_ref[:, cols] * x.astype(jnp.float32)

        each(half, tiles)


def finish_kernel(facts_ref, st_ref, kp_ref, vp0_ref, vp1_ref, c_ref, near0_ref, near1_ref, sq0_ref, sq1_ref, part_ref, taps_ref, gain_ref, out_ref, prev, squares, scale, bias):
    rows = st_ref.shape[0]
    half = near0_ref.shape[0]
    width = prev.shape[0] * LANES
    odd = facts_ref[ODD] == 1
    shared = facts_ref[BEFORE] > rows

    @pl.when(odd)
    def _():
        squares[...] = sq0_ref[...] + sq1_ref[...]
        for part, near_ref in enumerate((near0_ref, near1_ref)):

            @pl.loop(0, half)
            def _(h):
                prev[part * half + h] = near_ref[h]

    @pl.when(jnp.logical_not(odd) & shared)
    def _():
        squares[...] = jnp.zeros_like(squares)

        def heads(first):
            total = squares[...]
            for h in range(UNROLL):
                a = c_ref[:, columns(first + h)]
                prev[first + h] = a
                a = a.astype(jnp.float32)
                total += a * a
            squares[...] = total

        each(2 * half, heads)

    @pl.when(jnp.logical_not(odd) & jnp.logical_not(shared))
    def _():
        squares[...] = jnp.zeros_like(squares)
        bias[...] = bias_of(rows, rows, -rows, -rows, st_ref[0:1, :])
        for part, vp_ref in enumerate((vp0_ref, vp1_ref)):

            def heads(first):
                at = lambda h: columns(part * half + first + h)
                total = [squares[...]]

                def use(h, o, l, top):
                    a = (o / l).astype(jnp.bfloat16)
                    prev[part * half + first + h] = a
                    a = a.astype(jnp.float32)
                    total[0] += a * a

                attend(UNROLL, lambda h: c_ref[:, at(h)], lambda h: kp_ref[:, at(h)], lambda h: vp_ref[first + h], bias[...], use)
                squares[...] = total[0]

            each(half, heads)

    scale[...] = scale_of(squares[...], width)

    def tiles(first):
        for c in range(UNROLL):
            cols = columns(first + c)
            x = (prev[first + c].astype(jnp.float32) * scale[...] * gain_ref[:, cols]).astype(jnp.bfloat16)
            y = jnp.dot(taps_ref[first + c], spread(x, taps_ref.shape[2] // rows), preferred_element_type=jnp.float32)
            out_ref[:, cols] = (y + part_ref[:, cols]).astype(jnp.bfloat16)

    each(2 * half, tiles)


def run(kernel, name, facts, out_shape, scratch, args):
    many = isinstance(out_shape, tuple)
    vmem = pl.BlockSpec(memory_space=pltpu.VMEM)
    return pl.pallas_call(
        kernel,
        out_shape=out_shape,
        in_specs=[pl.BlockSpec(memory_space=pltpu.SMEM)] + [vmem] * len(args),
        out_specs=(vmem,) * len(out_shape) if many else vmem,
        scratch_shapes=scratch,
        compiler_params=pltpu.CompilerParams(vmem_limit_bytes=VMEM_BYTES),
        cost_estimate=pl.CostEstimate(flops=2**20, bytes_accessed=2**16, transcendentals=0),
        name=name,
    )(facts, *args)


def shards(queries, key_rows, value_rows, lengths, norm_gain, filters, bypass):
    rows, width = queries.shape
    heads = width // HEAD_DIM
    half = heads // 2
    groups, taps = filters.shape
    n = lax.axis_size("ctx")
    st, facts = places(lengths, lax.axis_index("ctx") * rows, rows)

    back = [(i, i - 1) for i in range(2, n, 2)]
    within = [(i, i + 1) for i in range(0, n - 1, 2)]
    across = [(i, i + 1) for i in range(1, n - 1, 2)]

    bf16 = lambda *shape: jax.ShapeDtypeStruct(shape, jnp.bfloat16)
    f32 = lambda *shape: jax.ShapeDtypeStruct(shape, jnp.float32)

    query_back = permuted(queries, back)
    key_near = permuted(key_rows, within)
    value_near = permuted(value_rows, within)
    query_near = permuted(queries, within)

    taps_far, taps_near = run(
        taps_kernel,
        "taps",
        facts,
        (bf16(heads, rows, groups // heads * rows),) * 2,
        [pltpu.VMEM((rows, 2 * rows), jnp.bfloat16), pltpu.VMEM((heads, groups // heads, taps), jnp.float32)],
        (st, filters),
    )
    key_across = permuted(after(key_rows, taps_far), across)

    slot_b0, slot_b1, slot_c = run(
        share_kernel,
        "share",
        facts,
        (bf16(half + 1, rows, HEAD_DIM), bf16(half + 1, rows, HEAD_DIM), bf16(rows, width)),
        [pltpu.VMEM((2 * rows, 2 * rows), jnp.float32), pltpu.VMEM((rows, LANES), jnp.float32)],
        (query_back, queries, key_near, key_rows, value_near, value_rows),
    )
    b_across = [permuted(x, across) for x in (slot_b0, slot_b1)]
    c_across = permuted(slot_c, across)
    key_far = permuted(after(key_across, slot_c), within)
    value_far = [permuted(x, within) for x in b_across]

    att, near, squares, near_squares = zip(
        *[
            run(
                lambda *refs, part=part: attention_kernel(part, *refs),
                "attention",
                facts,
                (bf16(half, rows, HEAD_DIM), bf16(half, rows, HEAD_DIM), f32(rows, LANES), f32(rows, LANES)),
                [pltpu.VMEM((rows, 3 * rows), jnp.float32), pltpu.VMEM((rows, 2 * rows), jnp.float32)],
                (st, queries, key_rows, value_rows, key_across, b_across[part], query_near, key_near, value_near, key_far, value_far[part]),
            )
            for part in range(2)
        ]
    )

    gain = norm_gain.reshape(1, width)
    part = run(
        own_kernel,
        "own",
        facts,
        f32(rows, width),
        [pltpu.VMEM((rows, LANES), jnp.float32)],
        (*att, *squares, taps_near, gain, bypass.reshape(1, width)),
    )
    return run(
        finish_kernel,
        "finish",
        facts,
        bf16(rows, width),
        [
            pltpu.VMEM((heads, rows, LANES), jnp.bfloat16),
            pltpu.VMEM((rows, LANES), jnp.float32),
            pltpu.VMEM((rows, LANES), jnp.float32),
            pltpu.VMEM((rows, rows), jnp.float32),
        ],
        (st, key_across, *b_across, c_across, *near, *near_squares, part, taps_far, gain),
    )


def solution(mesh):
    rows = P(("dp", "ctx"), None)
    in_specs = (rows, rows, rows, P("dp"), P(), P(), P())
    return jax.shard_map(shards, mesh=mesh, in_specs=in_specs, out_specs=rows, check_vma=False)
```

```python
import math

import jax
import jax.numpy as jnp
from jax import lax
from jax.experimental import pallas as pl
from jax.experimental.pallas import tpu as pltpu
from jax.sharding import PartitionSpec as P

HEAD_DIM = 128
LANES = 128
NEG = -1e30
FACTOR = 1.0 / math.sqrt(HEAD_DIM) * math.log2(math.e)
CONTRACT_LAST = (((1,), (1,)), ((), ()))
VMEM_BYTES = 16 * 2**20
UNROLL = 8

ODD, BEFORE, NEXT_BEFORE, NEXT_AFTER = range(4)


def permuted(x, pairs):
    return lax.ppermute(x, "ctx", pairs)


def after(x, *others):
    return lax.optimization_barrier((x, *others))[0]


def places(lengths, first_row, count):
    ends = jnp.cumsum(lengths)
    position = first_row + jnp.arange(count + 1, dtype=jnp.int32)
    passed = ends[None, :] <= position[:, None]
    starts = jnp.sum(jnp.where(passed, lengths[None, :], 0), axis=1) - first_row
    past = jnp.min(jnp.where(passed[count], jnp.int32(2**30), ends)) - first_row - count
    odd = (first_row // count) % 2
    facts = jnp.stack([odd, -starts[0], count - starts[count], past]).astype(jnp.int32)
    return starts[:count].astype(jnp.int32).reshape(count, 1), facts


def bias_of(rows, columns, row_first, key_first, start):
    row = lax.broadcasted_iota(jnp.int32, (rows, columns), 0) + row_first
    key = lax.broadcasted_iota(jnp.int32, (rows, columns), 1) + key_first
    return jnp.where((key >= start) & (key <= row), 0.0, NEG)


def scores_of(query, key):
    return lax.dot_general(query, key, CONTRACT_LAST, preferred_element_type=jnp.float32)


def raised(scores, bias):
    s = scores + bias
    top = jnp.max(s, axis=1, keepdims=True)
    return jnp.exp2((s - top) * FACTOR).astype(jnp.bfloat16), top


def summed(weights, value):
    ones = jnp.ones(value.shape, jnp.bfloat16)
    o = jnp.dot(weights, jnp.concatenate([value, ones], axis=1), preferred_element_type=jnp.float32)
    return o[:, :LANES], o[:, LANES:]


def columns(head):
    if isinstance(head, int):
        return slice(head * HEAD_DIM, (head + 1) * HEAD_DIM)
    return pl.ds(pl.multiple_of(head * HEAD_DIM, HEAD_DIM), HEAD_DIM)


def attend(heads, query, key, value, bias, use):
    ahead = scores_of(query(0), key(0))
    held = None
    for h in range(heads):
        now = ahead
        if h + 1 < heads:
            ahead = scores_of(query(h + 1), key(h + 1))
        weights, top = raised(now, bias)
        if held is not None:
            use(h - 1, *summed(held[0], value(h - 1)), held[1])
        held = weights, top
    use(heads - 1, *summed(held[0], value(heads - 1)), held[1])


def each(count, body):
    @pl.loop(0, count // UNROLL)
    def _(step):
        body(step * UNROLL)


def taps_kernel(facts_ref, st_ref, filters_ref, far_ref, near_ref, keep, lines):
    rows = st_ref.shape[0]
    tiles = far_ref.shape[0]
    groups = filters_ref.shape[0] // tiles
    st = st_ref[...]
    row = lax.broadcasted_iota(jnp.int32, (rows, 2 * rows), 0)
    key = lax.broadcasted_iota(jnp.int32, (rows, 2 * rows), 1) - rows
    keep[...] = jnp.where((key >= st) & (key <= row) & (key > row - rows), 1.0, 0.0).astype(jnp.bfloat16)
    tap = lax.broadcasted_iota(jnp.int32, (rows, rows), 0)
    place = lax.broadcasted_iota(jnp.int32, (rows, rows), 1)
    turn = jnp.where((tap + place == 0) | (tap + place == rows), 1.0, 0.0).astype(jnp.bfloat16)
    lines[...] = jnp.dot(filters_ref[...], turn, preferred_element_type=jnp.float32).reshape(lines.shape)

    @pl.loop(0, tiles)
    def _(c):
        some = lines[c]
        for g in range(groups):
            line = jnp.broadcast_to(some[g : g + 1], (rows, rows))
            ring = pltpu.roll(line, 0, 1, stride=1, stride_axis=0).astype(jnp.bfloat16)
            cols = slice(g * rows, (g + 1) * rows)
            far_ref[c, :, cols] = ring * keep[:, :rows]
            near_ref[c, :, cols] = ring * keep[:, rows:]


def share_kernel(facts_ref, qb_ref, q_ref, kn_ref, ko_ref, vn_ref, vo_ref, b0_ref, b1_ref, c_ref, bias, stat_ref):
    rows = q_ref.shape[0]
    before = facts_ref[NEXT_BEFORE]
    past = facts_ref[NEXT_AFTER]
    odd = facts_ref[ODD] == 1
    half = b0_ref.shape[0] - 1

    @pl.when(odd & (before <= rows))
    def _():
        c_ref[...] = q_ref[...]
        for part, b_ref in enumerate((b0_ref, b1_ref)):

            @pl.loop(0, half)
            def _(h):
                b_ref[h] = vo_ref[:, columns(part * half + h)]

    @pl.when(odd & (before > rows))
    def _():
        bias[:rows] = bias_of(rows, 2 * rows, rows, -rows, rows - before)
        bias[rows:] = bias_of(rows, 2 * rows, 0, -rows, rows - before)
        lane = lax.broadcasted_iota(jnp.int32, (rows, LANES), 1)
        ours = lax.broadcasted_iota(jnp.int32, (rows, LANES), 0) < past
        for part, b_ref in enumerate((b0_ref, b1_ref)):
            stat_ref[...] = jnp.zeros_like(stat_ref)

            def heads(first):
                at = lambda h: columns(part * half + first + h)
                stat = [stat_ref[...]]

                def use(h, o, l, top):
                    o = (o / l).astype(jnp.bfloat16)
                    b_ref[first + h] = o[:rows]
                    c_ref[:, at(h)] = o[rows:]
                    lse = jnp.where(ours, top[:rows] * FACTOR + jnp.log2(l[:rows]), NEG)
                    stat[0] = jnp.where(lane == first + h, lse, stat[0])

                attend(
                    UNROLL,
                    lambda h: jnp.concatenate([qb_ref[:, at(h)], q_ref[:, at(h)]], axis=0),
                    lambda h: jnp.concatenate([kn_ref[:, at(h)], ko_ref[:, at(h)]], axis=0),
                    lambda h: jnp.concatenate([vn_ref[:, at(h)], vo_ref[:, at(h)]], axis=0),
                    bias[...],
                    use,
                )
                stat_ref[...] = stat[0]

            each(half, heads)
            total = stat_ref[...]
            high = total.astype(jnp.bfloat16).astype(jnp.float32)
            middle = (total - high).astype(jnp.bfloat16).astype(jnp.float32)
            low = total - high - middle
            packed = high + pltpu.roll(middle, half, 1) + pltpu.roll(low, 2 * half, 1)
            b_ref[half] = packed.astype(jnp.bfloat16)


def scale_of(squares, width):
    total = jnp.sum(squares, axis=1, keepdims=True)
    return jnp.broadcast_to(lax.rsqrt(total * (1.0 / width) + 1e-06), squares.shape)


def spread(x, groups):
    size = LANES // groups
    lane_group = lax.broadcasted_iota(jnp.int32, x.shape, 1) // size
    return jnp.concatenate([jnp.where(lane_group == g, x, jnp.zeros_like(x)) for g in range(groups)], axis=0)


def convolve_own(att, squares, scale, taps_ref, gain_ref, bypass_ref, out_ref):
    count, rows, _ = att.shape
    scale[...] = scale_of(squares, count * LANES)

    def tiles(first):
        for c in range(UNROLL):
            cols = columns(first + c)
            x = (att[first + c].astype(jnp.float32) * scale[...] * gain_ref[:, cols]).astype(jnp.bfloat16)
            y = jnp.dot(taps_ref[first + c], spread(x, taps_ref.shape[2] // rows), preferred_element_type=jnp.float32)
            out_ref[:, cols] = y + bypass_ref[:, cols] * x.astype(jnp.float32)

    each(count, tiles)


def even_kernel(facts_ref, st_ref, q_ref, ko_ref, vo_ref, kp_ref, vp0_ref, vp1_ref, qn_ref, kn_ref, kf_ref, taps_ref, gain_ref, bypass_ref, three_ref, two_ref, out_ref, att, squares, scale, bias_own, bias_prev):
    rows = q_ref.shape[0]
    odd = facts_ref[ODD] == 1
    half = vp0_ref.shape[0] - 1
    low = jnp.where((facts_ref[ODD] == 0) & (facts_ref[BEFORE] > rows), 0, -(2**20))
    bias_own[...] = bias_of(rows, 3 * rows, 0, -2 * rows, jnp.maximum(st_ref[...], low))

    @pl.when(odd)
    def _():
        bias_prev[...] = bias_of(rows, 2 * rows, -rows, -2 * rows, st_ref[0:1, :])

        def heads(first):
            def scores(h):
                at = columns(first + h)
                key = jnp.concatenate([kf_ref[:, at], kn_ref[:, at], ko_ref[:, at]], axis=0)
                return scores_of(q_ref[:, at], key), scores_of(qn_ref[:, at], key[: 2 * rows])

            ahead = scores(0)
            for h in range(UNROLL):
                now = ahead
                if h + 1 < UNROLL:
                    ahead = scores(h + 1)
                three_ref[first + h] = raised(now[0], bias_own[...])[0]
                two_ref[first + h] = raised(now[1], bias_prev[...])[0]

        each(2 * half, heads)

    @pl.when(jnp.logical_not(odd))
    def _():
        lane = lax.broadcasted_iota(jnp.int32, (rows, LANES), 1)
        squares[...] = jnp.zeros_like(squares)
        for part, vp_ref in enumerate((vp0_ref, vp1_ref)):

            def heads(first):
                at = lambda h: columns(part * half + first + h)
                packed = vp_ref[half].astype(jnp.float32)
                stat = packed + pltpu.roll(packed, LANES - half, 1) + pltpu.roll(packed, LANES - 2 * half, 1)
                stat = jnp.where(facts_ref[BEFORE] > rows, stat, NEG)
                total = [squares[...]]

                def use(h, o, l, top):
                    lse = jnp.sum(jnp.where(lane == first + h, stat, 0.0), axis=1, keepdims=True)
                    top = top * FACTOR
                    high = jnp.maximum(top, lse)
                    here = jnp.exp2(top - high)
                    there = jnp.exp2(lse - high)
                    o = o * here + vp_ref[first + h].astype(jnp.float32) * there
                    a = (o / (l * here + there)).astype(jnp.bfloat16)
                    att[part * half + first + h] = a
                    a = a.astype(jnp.float32)
                    total[0] += a * a

                attend(
                    UNROLL,
                    lambda h: q_ref[:, at(h)],
                    lambda h: jnp.concatenate([kp_ref[:, at(h)], ko_ref[:, at(h)]], axis=0),
                    lambda h: jnp.concatenate([vp_ref[first + h], vo_ref[:, at(h)]], axis=0),
                    bias_own[:, rows:],
                    use,
                )
                squares[...] = total[0]

            each(half, heads)
        convolve_own(att, squares[...], scale, taps_ref, gain_ref, bypass_ref, out_ref)


def odd_kernel(facts_ref, three_ref, two_ref, vo_ref, vn_ref, vf0_ref, vf1_ref, taps_ref, gain_ref, bypass_ref, near_ref, sq_near_ref, out_ref, att, squares, scale):
    rows = vo_ref.shape[0]
    half = vf0_ref.shape[0] - 1

    @pl.when(facts_ref[ODD] == 1)
    def _():
        squares[...] = jnp.zeros_like(squares)
        sq_near_ref[...] = jnp.zeros_like(sq_near_ref)
        for part, vf_ref in enumerate((vf0_ref, vf1_ref)):

            def heads(first):
                total, total_near = squares[...], sq_near_ref[...]
                for h in range(UNROLL):
                    head = part * half + first + h
                    at = columns(head)
                    value = jnp.concatenate([vf_ref[first + h], vn_ref[:, at], vo_ref[:, at]], axis=0)
                    o, l = summed(three_ref[head], value)
                    a = (o / l).astype(jnp.bfloat16)
                    att[head] = a
                    a = a.astype(jnp.float32)
                    total += a * a
                    o, l = summed(two_ref[head], value[: 2 * rows])
                    a = (o / l).astype(jnp.bfloat16)
                    near_ref[head] = a
                    a = a.astype(jnp.float32)
                    total_near += a * a
                squares[...] = total
                sq_near_ref[...] = total_near

            each(half, heads)
        convolve_own(att, squares[...], scale, taps_ref, gain_ref, bypass_ref, out_ref)


def finish_kernel(facts_ref, st_ref, kp_ref, vp0_ref, vp1_ref, c_ref, near_ref, sq_ref, even_ref, odd_ref, taps_ref, gain_ref, out_ref, prev, squares, scale, bias):
    rows = st_ref.shape[0]
    half = vp0_ref.shape[0] - 1
    width = prev.shape[0] * LANES
    odd = facts_ref[ODD] == 1
    shared = facts_ref[BEFORE] > rows

    @pl.when(odd)
    def _():
        squares[...] = sq_ref[...]

        @pl.loop(0, 2 * half)
        def _(h):
            prev[h] = near_ref[h]

    @pl.when(jnp.logical_not(odd) & shared)
    def _():
        squares[...] = jnp.zeros_like(squares)

        def heads(first):
            total = squares[...]
            for h in range(UNROLL):
                a = c_ref[:, columns(first + h)]
                prev[first + h] = a
                a = a.astype(jnp.float32)
                total += a * a
            squares[...] = total

        each(2 * half, heads)

    @pl.when(jnp.logical_not(odd) & jnp.logical_not(shared))
    def _():
        squares[...] = jnp.zeros_like(squares)
        bias[...] = bias_of(rows, rows, -rows, -rows, st_ref[0:1, :])
        for part, vp_ref in enumerate((vp0_ref, vp1_ref)):

            def heads(first):
                at = lambda h: columns(part * half + first + h)
                total = [squares[...]]

                def use(h, o, l, top):
                    a = (o / l).astype(jnp.bfloat16)
                    prev[part * half + first + h] = a
                    a = a.astype(jnp.float32)
                    total[0] += a * a

                attend(UNROLL, lambda h: c_ref[:, at(h)], lambda h: kp_ref[:, at(h)], lambda h: vp_ref[first + h], bias[...], use)
                squares[...] = total[0]

            each(half, heads)

    scale[...] = scale_of(squares[...], width)

    def tiles(first):
        for c in range(UNROLL):
            cols = columns(first + c)
            x = (prev[first + c].astype(jnp.float32) * scale[...] * gain_ref[:, cols]).astype(jnp.bfloat16)
            y = jnp.dot(taps_ref[first + c], spread(x, taps_ref.shape[2] // rows), preferred_element_type=jnp.float32)
            out_ref[:, cols] = (y + jnp.where(odd, odd_ref[:, cols], even_ref[:, cols])).astype(jnp.bfloat16)

    each(2 * half, tiles)


def run(kernel, name, facts, out_shape, scratch, args):
    many = isinstance(out_shape, tuple)
    vmem = pl.BlockSpec(memory_space=pltpu.VMEM)
    return pl.pallas_call(
        kernel,
        out_shape=out_shape,
        in_specs=[pl.BlockSpec(memory_space=pltpu.SMEM)] + [vmem] * len(args),
        out_specs=(vmem,) * len(out_shape) if many else vmem,
        scratch_shapes=scratch,
        compiler_params=pltpu.CompilerParams(vmem_limit_bytes=VMEM_BYTES),
        cost_estimate=pl.CostEstimate(flops=2**20, bytes_accessed=2**16, transcendentals=0),
        name=name,
    )(facts, *args)


def shards(queries, key_rows, value_rows, lengths, norm_gain, filters, bypass):
    rows, width = queries.shape
    heads = width // HEAD_DIM
    half = heads // 2
    groups, taps = filters.shape
    n = lax.axis_size("ctx")
    st, facts = places(lengths, lax.axis_index("ctx") * rows, rows)

    back = [(i, i - 1) for i in range(2, n, 2)]
    within = [(i, i + 1) for i in range(0, n - 1, 2)]
    across = [(i, i + 1) for i in range(1, n - 1, 2)]

    bf16 = lambda *shape: jax.ShapeDtypeStruct(shape, jnp.bfloat16)
    f32 = lambda *shape: jax.ShapeDtypeStruct(shape, jnp.float32)

    query_back = permuted(queries, back)
    key_near = permuted(key_rows, within)
    value_near = permuted(value_rows, within)
    query_near = permuted(queries, within)

    taps_far, taps_near = run(
        taps_kernel,
        "taps",
        facts,
        (bf16(heads, rows, groups // heads * rows),) * 2,
        [pltpu.VMEM((rows, 2 * rows), jnp.bfloat16), pltpu.VMEM((heads, groups // heads, taps), jnp.float32)],
        (st, filters),
    )
    key_across = permuted(after(key_rows, facts), across)

    slot_b0, slot_b1, slot_c = run(
        share_kernel,
        "share",
        after(facts, taps_far),
        (bf16(half + 1, rows, HEAD_DIM), bf16(half + 1, rows, HEAD_DIM), bf16(rows, width)),
        [pltpu.VMEM((2 * rows, 2 * rows), jnp.float32), pltpu.VMEM((rows, LANES), jnp.float32)],
        (query_back, queries, key_near, key_rows, value_near, value_rows),
    )
    b_across = [permuted(x, across) for x in (slot_b0, slot_b1)]
    c_across = permuted(slot_c, across)
    key_far = permuted(after(key_across, slot_c), within)
    value_far = [permuted(x, within) for x in b_across]

    gain = norm_gain.reshape(1, width)
    skip = bypass.reshape(1, width)
    own_scratch = [
        pltpu.VMEM((heads, rows, HEAD_DIM), jnp.bfloat16),
        pltpu.VMEM((rows, LANES), jnp.float32),
        pltpu.VMEM((rows, LANES), jnp.float32),
    ]
    three, two, even_part = run(
        even_kernel,
        "even",
        facts,
        (bf16(heads, rows, 3 * rows), bf16(heads, rows, 2 * rows), f32(rows, width)),
        own_scratch + [pltpu.VMEM((rows, 3 * rows), jnp.float32), pltpu.VMEM((rows, 2 * rows), jnp.float32)],
        (st, queries, key_rows, value_rows, key_across, *b_across, query_near, key_near, key_far, taps_near, gain, skip),
    )
    near, near_squares, odd_part = run(
        odd_kernel,
        "odd",
        facts,
        (bf16(heads, rows, HEAD_DIM), f32(rows, LANES), f32(rows, width)),
        own_scratch,
        (three, two, value_rows, value_near, *value_far, taps_near, gain, skip),
    )
    return run(
        finish_kernel,
        "finish",
        facts,
        bf16(rows, width),
        [
            pltpu.VMEM((heads, rows, LANES), jnp.bfloat16),
            pltpu.VMEM((rows, LANES), jnp.float32),
            pltpu.VMEM((rows, LANES), jnp.float32),
            pltpu.VMEM((rows, rows), jnp.float32),
        ],
        (st, key_across, *b_across, c_across, near, near_squares, even_part, odd_part, taps_far, gain),
    )


def solution(mesh):
    rows = P(("dp", "ctx"), None)
    in_specs = (rows, rows, rows, P("dp"), P(), P(), P())
    return jax.shard_map(shards, mesh=mesh, in_specs=in_specs, out_specs=rows, check_vma=False)
```

```python
import math

import jax
import jax.numpy as jnp
from jax import lax
from jax.experimental import pallas as pl
from jax.experimental.pallas import tpu as pltpu
from jax.sharding import PartitionSpec as P

HEAD_DIM = 128
LANES = 128
NEG = -1e30
FACTOR = 1.0 / math.sqrt(HEAD_DIM) * math.log2(math.e)
CONTRACT_LAST = (((1,), (1,)), ((), ()))
VMEM_BYTES = 16 * 2**20
UNROLL = 8

ODD, BEFORE, NEXT_BEFORE, NEXT_AFTER = range(4)


def permuted(x, pairs):
    return lax.ppermute(x, "ctx", pairs)


def after(x, *others):
    return lax.optimization_barrier((x, *others))[0]


def facts_of(place_ref, lengths_ref, rows):
    first = place_ref[0] * rows
    after_last = first + rows

    def look(d, carry):
        begin, start, next_start, past = carry
        end = begin + lengths_ref[d]
        start = jnp.where((begin <= first) & (first < end), begin, start)
        here = (begin <= after_last) & (after_last < end)
        next_start = jnp.where(here, begin, next_start)
        past = jnp.where(here, end, past)
        return end, start, next_start, past

    _, start, next_start, past = lax.fori_loop(0, lengths_ref.shape[0], look, (jnp.int32(0), first, after_last, after_last))
    return lax.rem(place_ref[0], 2), first - start, after_last - next_start, past - after_last


def starts_of(place_ref, lengths_ref, rows):
    first = place_ref[0] * rows
    position = lax.broadcasted_iota(jnp.int32, (rows, 1), 0)

    def look(d, carry):
        begin, starts = carry
        return begin + lengths_ref[d], jnp.where(position >= begin, begin, starts)

    return lax.fori_loop(0, lengths_ref.shape[0], look, (-first, jnp.full((rows, 1), -first, jnp.int32)))[1]


def bias_of(rows, columns, row_first, key_first, start):
    row = lax.broadcasted_iota(jnp.int32, (rows, columns), 0) + row_first
    key = lax.broadcasted_iota(jnp.int32, (rows, columns), 1) + key_first
    return jnp.where((key >= start) & (key <= row), 0.0, NEG)


def scores_of(query, key):
    return lax.dot_general(query, key, CONTRACT_LAST, preferred_element_type=jnp.float32)


def raised(scores, bias):
    s = scores + bias
    top = jnp.max(s, axis=1, keepdims=True)
    return jnp.exp2((s - top) * FACTOR).astype(jnp.bfloat16), top


def summed(weights, value):
    ones = jnp.ones(value.shape, jnp.bfloat16)
    o = jnp.dot(weights, jnp.concatenate([value, ones], axis=1), preferred_element_type=jnp.float32)
    return o[:, :LANES], o[:, LANES:]


def columns(head):
    if isinstance(head, int):
        return slice(head * HEAD_DIM, (head + 1) * HEAD_DIM)
    return pl.ds(pl.multiple_of(head * HEAD_DIM, HEAD_DIM), HEAD_DIM)


def attend(heads, query, key, value, bias, use):
    ahead = scores_of(query(0), key(0))
    held = None
    for h in range(heads):
        now = ahead
        if h + 1 < heads:
            ahead = scores_of(query(h + 1), key(h + 1))
        weights, top = raised(now, bias)
        if held is not None:
            use(h - 1, *summed(held[0], value(h - 1)), held[1])
        held = weights, top
    use(heads - 1, *summed(held[0], value(heads - 1)), held[1])


def each(count, body):
    @pl.loop(0, count // UNROLL)
    def _(step):
        body(step * UNROLL)


def taps_kernel(place_ref, lengths_ref, filters_ref, far_ref, near_ref, keep, lines):
    tiles, rows, _ = far_ref.shape
    groups = filters_ref.shape[0] // tiles
    st = starts_of(place_ref, lengths_ref, rows)
    row = lax.broadcasted_iota(jnp.int32, (rows, 2 * rows), 0)
    key = lax.broadcasted_iota(jnp.int32, (rows, 2 * rows), 1) - rows
    keep[...] = jnp.where((key >= st) & (key <= row) & (key > row - rows), 1.0, 0.0).astype(jnp.bfloat16)
    tap = lax.broadcasted_iota(jnp.int32, (rows, rows), 0)
    place = lax.broadcasted_iota(jnp.int32, (rows, rows), 1)
    turn = jnp.where((tap + place == 0) | (tap + place == rows), 1.0, 0.0).astype(jnp.bfloat16)
    lines[...] = jnp.dot(filters_ref[...], turn, preferred_element_type=jnp.float32).reshape(lines.shape)

    @pl.loop(0, tiles)
    def _(c):
        some = lines[c]
        for g in range(groups):
            line = jnp.broadcast_to(some[g : g + 1], (rows, rows))
            ring = pltpu.roll(line, 0, 1, stride=1, stride_axis=0).astype(jnp.bfloat16)
            cols = slice(g * rows, (g + 1) * rows)
            far_ref[c, :, cols] = ring * keep[:, :rows]
            near_ref[c, :, cols] = ring * keep[:, rows:]


def gate_kernel(place_ref, arrived_ref, out_ref):
    out_ref[0] = place_ref[0]


def share_kernel(place_ref, lengths_ref, qb_ref, q_hbm, kn_ref, ko_hbm, vn_ref, vo_hbm, b0_ref, b1_ref, c_ref, q_ref, ko_ref, vo_ref, bias, stat_ref, sems):
    rows = q_ref.shape[0]
    moves = [
        pltpu.make_async_copy(source, target, sems.at[i])
        for i, (source, target) in enumerate(((q_hbm, q_ref), (ko_hbm, ko_ref), (vo_hbm, vo_ref)))
    ]
    for move in moves:
        move.start()
    facts = facts_of(place_ref, lengths_ref, rows)
    for move in moves:
        move.wait()
    before = facts[NEXT_BEFORE]
    past = facts[NEXT_AFTER]
    odd = facts[ODD] == 1
    half = b0_ref.shape[0] - 1

    @pl.when(odd & (before <= rows))
    def _():
        c_ref[...] = q_ref[...]
        for part, b_ref in enumerate((b0_ref, b1_ref)):

            @pl.loop(0, half)
            def _(h):
                b_ref[h] = vo_ref[:, columns(part * half + h)]

    @pl.when(odd & (before > rows))
    def _():
        bias[:rows] = bias_of(rows, 2 * rows, rows, -rows, rows - before)
        bias[rows:] = bias_of(rows, 2 * rows, 0, -rows, rows - before)
        lane = lax.broadcasted_iota(jnp.int32, (rows, LANES), 1)
        ours = lax.broadcasted_iota(jnp.int32, (rows, LANES), 0) < past
        for part, b_ref in enumerate((b0_ref, b1_ref)):
            stat_ref[...] = jnp.zeros_like(stat_ref)

            def heads(first):
                at = lambda h: columns(part * half + first + h)
                stat = [stat_ref[...]]

                def use(h, o, l, top):
                    o = (o / l).astype(jnp.bfloat16)
                    b_ref[first + h] = o[:rows]
                    c_ref[:, at(h)] = o[rows:]
                    lse = jnp.where(ours, top[:rows] * FACTOR + jnp.log2(l[:rows]), NEG)
                    stat[0] = jnp.where(lane == first + h, lse, stat[0])

                attend(
                    UNROLL,
                    lambda h: jnp.concatenate([qb_ref[:, at(h)], q_ref[:, at(h)]], axis=0),
                    lambda h: jnp.concatenate([kn_ref[:, at(h)], ko_ref[:, at(h)]], axis=0),
                    lambda h: jnp.concatenate([vn_ref[:, at(h)], vo_ref[:, at(h)]], axis=0),
                    bias[...],
                    use,
                )
                stat_ref[...] = stat[0]

            each(half, heads)
            total = stat_ref[...]
            high = total.astype(jnp.bfloat16).astype(jnp.float32)
            middle = (total - high).astype(jnp.bfloat16).astype(jnp.float32)
            low = total - high - middle
            packed = high + pltpu.roll(middle, half, 1) + pltpu.roll(low, 2 * half, 1)
            b_ref[half] = packed.astype(jnp.bfloat16)


def scale_of(squares, width):
    total = jnp.sum(squares, axis=1, keepdims=True)
    return jnp.broadcast_to(lax.rsqrt(total * (1.0 / width) + 1e-06), squares.shape)


def spread(x, groups):
    size = LANES // groups
    lane_group = lax.broadcasted_iota(jnp.int32, x.shape, 1) // size
    return jnp.concatenate([jnp.where(lane_group == g, x, jnp.zeros_like(x)) for g in range(groups)], axis=0)


def convolve_own(att, squares, scale, taps_ref, gain_ref, bypass_ref, out_ref):
    count, rows, _ = att.shape
    scale[...] = scale_of(squares, count * LANES)

    def tiles(first):
        for c in range(UNROLL):
            cols = columns(first + c)
            x = (att[first + c].astype(jnp.float32) * scale[...] * gain_ref[:, cols]).astype(jnp.bfloat16)
            y = jnp.dot(taps_ref[first + c], spread(x, taps_ref.shape[2] // rows), preferred_element_type=jnp.float32)
            out_ref[:, cols] = y + bypass_ref[:, cols] * x.astype(jnp.float32)

    each(count, tiles)


def even_kernel(place_ref, lengths_ref, q_ref, ko_ref, vo_ref, kp_ref, vp0_ref, vp1_ref, qn_ref, kn_ref, kf_ref, taps_ref, gain_ref, bypass_ref, three_ref, two_ref, out_ref, att, squares, scale, bias_own, bias_prev):
    rows = q_ref.shape[0]
    facts = facts_of(place_ref, lengths_ref, rows)
    odd = facts[ODD] == 1
    half = vp0_ref.shape[0] - 1
    low = jnp.where((facts[ODD] == 0) & (facts[BEFORE] > rows), 0, -(2**20))
    bias_own[...] = bias_of(rows, 3 * rows, 0, -2 * rows, jnp.maximum(starts_of(place_ref, lengths_ref, rows), low))

    @pl.when(odd)
    def _():
        bias_prev[...] = bias_of(rows, 2 * rows, -rows, -2 * rows, -facts[BEFORE])

        def heads(first):
            def scores(h):
                at = columns(first + h)
                key = jnp.concatenate([kf_ref[:, at], kn_ref[:, at], ko_ref[:, at]], axis=0)
                return scores_of(q_ref[:, at], key), scores_of(qn_ref[:, at], key[: 2 * rows])

            ahead = scores(0)
            for h in range(UNROLL):
                now = ahead
                if h + 1 < UNROLL:
                    ahead = scores(h + 1)
                three_ref[first + h] = raised(now[0], bias_own[...])[0]
                two_ref[first + h] = raised(now[1], bias_prev[...])[0]

        each(2 * half, heads)

    @pl.when(jnp.logical_not(odd))
    def _():
        lane = lax.broadcasted_iota(jnp.int32, (rows, LANES), 1)
        squares[...] = jnp.zeros_like(squares)
        for part, vp_ref in enumerate((vp0_ref, vp1_ref)):

            def heads(first):
                at = lambda h: columns(part * half + first + h)
                packed = vp_ref[half].astype(jnp.float32)
                stat = packed + pltpu.roll(packed, LANES - half, 1) + pltpu.roll(packed, LANES - 2 * half, 1)
                stat = jnp.where(facts[BEFORE] > rows, stat, NEG)
                total = [squares[...]]

                def use(h, o, l, top):
                    lse = jnp.sum(jnp.where(lane == first + h, stat, 0.0), axis=1, keepdims=True)
                    top = top * FACTOR
                    high = jnp.maximum(top, lse)
                    here = jnp.exp2(top - high)
                    there = jnp.exp2(lse - high)
                    o = o * here + vp_ref[first + h].astype(jnp.float32) * there
                    a = (o / (l * here + there)).astype(jnp.bfloat16)
                    att[part * half + first + h] = a
                    a = a.astype(jnp.float32)
                    total[0] += a * a

                attend(
                    UNROLL,
                    lambda h: q_ref[:, at(h)],
                    lambda h: jnp.concatenate([kp_ref[:, at(h)], ko_ref[:, at(h)]], axis=0),
                    lambda h: jnp.concatenate([vp_ref[first + h], vo_ref[:, at(h)]], axis=0),
                    bias_own[:, rows:],
                    use,
                )
                squares[...] = total[0]

            each(half, heads)
        convolve_own(att, squares[...], scale, taps_ref, gain_ref, bypass_ref, out_ref)


def odd_kernel(place_ref, lengths_ref, three_ref, two_ref, vo_ref, vn_ref, vf0_ref, vf1_ref, taps_ref, gain_ref, bypass_ref, near_ref, sq_near_ref, out_ref, att, squares, scale):
    rows = vo_ref.shape[0]
    half = vf0_ref.shape[0] - 1

    @pl.when(lax.rem(place_ref[0], 2) == 1)
    def _():
        squares[...] = jnp.zeros_like(squares)
        sq_near_ref[...] = jnp.zeros_like(sq_near_ref)
        for part, vf_ref in enumerate((vf0_ref, vf1_ref)):

            def heads(first):
                total, total_near = squares[...], sq_near_ref[...]
                for h in range(UNROLL):
                    head = part * half + first + h
                    at = columns(head)
                    value = jnp.concatenate([vf_ref[first + h], vn_ref[:, at], vo_ref[:, at]], axis=0)
                    o, l = summed(three_ref[head], value)
                    a = (o / l).astype(jnp.bfloat16)
                    att[head] = a
                    a = a.astype(jnp.float32)
                    total += a * a
                    o, l = summed(two_ref[head], value[: 2 * rows])
                    a = (o / l).astype(jnp.bfloat16)
                    near_ref[head] = a
                    a = a.astype(jnp.float32)
                    total_near += a * a
                squares[...] = total
                sq_near_ref[...] = total_near

            each(half, heads)
        convolve_own(att, squares[...], scale, taps_ref, gain_ref, bypass_ref, out_ref)


def finish_kernel(place_ref, lengths_ref, kp_ref, vp0_ref, vp1_ref, c_ref, near_ref, sq_ref, even_ref, odd_ref, taps_ref, gain_ref, out_ref, prev, squares, scale, bias):
    rows = c_ref.shape[0]
    facts = facts_of(place_ref, lengths_ref, rows)
    half = vp0_ref.shape[0] - 1
    width = prev.shape[0] * LANES
    odd = facts[ODD] == 1
    shared = facts[BEFORE] > rows

    @pl.when(odd)
    def _():
        squares[...] = sq_ref[...]

        @pl.loop(0, 2 * half)
        def _(h):
            prev[h] = near_ref[h]

    @pl.when(jnp.logical_not(odd) & shared)
    def _():
        squares[...] = jnp.zeros_like(squares)

        def heads(first):
            total = squares[...]
            for h in range(UNROLL):
                a = c_ref[:, columns(first + h)]
                prev[first + h] = a
                a = a.astype(jnp.float32)
                total += a * a
            squares[...] = total

        each(2 * half, heads)

    @pl.when(jnp.logical_not(odd) & jnp.logical_not(shared))
    def _():
        squares[...] = jnp.zeros_like(squares)
        bias[...] = bias_of(rows, rows, -rows, -rows, -facts[BEFORE])
        for part, vp_ref in enumerate((vp0_ref, vp1_ref)):

            def heads(first):
                at = lambda h: columns(part * half + first + h)
                total = [squares[...]]

                def use(h, o, l, top):
                    a = (o / l).astype(jnp.bfloat16)
                    prev[part * half + first + h] = a
                    a = a.astype(jnp.float32)
                    total[0] += a * a

                attend(UNROLL, lambda h: c_ref[:, at(h)], lambda h: kp_ref[:, at(h)], lambda h: vp_ref[first + h], bias[...], use)
                squares[...] = total[0]

            each(half, heads)

    scale[...] = scale_of(squares[...], width)

    def tiles(first):
        for c in range(UNROLL):
            cols = columns(first + c)
            x = (prev[first + c].astype(jnp.float32) * scale[...] * gain_ref[:, cols]).astype(jnp.bfloat16)
            y = jnp.dot(taps_ref[first + c], spread(x, taps_ref.shape[2] // rows), preferred_element_type=jnp.float32)
            out_ref[:, cols] = (y + jnp.where(odd, odd_ref[:, cols], even_ref[:, cols])).astype(jnp.bfloat16)

    each(2 * half, tiles)


def run(kernel, name, known, out_shape, scratch, args, in_place=()):
    many = isinstance(out_shape, tuple)
    vmem = pl.BlockSpec(memory_space=pltpu.VMEM)
    specs = [pl.BlockSpec(memory_space=pltpu.MemorySpace.HBM) if i in in_place else vmem for i in range(len(args))]
    return pl.pallas_call(
        kernel,
        out_shape=out_shape,
        in_specs=[pl.BlockSpec(memory_space=pltpu.SMEM)] * 2 + specs,
        out_specs=(vmem,) * len(out_shape) if many else vmem,
        scratch_shapes=scratch,
        compiler_params=pltpu.CompilerParams(vmem_limit_bytes=VMEM_BYTES),
        cost_estimate=pl.CostEstimate(flops=2**20, bytes_accessed=2**16, transcendentals=0),
        name=name,
    )(*known, *args)


def shards(queries, key_rows, value_rows, lengths, norm_gain, filters, bypass):
    rows, width = queries.shape
    heads = width // HEAD_DIM
    half = heads // 2
    groups, taps = filters.shape
    n = lax.axis_size("ctx")
    known = lax.axis_index("ctx").astype(jnp.int32).reshape(1), lengths

    back = [(i, i - 1) for i in range(2, n, 2)]
    within = [(i, i + 1) for i in range(0, n - 1, 2)]
    across = [(i, i + 1) for i in range(1, n - 1, 2)]

    bf16 = lambda *shape: jax.ShapeDtypeStruct(shape, jnp.bfloat16)
    f32 = lambda *shape: jax.ShapeDtypeStruct(shape, jnp.float32)

    query_back = permuted(queries, back)
    query_near = permuted(queries, within)
    key_near = permuted(key_rows, within)
    value_near = permuted(value_rows, within)

    key_across = permuted(after(key_rows, query_near), across)

    wide = bf16(rows, width)
    smem = pl.BlockSpec(memory_space=pltpu.SMEM)
    place = pl.pallas_call(
        gate_kernel,
        out_shape=jax.ShapeDtypeStruct((1,), jnp.int32),
        in_specs=[smem, pl.BlockSpec(memory_space=pl.ANY)],
        out_specs=smem,
        cost_estimate=pl.CostEstimate(flops=0, bytes_accessed=16 * 2**20, transcendentals=0),
        name="gate",
    )(known[0], query_back)
    slot_b0, slot_b1, slot_c, query_own, key_own, value_own = run(
        share_kernel,
        "share",
        (place, lengths),
        (bf16(half + 1, rows, HEAD_DIM), bf16(half + 1, rows, HEAD_DIM), wide, wide, wide, wide),
        [pltpu.VMEM((2 * rows, 2 * rows), jnp.float32), pltpu.VMEM((rows, LANES), jnp.float32), pltpu.SemaphoreType.DMA((3,))],
        (query_back, queries, key_near, key_rows, value_near, value_rows),
        (1, 3, 5),
    )
    b_across = [permuted(x, across) for x in (slot_b0, slot_b1)]
    c_across = permuted(slot_c, across)
    key_far = permuted(after(key_across, slot_c), within)
    taps_far, taps_near = run(
        taps_kernel,
        "taps",
        (known[0], after(lengths, slot_c)),
        (bf16(heads, rows, groups // heads * rows),) * 2,
        [pltpu.VMEM((rows, 2 * rows), jnp.bfloat16), pltpu.VMEM((heads, groups // heads, taps), jnp.float32)],
        (filters,),
    )
    value_far = [permuted(after(x, taps_far), within) for x in b_across]

    gain = norm_gain.reshape(1, width)
    skip = bypass.reshape(1, width)
    own_scratch = [
        pltpu.VMEM((heads, rows, HEAD_DIM), jnp.bfloat16),
        pltpu.VMEM((rows, LANES), jnp.float32),
        pltpu.VMEM((rows, LANES), jnp.float32),
    ]
    three, two, even_part = run(
        even_kernel,
        "even",
        known,
        (bf16(heads, rows, 3 * rows), bf16(heads, rows, 2 * rows), f32(rows, width)),
        own_scratch + [pltpu.VMEM((rows, 3 * rows), jnp.float32), pltpu.VMEM((rows, 2 * rows), jnp.float32)],
        (query_own, key_own, value_own, key_across, *b_across, query_near, key_near, key_far, taps_near, gain, skip),
    )
    near, near_squares, odd_part = run(
        odd_kernel,
        "odd",
        known,
        (bf16(heads, rows, HEAD_DIM), f32(rows, LANES), f32(rows, width)),
        own_scratch,
        (three, two, value_own, value_near, *value_far, taps_near, gain, skip),
    )
    return run(
        finish_kernel,
        "finish",
        known,
        bf16(rows, width),
        [
            pltpu.VMEM((heads, rows, LANES), jnp.bfloat16),
            pltpu.VMEM((rows, LANES), jnp.float32),
            pltpu.VMEM((rows, LANES), jnp.float32),
            pltpu.VMEM((rows, rows), jnp.float32),
        ],
        (key_across, *b_across, c_across, near, near_squares, even_part, odd_part, taps_far, gain),
    )


def solution(mesh):
    rows = P(("dp", "ctx"), None)
    in_specs = (rows, rows, rows, P("dp"), P(), P(), P())
    return jax.shard_map(shards, mesh=mesh, in_specs=in_specs, out_specs=rows, check_vma=False)
```

```python
import math

import jax
import jax.numpy as jnp
from jax import lax
from jax.experimental import pallas as pl
from jax.experimental.pallas import tpu as pltpu
from jax.sharding import PartitionSpec as P

HEAD_DIM = 128
LANES = 128
NEG = -1e30
FACTOR = 1.0 / math.sqrt(HEAD_DIM) * math.log2(math.e)
CONTRACT_LAST = (((1,), (1,)), ((), ()))
VMEM_BYTES = 16 * 2**20
UNROLL = 8

ODD, BEFORE, NEXT_BEFORE, NEXT_AFTER = range(4)


def permuted(x, pairs):
    return lax.ppermute(x, "ctx", pairs)


def after(x, *others):
    return lax.optimization_barrier((x, *others))[0]


def places(lengths, first_row, count):
    ends = jnp.cumsum(lengths)
    position = first_row + jnp.arange(count + 1, dtype=jnp.int32)
    passed = ends[None, :] <= position[:, None]
    starts = jnp.sum(jnp.where(passed, lengths[None, :], 0), axis=1) - first_row
    past = jnp.min(jnp.where(passed[count], jnp.int32(2**30), ends)) - first_row - count
    odd = (first_row // count) % 2
    facts = jnp.stack([odd, -starts[0], count - starts[count], past]).astype(jnp.int32)
    return starts[:count].astype(jnp.int32).reshape(count, 1), facts


def bias_of(rows, columns, row_first, key_first, start):
    row = lax.broadcasted_iota(jnp.int32, (rows, columns), 0) + row_first
    key = lax.broadcasted_iota(jnp.int32, (rows, columns), 1) + key_first
    return jnp.where((key >= start) & (key <= row), 0.0, NEG)


def scores_of(query, key):
    return lax.dot_general(query, key, CONTRACT_LAST, preferred_element_type=jnp.float32)


def raised(scores, bias):
    s = scores + bias
    top = jnp.max(s, axis=1, keepdims=True)
    return jnp.exp2((s - top) * FACTOR).astype(jnp.bfloat16), top


def summed(weights, value):
    ones = jnp.ones(value.shape, jnp.bfloat16)
    o = jnp.dot(weights, jnp.concatenate([value, ones], axis=1), preferred_element_type=jnp.float32)
    return o[:, :LANES], o[:, LANES:]


def columns(head):
    if isinstance(head, int):
        return slice(head * HEAD_DIM, (head + 1) * HEAD_DIM)
    return pl.ds(pl.multiple_of(head * HEAD_DIM, HEAD_DIM), HEAD_DIM)


def attend(heads, query, key, value, bias, use):
    ahead = scores_of(query(0), key(0))
    held = None
    for h in range(heads):
        now = ahead
        if h + 1 < heads:
            ahead = scores_of(query(h + 1), key(h + 1))
        weights, top = raised(now, bias)
        if held is not None:
            use(h - 1, *summed(held[0], value(h - 1)), held[1])
        held = weights, top
    use(heads - 1, *summed(held[0], value(heads - 1)), held[1])


def each(count, body):
    @pl.loop(0, count // UNROLL)
    def _(step):
        body(step * UNROLL)


def taps_kernel(facts_ref, st_ref, filters_ref, far_ref, near_ref, keep, lines):
    rows = st_ref.shape[0]
    tiles = far_ref.shape[0]
    groups = filters_ref.shape[0] // tiles
    st = st_ref[...]
    row = lax.broadcasted_iota(jnp.int32, (rows, 2 * rows), 0)
    key = lax.broadcasted_iota(jnp.int32, (rows, 2 * rows), 1) - rows
    keep[...] = jnp.where((key >= st) & (key <= row) & (key > row - rows), 1.0, 0.0).astype(jnp.bfloat16)
    tap = lax.broadcasted_iota(jnp.int32, (rows, rows), 0)
    place = lax.broadcasted_iota(jnp.int32, (rows, rows), 1)
    turn = jnp.where((tap + place == 0) | (tap + place == rows), 1.0, 0.0).astype(jnp.bfloat16)
    lines[...] = jnp.dot(filters_ref[...], turn, preferred_element_type=jnp.float32).reshape(lines.shape)

    @pl.loop(0, tiles)
    def _(c):
        some = lines[c]
        for g in range(groups):
            line = jnp.broadcast_to(some[g : g + 1], (rows, rows))
            ring = pltpu.roll(line, 0, 1, stride=1, stride_axis=0).astype(jnp.bfloat16)
            cols = slice(g * rows, (g + 1) * rows)
            far_ref[c, :, cols] = ring * keep[:, :rows]
            near_ref[c, :, cols] = ring * keep[:, rows:]


def gate_kernel(facts_ref, arrived_ref, out_ref):
    for i in range(out_ref.shape[0]):
        out_ref[i] = facts_ref[i]


def share_kernel(facts_ref, qb_ref, q_hbm, kn_ref, ko_hbm, vn_ref, vo_hbm, b0_ref, b1_ref, c_ref, q_ref, ko_ref, vo_ref, bias, stat_ref, sems):
    rows = q_ref.shape[0]
    moves = [
        pltpu.make_async_copy(source, target, sems.at[i])
        for i, (source, target) in enumerate(((q_hbm, q_ref), (ko_hbm, ko_ref), (vo_hbm, vo_ref)))
    ]
    for move in moves:
        move.start()
    for move in moves:
        move.wait()
    before = facts_ref[NEXT_BEFORE]
    past = facts_ref[NEXT_AFTER]
    odd = facts_ref[ODD] == 1
    half = b0_ref.shape[0] - 1

    @pl.when(odd & (before <= rows))
    def _():
        c_ref[...] = q_ref[...]
        for part, b_ref in enumerate((b0_ref, b1_ref)):

            @pl.loop(0, half)
            def _(h):
                b_ref[h] = vo_ref[:, columns(part * half + h)]

    @pl.when(odd & (before > rows))
    def _():
        bias[:rows] = bias_of(rows, 2 * rows, rows, -rows, rows - before)
        bias[rows:] = bias_of(rows, 2 * rows, 0, -rows, rows - before)
        lane = lax.broadcasted_iota(jnp.int32, (rows, LANES), 1)
        ours = lax.broadcasted_iota(jnp.int32, (rows, LANES), 0) < past
        for part, b_ref in enumerate((b0_ref, b1_ref)):
            stat_ref[...] = jnp.zeros_like(stat_ref)

            def heads(first):
                at = lambda h: columns(part * half + first + h)
                stat = [stat_ref[...]]

                def use(h, o, l, top):
                    o = (o / l).astype(jnp.bfloat16)
                    b_ref[first + h] = o[:rows]
                    c_ref[:, at(h)] = o[rows:]
                    lse = jnp.where(ours, top[:rows] * FACTOR + jnp.log2(l[:rows]), NEG)
                    stat[0] = jnp.where(lane == first + h, lse, stat[0])

                attend(
                    UNROLL,
                    lambda h: jnp.concatenate([qb_ref[:, at(h)], q_ref[:, at(h)]], axis=0),
                    lambda h: jnp.concatenate([kn_ref[:, at(h)], ko_ref[:, at(h)]], axis=0),
                    lambda h: jnp.concatenate([vn_ref[:, at(h)], vo_ref[:, at(h)]], axis=0),
                    bias[...],
                    use,
                )
                stat_ref[...] = stat[0]

            each(half, heads)
            total = stat_ref[...]
            high = total.astype(jnp.bfloat16).astype(jnp.float32)
            middle = (total - high).astype(jnp.bfloat16).astype(jnp.float32)
            low = total - high - middle
            packed = high + pltpu.roll(middle, half, 1) + pltpu.roll(low, 2 * half, 1)
            b_ref[half] = packed.astype(jnp.bfloat16)


def scale_of(squares, width):
    total = jnp.sum(squares, axis=1, keepdims=True)
    return jnp.broadcast_to(lax.rsqrt(total * (1.0 / width) + 1e-06), squares.shape)


def spread(x, groups):
    size = LANES // groups
    lane_group = lax.broadcasted_iota(jnp.int32, x.shape, 1) // size
    return jnp.concatenate([jnp.where(lane_group == g, x, jnp.zeros_like(x)) for g in range(groups)], axis=0)


def convolve_own(att, squares, scale, taps_ref, gain_ref, bypass_ref, out_ref):
    count, rows, _ = att.shape
    scale[...] = scale_of(squares, count * LANES)

    def tiles(first):
        for c in range(UNROLL):
            cols = columns(first + c)
            x = (att[first + c].astype(jnp.float32) * scale[...] * gain_ref[:, cols]).astype(jnp.bfloat16)
            y = jnp.dot(taps_ref[first + c], spread(x, taps_ref.shape[2] // rows), preferred_element_type=jnp.float32)
            out_ref[:, cols] = y + bypass_ref[:, cols] * x.astype(jnp.float32)

    each(count, tiles)


def even_kernel(facts_ref, st_ref, q_ref, ko_ref, vo_ref, kp_ref, vp0_ref, vp1_ref, qn_ref, kn_ref, kf_ref, taps_ref, gain_ref, bypass_ref, three_ref, two_ref, out_ref, att, squares, scale, bias_own, bias_prev):
    rows = q_ref.shape[0]
    odd = facts_ref[ODD] == 1
    half = vp0_ref.shape[0] - 1
    low = jnp.where((facts_ref[ODD] == 0) & (facts_ref[BEFORE] > rows), 0, -(2**20))
    bias_own[...] = bias_of(rows, 3 * rows, 0, -2 * rows, jnp.maximum(st_ref[...], low))

    @pl.when(odd)
    def _():
        bias_prev[...] = bias_of(rows, 2 * rows, -rows, -2 * rows, st_ref[0:1, :])

        def heads(first):
            def scores(h):
                at = columns(first + h)
                key = jnp.concatenate([kf_ref[:, at], kn_ref[:, at], ko_ref[:, at]], axis=0)
                return scores_of(q_ref[:, at], key), scores_of(qn_ref[:, at], key[: 2 * rows])

            ahead = scores(0)
            for h in range(UNROLL):
                now = ahead
                if h + 1 < UNROLL:
                    ahead = scores(h + 1)
                three_ref[first + h] = raised(now[0], bias_own[...])[0]
                two_ref[first + h] = raised(now[1], bias_prev[...])[0]

        each(2 * half, heads)

    @pl.when(jnp.logical_not(odd))
    def _():
        lane = lax.broadcasted_iota(jnp.int32, (rows, LANES), 1)
        squares[...] = jnp.zeros_like(squares)
        for part, vp_ref in enumerate((vp0_ref, vp1_ref)):

            def heads(first):
                at = lambda h: columns(part * half + first + h)
                packed = vp_ref[half].astype(jnp.float32)
                stat = packed + pltpu.roll(packed, LANES - half, 1) + pltpu.roll(packed, LANES - 2 * half, 1)
                stat = jnp.where(facts_ref[BEFORE] > rows, stat, NEG)
                total = [squares[...]]

                def use(h, o, l, top):
                    lse = jnp.sum(jnp.where(lane == first + h, stat, 0.0), axis=1, keepdims=True)
                    top = top * FACTOR
                    high = jnp.maximum(top, lse)
                    here = jnp.exp2(top - high)
                    there = jnp.exp2(lse - high)
                    o = o * here + vp_ref[first + h].astype(jnp.float32) * there
                    a = (o / (l * here + there)).astype(jnp.bfloat16)
                    att[part * half + first + h] = a
                    a = a.astype(jnp.float32)
                    total[0] += a * a

                attend(
                    UNROLL,
                    lambda h: q_ref[:, at(h)],
                    lambda h: jnp.concatenate([kp_ref[:, at(h)], ko_ref[:, at(h)]], axis=0),
                    lambda h: jnp.concatenate([vp_ref[first + h], vo_ref[:, at(h)]], axis=0),
                    bias_own[:, rows:],
                    use,
                )
                squares[...] = total[0]

            each(half, heads)
        convolve_own(att, squares[...], scale, taps_ref, gain_ref, bypass_ref, out_ref)


def odd_kernel(facts_ref, three_ref, two_ref, vo_ref, vn_ref, vf0_ref, vf1_ref, taps_ref, gain_ref, bypass_ref, near_ref, sq_near_ref, out_ref, att, squares, scale):
    rows = vo_ref.shape[0]
    half = vf0_ref.shape[0] - 1

    @pl.when(facts_ref[ODD] == 1)
    def _():
        squares[...] = jnp.zeros_like(squares)
        sq_near_ref[...] = jnp.zeros_like(sq_near_ref)
        for part, vf_ref in enumerate((vf0_ref, vf1_ref)):

            def heads(first):
                total, total_near = squares[...], sq_near_ref[...]
                for h in range(UNROLL):
                    head = part * half + first + h
                    at = columns(head)
                    value = jnp.concatenate([vf_ref[first + h], vn_ref[:, at], vo_ref[:, at]], axis=0)
                    o, l = summed(three_ref[head], value)
                    a = (o / l).astype(jnp.bfloat16)
                    att[head] = a
                    a = a.astype(jnp.float32)
                    total += a * a
                    o, l = summed(two_ref[head], value[: 2 * rows])
                    a = (o / l).astype(jnp.bfloat16)
                    near_ref[head] = a
                    a = a.astype(jnp.float32)
                    total_near += a * a
                squares[...] = total
                sq_near_ref[...] = total_near

            each(half, heads)
        convolve_own(att, squares[...], scale, taps_ref, gain_ref, bypass_ref, out_ref)


def finish_kernel(facts_ref, st_ref, kp_ref, vp0_ref, vp1_ref, c_ref, near_ref, sq_ref, even_ref, odd_ref, taps_ref, gain_ref, out_ref, prev, squares, scale, bias):
    rows = st_ref.shape[0]
    half = vp0_ref.shape[0] - 1
    width = prev.shape[0] * LANES
    odd = facts_ref[ODD] == 1
    shared = facts_ref[BEFORE] > rows

    @pl.when(odd)
    def _():
        squares[...] = sq_ref[...]

        @pl.loop(0, 2 * half)
        def _(h):
            prev[h] = near_ref[h]

    @pl.when(jnp.logical_not(odd) & shared)
    def _():
        squares[...] = jnp.zeros_like(squares)

        def heads(first):
            total = squares[...]
            for h in range(UNROLL):
                a = c_ref[:, columns(first + h)]
                prev[first + h] = a
                a = a.astype(jnp.float32)
                total += a * a
            squares[...] = total

        each(2 * half, heads)

    @pl.when(jnp.logical_not(odd) & jnp.logical_not(shared))
    def _():
        squares[...] = jnp.zeros_like(squares)
        bias[...] = bias_of(rows, rows, -rows, -rows, st_ref[0:1, :])
        for part, vp_ref in enumerate((vp0_ref, vp1_ref)):

            def heads(first):
                at = lambda h: columns(part * half + first + h)
                total = [squares[...]]

                def use(h, o, l, top):
                    a = (o / l).astype(jnp.bfloat16)
                    prev[part * half + first + h] = a
                    a = a.astype(jnp.float32)
                    total[0] += a * a

                attend(UNROLL, lambda h: c_ref[:, at(h)], lambda h: kp_ref[:, at(h)], lambda h: vp_ref[first + h], bias[...], use)
                squares[...] = total[0]

            each(half, heads)

    scale[...] = scale_of(squares[...], width)

    def tiles(first):
        for c in range(UNROLL):
            cols = columns(first + c)
            x = (prev[first + c].astype(jnp.float32) * scale[...] * gain_ref[:, cols]).astype(jnp.bfloat16)
            y = jnp.dot(taps_ref[first + c], spread(x, taps_ref.shape[2] // rows), preferred_element_type=jnp.float32)
            out_ref[:, cols] = (y + jnp.where(odd, odd_ref[:, cols], even_ref[:, cols])).astype(jnp.bfloat16)

    each(2 * half, tiles)


def run(kernel, name, facts, out_shape, scratch, args, in_place=()):
    many = isinstance(out_shape, tuple)
    vmem = pl.BlockSpec(memory_space=pltpu.VMEM)
    specs = [pl.BlockSpec(memory_space=pltpu.MemorySpace.HBM) if i in in_place else vmem for i in range(len(args))]
    return pl.pallas_call(
        kernel,
        out_shape=out_shape,
        in_specs=[pl.BlockSpec(memory_space=pltpu.SMEM)] + specs,
        out_specs=(vmem,) * len(out_shape) if many else vmem,
        scratch_shapes=scratch,
        compiler_params=pltpu.CompilerParams(vmem_limit_bytes=VMEM_BYTES),
        cost_estimate=pl.CostEstimate(flops=2**20, bytes_accessed=2**16, transcendentals=0),
        name=name,
    )(facts, *args)


def shards(queries, key_rows, value_rows, lengths, norm_gain, filters, bypass):
    rows, width = queries.shape
    heads = width // HEAD_DIM
    half = heads // 2
    groups, taps = filters.shape
    n = lax.axis_size("ctx")
    st, facts = places(lengths, lax.axis_index("ctx") * rows, rows)

    back = [(i, i - 1) for i in range(2, n, 2)]
    within = [(i, i + 1) for i in range(0, n - 1, 2)]
    across = [(i, i + 1) for i in range(1, n - 1, 2)]

    bf16 = lambda *shape: jax.ShapeDtypeStruct(shape, jnp.bfloat16)
    f32 = lambda *shape: jax.ShapeDtypeStruct(shape, jnp.float32)

    query_back = permuted(queries, back)
    key_near = permuted(key_rows, within)
    value_near = permuted(value_rows, within)
    query_near = permuted(queries, within)

    key_across = permuted(after(key_rows, facts), across)

    wide = bf16(rows, width)
    smem = pl.BlockSpec(memory_space=pltpu.SMEM)
    gated = pl.pallas_call(
        gate_kernel,
        out_shape=jax.ShapeDtypeStruct(facts.shape, jnp.int32),
        in_specs=[smem, pl.BlockSpec(memory_space=pl.ANY)],
        out_specs=smem,
        cost_estimate=pl.CostEstimate(flops=0, bytes_accessed=16 * 2**20, transcendentals=0),
        name="gate",
    )(facts, query_back)
    slot_b0, slot_b1, slot_c, query_own, key_own, value_own = run(
        share_kernel,
        "share",
        after(gated, query_near),
        (bf16(half + 1, rows, HEAD_DIM), bf16(half + 1, rows, HEAD_DIM), wide, wide, wide, wide),
        [pltpu.VMEM((2 * rows, 2 * rows), jnp.float32), pltpu.VMEM((rows, LANES), jnp.float32), pltpu.SemaphoreType.DMA((3,))],
        (query_back, queries, key_near, key_rows, value_near, value_rows),
        (1, 3, 5),
    )
    b_across = [permuted(x, across) for x in (slot_b0, slot_b1)]
    c_across = permuted(slot_c, across)
    taps_far, taps_near = run(
        taps_kernel,
        "taps",
        after(facts, slot_c),
        (bf16(heads, rows, groups // heads * rows),) * 2,
        [pltpu.VMEM((rows, 2 * rows), jnp.bfloat16), pltpu.VMEM((heads, groups // heads, taps), jnp.float32)],
        (st, filters),
    )
    key_far = permuted(after(key_across, taps_far), within)
    value_far = [permuted(after(x, taps_far), within) for x in b_across]

    gain = norm_gain.reshape(1, width)
    skip = bypass.reshape(1, width)
    own_scratch = [
        pltpu.VMEM((heads, rows, HEAD_DIM), jnp.bfloat16),
        pltpu.VMEM((rows, LANES), jnp.float32),
        pltpu.VMEM((rows, LANES), jnp.float32),
    ]
    three, two, even_part = run(
        even_kernel,
        "even",
        facts,
        (bf16(heads, rows, 3 * rows), bf16(heads, rows, 2 * rows), f32(rows, width)),
        own_scratch + [pltpu.VMEM((rows, 3 * rows), jnp.float32), pltpu.VMEM((rows, 2 * rows), jnp.float32)],
        (st, query_own, key_own, value_own, key_across, *b_across, query_near, key_near, key_far, taps_near, gain, skip),
    )
    near, near_squares, odd_part = run(
        odd_kernel,
        "odd",
        facts,
        (bf16(heads, rows, HEAD_DIM), f32(rows, LANES), f32(rows, width)),
        own_scratch,
        (three, two, value_own, value_near, *value_far, taps_near, gain, skip),
    )
    return run(
        finish_kernel,
        "finish",
        facts,
        bf16(rows, width),
        [
            pltpu.VMEM((heads, rows, LANES), jnp.bfloat16),
            pltpu.VMEM((rows, LANES), jnp.float32),
            pltpu.VMEM((rows, LANES), jnp.float32),
            pltpu.VMEM((rows, rows), jnp.float32),
        ],
        (st, key_across, *b_across, c_across, near, near_squares, even_part, odd_part, taps_far, gain),
    )


def solution(mesh):
    rows = P(("dp", "ctx"), None)
    in_specs = (rows, rows, rows, P("dp"), P(), P(), P())
    return jax.shard_map(shards, mesh=mesh, in_specs=in_specs, out_specs=rows, check_vma=False)
```

```python
import math

import jax
import jax.numpy as jnp
from jax import lax
from jax.experimental import pallas as pl
from jax.experimental.pallas import tpu as pltpu
from jax.sharding import PartitionSpec as P

HEAD_DIM = 128
LANES = 128
NEG = -1e30
FACTOR = 1.0 / math.sqrt(HEAD_DIM) * math.log2(math.e)
CONTRACT_LAST = (((1,), (1,)), ((), ()))
VMEM_BYTES = 10 * 2**20
UNROLL = 8

ODD, BEFORE, NEXT_BEFORE, NEXT_AFTER = range(4)


def permuted(x, pairs):
    return lax.ppermute(x, "ctx", pairs)


def after(x, *others):
    return lax.optimization_barrier((x, *others))[0]


def places(lengths, first_row, count):
    ends = jnp.cumsum(lengths)
    position = first_row + jnp.arange(count + 1, dtype=jnp.int32)
    passed = ends[None, :] <= position[:, None]
    starts = jnp.sum(jnp.where(passed, lengths[None, :], 0), axis=1) - first_row
    past = jnp.min(jnp.where(passed[count], jnp.int32(2**30), ends)) - first_row - count
    odd = (first_row // count) % 2
    facts = jnp.stack([odd, -starts[0], count - starts[count], past]).astype(jnp.int32)
    return starts[:count].astype(jnp.int32).reshape(count, 1), facts


def bias_of(rows, columns, row_first, key_first, start):
    row = lax.broadcasted_iota(jnp.int32, (rows, columns), 0) + row_first
    key = lax.broadcasted_iota(jnp.int32, (rows, columns), 1) + key_first
    return jnp.where((key >= start) & (key <= row), 0.0, NEG)


def scores_of(query, key):
    return lax.dot_general(query, key, CONTRACT_LAST, preferred_element_type=jnp.float32)


def raised(scores, bias):
    s = scores + bias
    top = jnp.max(s, axis=1, keepdims=True)
    return jnp.exp2((s - top) * FACTOR).astype(jnp.bfloat16), top


def summed(weights, value):
    ones = jnp.ones(value.shape, jnp.bfloat16)
    o = jnp.dot(weights, jnp.concatenate([value, ones], axis=1), preferred_element_type=jnp.float32)
    return o[:, :LANES], o[:, LANES:]


def columns(head):
    if isinstance(head, int):
        return slice(head * HEAD_DIM, (head + 1) * HEAD_DIM)
    return pl.ds(pl.multiple_of(head * HEAD_DIM, HEAD_DIM), HEAD_DIM)


def attend(heads, query, key, value, bias, use):
    ahead = scores_of(query(0), key(0))
    held = None
    for h in range(heads):
        now = ahead
        if h + 1 < heads:
            ahead = scores_of(query(h + 1), key(h + 1))
        weights, top = raised(now, bias)
        if held is not None:
            use(h - 1, *summed(held[0], value(h - 1)), held[1])
        held = weights, top
    use(heads - 1, *summed(held[0], value(heads - 1)), held[1])


def each(count, body):
    @pl.loop(0, count // UNROLL)
    def _(step):
        body(step * UNROLL)


def taps_kernel(facts_ref, st_ref, filters_ref, far_ref, near_ref, keep, lines):
    rows = st_ref.shape[0]
    tiles = far_ref.shape[0]
    groups = filters_ref.shape[0] // tiles
    st = st_ref[...]
    row = lax.broadcasted_iota(jnp.int32, (rows, 2 * rows), 0)
    key = lax.broadcasted_iota(jnp.int32, (rows, 2 * rows), 1) - rows
    keep[...] = jnp.where((key >= st) & (key <= row) & (key > row - rows), 1.0, 0.0).astype(jnp.bfloat16)
    tap = lax.broadcasted_iota(jnp.int32, (rows, rows), 0)
    place = lax.broadcasted_iota(jnp.int32, (rows, rows), 1)
    turn = jnp.where((tap + place == 0) | (tap + place == rows), 1.0, 0.0).astype(jnp.bfloat16)
    lines[...] = jnp.dot(filters_ref[...], turn, preferred_element_type=jnp.float32).reshape(lines.shape)

    @pl.loop(0, tiles)
    def _(c):
        some = lines[c]
        for g in range(groups):
            line = jnp.broadcast_to(some[g : g + 1], (rows, rows))
            ring = pltpu.roll(line, 0, 1, stride=1, stride_axis=0).astype(jnp.bfloat16)
            cols = slice(g * rows, (g + 1) * rows)
            far_ref[c, :, cols] = ring * keep[:, :rows]
            near_ref[c, :, cols] = ring * keep[:, rows:]


def share_kernel(facts_ref, qb_ref, q_ref, kn_ref, ko_ref, vn_ref, vo_ref, b0_ref, b1_ref, c_ref, bias, stat_ref):
    rows = q_ref.shape[0]
    before = facts_ref[NEXT_BEFORE]
    past = facts_ref[NEXT_AFTER]
    odd = facts_ref[ODD] == 1
    half = b0_ref.shape[0] - 1

    @pl.when(odd & (before <= rows))
    def _():
        c_ref[...] = q_ref[...]
        for part, b_ref in enumerate((b0_ref, b1_ref)):

            @pl.loop(0, half)
            def _(h):
                b_ref[h] = vo_ref[:, columns(part * half + h)]

    @pl.when(odd & (before > rows))
    def _():
        bias[:rows] = bias_of(rows, 2 * rows, rows, -rows, rows - before)
        bias[rows:] = bias_of(rows, 2 * rows, 0, -rows, rows - before)
        lane = lax.broadcasted_iota(jnp.int32, (rows, LANES), 1)
        ours = lax.broadcasted_iota(jnp.int32, (rows, LANES), 0) < past
        for part, b_ref in enumerate((b0_ref, b1_ref)):
            stat_ref[...] = jnp.zeros_like(stat_ref)

            def heads(first):
                at = lambda h: columns(part * half + first + h)
                stat = [stat_ref[...]]

                def use(h, o, l, top):
                    o = (o / l).astype(jnp.bfloat16)
                    b_ref[first + h] = o[:rows]
                    c_ref[:, at(h)] = o[rows:]
                    lse = jnp.where(ours, top[:rows] * FACTOR + jnp.log2(l[:rows]), NEG)
                    stat[0] = jnp.where(lane == first + h, lse, stat[0])

                attend(
                    UNROLL,
                    lambda h: jnp.concatenate([qb_ref[:, at(h)], q_ref[:, at(h)]], axis=0),
                    lambda h: jnp.concatenate([kn_ref[:, at(h)], ko_ref[:, at(h)]], axis=0),
                    lambda h: jnp.concatenate([vn_ref[:, at(h)], vo_ref[:, at(h)]], axis=0),
                    bias[...],
                    use,
                )
                stat_ref[...] = stat[0]

            each(half, heads)
            total = stat_ref[...]
            high = total.astype(jnp.bfloat16).astype(jnp.float32)
            middle = (total - high).astype(jnp.bfloat16).astype(jnp.float32)
            low = total - high - middle
            packed = high + pltpu.roll(middle, half, 1) + pltpu.roll(low, 2 * half, 1)
            b_ref[half] = packed.astype(jnp.bfloat16)


def scale_of(squares, width):
    total = jnp.sum(squares, axis=1, keepdims=True)
    return jnp.broadcast_to(lax.rsqrt(total * (1.0 / width) + 1e-06), squares.shape)


def spread(x, groups):
    size = LANES // groups
    lane_group = lax.broadcasted_iota(jnp.int32, x.shape, 1) // size
    return jnp.concatenate([jnp.where(lane_group == g, x, jnp.zeros_like(x)) for g in range(groups)], axis=0)


def convolve_own(att, squares, scale, taps_ref, gain_ref, bypass_ref, out_ref):
    count, rows, _ = att.shape
    scale[...] = scale_of(squares, count * LANES)

    def tiles(first):
        for c in range(UNROLL):
            cols = columns(first + c)
            x = (att[first + c].astype(jnp.float32) * scale[...] * gain_ref[:, cols]).astype(jnp.bfloat16)
            y = jnp.dot(taps_ref[first + c], spread(x, taps_ref.shape[2] // rows), preferred_element_type=jnp.float32)
            out_ref[:, cols] = y + bypass_ref[:, cols] * x.astype(jnp.float32)

    each(count, tiles)


def even_kernel(facts_ref, st_ref, q_ref, ko_ref, vo_ref, kp_ref, vp0_ref, vp1_ref, qn_ref, kn_ref, kf_ref, taps_ref, gain_ref, bypass_ref, three_ref, two_ref, out_ref, att, squares, scale, bias_own, bias_prev):
    rows = q_ref.shape[0]
    odd = facts_ref[ODD] == 1
    half = vp0_ref.shape[0] - 1
    low = jnp.where((facts_ref[ODD] == 0) & (facts_ref[BEFORE] > rows), 0, -(2**20))
    bias_own[...] = bias_of(rows, 3 * rows, 0, -2 * rows, jnp.maximum(st_ref[...], low))

    @pl.when(odd)
    def _():
        bias_prev[...] = bias_of(rows, 2 * rows, -rows, -2 * rows, st_ref[0:1, :])

        def heads(first):
            def scores(h):
                at = columns(first + h)
                key = jnp.concatenate([kf_ref[:, at], kn_ref[:, at], ko_ref[:, at]], axis=0)
                return scores_of(q_ref[:, at], key), scores_of(qn_ref[:, at], key[: 2 * rows])

            ahead = scores(0)
            for h in range(UNROLL):
                now = ahead
                if h + 1 < UNROLL:
                    ahead = scores(h + 1)
                three_ref[first + h] = raised(now[0], bias_own[...])[0]
                two_ref[first + h] = raised(now[1], bias_prev[...])[0]

        each(2 * half, heads)

    @pl.when(jnp.logical_not(odd))
    def _():
        lane = lax.broadcasted_iota(jnp.int32, (rows, LANES), 1)
        squares[...] = jnp.zeros_like(squares)
        for part, vp_ref in enumerate((vp0_ref, vp1_ref)):

            def heads(first):
                at = lambda h: columns(part * half + first + h)
                packed = vp_ref[half].astype(jnp.float32)
                stat = packed + pltpu.roll(packed, LANES - half, 1) + pltpu.roll(packed, LANES - 2 * half, 1)
                stat = jnp.where(facts_ref[BEFORE] > rows, stat, NEG)
                total = [squares[...]]

                def use(h, o, l, top):
                    lse = jnp.sum(jnp.where(lane == first + h, stat, 0.0), axis=1, keepdims=True)
                    top = top * FACTOR
                    high = jnp.maximum(top, lse)
                    here = jnp.exp2(top - high)
                    there = jnp.exp2(lse - high)
                    o = o * here + vp_ref[first + h].astype(jnp.float32) * there
                    a = (o / (l * here + there)).astype(jnp.bfloat16)
                    att[part * half + first + h] = a
                    a = a.astype(jnp.float32)
                    total[0] += a * a

                attend(
                    UNROLL,
                    lambda h: q_ref[:, at(h)],
                    lambda h: jnp.concatenate([kp_ref[:, at(h)], ko_ref[:, at(h)]], axis=0),
                    lambda h: jnp.concatenate([vp_ref[first + h], vo_ref[:, at(h)]], axis=0),
                    bias_own[:, rows:],
                    use,
                )
                squares[...] = total[0]

            each(half, heads)
        convolve_own(att, squares[...], scale, taps_ref, gain_ref, bypass_ref, out_ref)


def odd_kernel(facts_ref, three_ref, two_ref, vo_ref, vn_ref, vf0_ref, vf1_ref, taps_ref, gain_ref, bypass_ref, near_ref, sq_near_ref, out_ref, att, squares, scale):
    rows = vo_ref.shape[0]
    half = vf0_ref.shape[0] - 1

    @pl.when(facts_ref[ODD] == 1)
    def _():
        squares[...] = jnp.zeros_like(squares)
        sq_near_ref[...] = jnp.zeros_like(sq_near_ref)
        for part, vf_ref in enumerate((vf0_ref, vf1_ref)):

            def heads(first):
                total, total_near = squares[...], sq_near_ref[...]
                for h in range(UNROLL):
                    head = part * half + first + h
                    at = columns(head)
                    value = jnp.concatenate([vf_ref[first + h], vn_ref[:, at], vo_ref[:, at]], axis=0)
                    o, l = summed(three_ref[head], value)
                    a = (o / l).astype(jnp.bfloat16)
                    att[head] = a
                    a = a.astype(jnp.float32)
                    total += a * a
                    o, l = summed(two_ref[head], value[: 2 * rows])
                    a = (o / l).astype(jnp.bfloat16)
                    near_ref[head] = a
                    a = a.astype(jnp.float32)
                    total_near += a * a
                squares[...] = total
                sq_near_ref[...] = total_near

            each(half, heads)
        convolve_own(att, squares[...], scale, taps_ref, gain_ref, bypass_ref, out_ref)


def finish_kernel(facts_ref, st_ref, kp_ref, vp0_ref, vp1_ref, c_ref, near_ref, sq_ref, even_ref, odd_ref, taps_ref, gain_ref, out_ref, prev, squares, scale, bias):
    rows = st_ref.shape[0]
    half = vp0_ref.shape[0] - 1
    width = prev.shape[0] * LANES
    odd = facts_ref[ODD] == 1
    shared = facts_ref[BEFORE] > rows

    @pl.when(odd)
    def _():
        squares[...] = sq_ref[...]

        @pl.loop(0, 2 * half)
        def _(h):
            prev[h] = near_ref[h]

    @pl.when(jnp.logical_not(odd) & shared)
    def _():
        squares[...] = jnp.zeros_like(squares)

        def heads(first):
            total = squares[...]
            for h in range(UNROLL):
                a = c_ref[:, columns(first + h)]
                prev[first + h] = a
                a = a.astype(jnp.float32)
                total += a * a
            squares[...] = total

        each(2 * half, heads)

    @pl.when(jnp.logical_not(odd) & jnp.logical_not(shared))
    def _():
        squares[...] = jnp.zeros_like(squares)
        bias[...] = bias_of(rows, rows, -rows, -rows, st_ref[0:1, :])
        for part, vp_ref in enumerate((vp0_ref, vp1_ref)):

            def heads(first):
                at = lambda h: columns(part * half + first + h)
                total = [squares[...]]

                def use(h, o, l, top):
                    a = (o / l).astype(jnp.bfloat16)
                    prev[part * half + first + h] = a
                    a = a.astype(jnp.float32)
                    total[0] += a * a

                attend(UNROLL, lambda h: c_ref[:, at(h)], lambda h: kp_ref[:, at(h)], lambda h: vp_ref[first + h], bias[...], use)
                squares[...] = total[0]

            each(half, heads)

    scale[...] = scale_of(squares[...], width)

    def tiles(first):
        for c in range(UNROLL):
            cols = columns(first + c)
            x = (prev[first + c].astype(jnp.float32) * scale[...] * gain_ref[:, cols]).astype(jnp.bfloat16)
            y = jnp.dot(taps_ref[first + c], spread(x, taps_ref.shape[2] // rows), preferred_element_type=jnp.float32)
            out_ref[:, cols] = (y + jnp.where(odd, odd_ref[:, cols], even_ref[:, cols])).astype(jnp.bfloat16)

    each(2 * half, tiles)


def run(kernel, name, facts, out_shape, scratch, args):
    many = isinstance(out_shape, tuple)
    vmem = pl.BlockSpec(memory_space=pltpu.VMEM)
    return pl.pallas_call(
        kernel,
        out_shape=out_shape,
        in_specs=[pl.BlockSpec(memory_space=pltpu.SMEM)] + [vmem] * len(args),
        out_specs=(vmem,) * len(out_shape) if many else vmem,
        scratch_shapes=scratch,
        compiler_params=pltpu.CompilerParams(vmem_limit_bytes=VMEM_BYTES),
        cost_estimate=pl.CostEstimate(flops=2**20, bytes_accessed=2**16, transcendentals=0),
        name=name,
    )(facts, *args)


def shards(queries, key_rows, value_rows, lengths, norm_gain, filters, bypass):
    rows, width = queries.shape
    heads = width // HEAD_DIM
    half = heads // 2
    groups, taps = filters.shape
    n = lax.axis_size("ctx")
    st, facts = places(lengths, lax.axis_index("ctx") * rows, rows)

    back = [(i, i - 1) for i in range(2, n, 2)]
    within = [(i, i + 1) for i in range(0, n - 1, 2)]
    across = [(i, i + 1) for i in range(1, n - 1, 2)]

    bf16 = lambda *shape: jax.ShapeDtypeStruct(shape, jnp.bfloat16)
    f32 = lambda *shape: jax.ShapeDtypeStruct(shape, jnp.float32)

    query_back = permuted(queries, back)
    key_near = permuted(key_rows, within)
    value_near = permuted(value_rows, within)
    query_near = permuted(queries, within)

    key_across = permuted(after(key_rows, facts), across)

    slot_b0, slot_b1, slot_c = run(
        share_kernel,
        "share",
        after(facts, query_near),
        (bf16(half + 1, rows, HEAD_DIM), bf16(half + 1, rows, HEAD_DIM), bf16(rows, width)),
        [pltpu.VMEM((2 * rows, 2 * rows), jnp.float32), pltpu.VMEM((rows, LANES), jnp.float32)],
        (query_back, queries, key_near, key_rows, value_near, value_rows),
    )
    b_across = [permuted(x, across) for x in (slot_b0, slot_b1)]
    c_across = permuted(slot_c, across)
    key_far = permuted(after(key_across, slot_c), within)
    taps_far, taps_near = run(
        taps_kernel,
        "taps",
        after(facts, slot_c),
        (bf16(heads, rows, groups // heads * rows),) * 2,
        [pltpu.VMEM((rows, 2 * rows), jnp.bfloat16), pltpu.VMEM((heads, groups // heads, taps), jnp.float32)],
        (st, filters),
    )
    value_far = [permuted(after(x, taps_far), within) for x in b_across]

    gain = norm_gain.reshape(1, width)
    skip = bypass.reshape(1, width)
    own_scratch = [
        pltpu.VMEM((heads, rows, HEAD_DIM), jnp.bfloat16),
        pltpu.VMEM((rows, LANES), jnp.float32),
        pltpu.VMEM((rows, LANES), jnp.float32),
    ]
    three, two, even_part = run(
        even_kernel,
        "even",
        facts,
        (bf16(heads, rows, 3 * rows), bf16(heads, rows, 2 * rows), f32(rows, width)),
        own_scratch + [pltpu.VMEM((rows, 3 * rows), jnp.float32), pltpu.VMEM((rows, 2 * rows), jnp.float32)],
        (st, queries, key_rows, value_rows, key_across, *b_across, query_near, key_near, key_far, taps_near, gain, skip),
    )
    near, near_squares, odd_part = run(
        odd_kernel,
        "odd",
        facts,
        (bf16(heads, rows, HEAD_DIM), f32(rows, LANES), f32(rows, width)),
        own_scratch,
        (three, two, value_rows, value_near, *value_far, taps_near, gain, skip),
    )
    return run(
        finish_kernel,
        "finish",
        facts,
        bf16(rows, width),
        [
            pltpu.VMEM((heads, rows, LANES), jnp.bfloat16),
            pltpu.VMEM((rows, LANES), jnp.float32),
            pltpu.VMEM((rows, LANES), jnp.float32),
            pltpu.VMEM((rows, rows), jnp.float32),
        ],
        (st, key_across, *b_across, c_across, near, near_squares, even_part, odd_part, taps_far, gain),
    )


def solution(mesh):
    rows = P(("dp", "ctx"), None)
    in_specs = (rows, rows, rows, P("dp"), P(), P(), P())
    return jax.shard_map(shards, mesh=mesh, in_specs=in_specs, out_specs=rows, check_vma=False)
```

```python
import math

import jax
import jax.numpy as jnp
from jax import lax
from jax.experimental import pallas as pl
from jax.experimental.pallas import tpu as pltpu
from jax.sharding import PartitionSpec as P

HEAD_DIM = 128
LANES = 128
NEG = -1e30
FACTOR = 1.0 / math.sqrt(HEAD_DIM) * math.log2(math.e)
CONTRACT_LAST = (((1,), (1,)), ((), ()))
VMEM_BYTES = 16 * 2**20
UNROLL = 8

ODD, BEFORE, NEXT_BEFORE, NEXT_AFTER = range(4)


def permuted(x, pairs):
    return lax.ppermute(x, "ctx", pairs)


def after(x, *others):
    return lax.optimization_barrier((x, *others))[0]


def places(lengths, first_row, count):
    ends = jnp.cumsum(lengths)
    position = first_row + jnp.arange(count + 1, dtype=jnp.int32)
    passed = ends[None, :] <= position[:, None]
    starts = jnp.sum(jnp.where(passed, lengths[None, :], 0), axis=1) - first_row
    past = jnp.min(jnp.where(passed[count], jnp.int32(2**30), ends)) - first_row - count
    odd = (first_row // count) % 2
    facts = jnp.stack([odd, -starts[0], count - starts[count], past]).astype(jnp.int32)
    return starts[:count].astype(jnp.int32).reshape(count, 1), facts


def bias_of(rows, columns, row_first, key_first, start):
    row = lax.broadcasted_iota(jnp.int32, (rows, columns), 0) + row_first
    key = lax.broadcasted_iota(jnp.int32, (rows, columns), 1) + key_first
    return jnp.where((key >= start) & (key <= row), 0.0, NEG)


def scores_of(query, key):
    return lax.dot_general(query, key, CONTRACT_LAST, preferred_element_type=jnp.float32)


def raised(scores, bias):
    s = scores + bias
    top = jnp.max(s, axis=1, keepdims=True)
    return jnp.exp2((s - top) * FACTOR).astype(jnp.bfloat16), top


def summed(weights, value):
    ones = jnp.ones(value.shape, jnp.bfloat16)
    o = jnp.dot(weights, jnp.concatenate([value, ones], axis=1), preferred_element_type=jnp.float32)
    return o[:, :LANES], o[:, LANES:]


def columns(head):
    if isinstance(head, int):
        return slice(head * HEAD_DIM, (head + 1) * HEAD_DIM)
    return pl.ds(pl.multiple_of(head * HEAD_DIM, HEAD_DIM), HEAD_DIM)


def attend(heads, query, key, value, bias, use):
    ahead = scores_of(query(0), key(0))
    held = None
    for h in range(heads):
        now = ahead
        if h + 1 < heads:
            ahead = scores_of(query(h + 1), key(h + 1))
        weights, top = raised(now, bias)
        if held is not None:
            use(h - 1, *summed(held[0], value(h - 1)), held[1])
        held = weights, top
    use(heads - 1, *summed(held[0], value(heads - 1)), held[1])


def each(count, body):
    @pl.loop(0, count // UNROLL)
    def _(step):
        body(step * UNROLL)


def taps_kernel(facts_ref, st_ref, filters_ref, far_ref, near_ref, keep, lines):
    rows = st_ref.shape[0]
    tiles = far_ref.shape[0]
    groups = filters_ref.shape[0] // tiles
    st = st_ref[...]
    row = lax.broadcasted_iota(jnp.int32, (rows, 2 * rows), 0)
    key = lax.broadcasted_iota(jnp.int32, (rows, 2 * rows), 1) - rows
    keep[...] = jnp.where((key >= st) & (key <= row) & (key > row - rows), 1.0, 0.0).astype(jnp.bfloat16)
    tap = lax.broadcasted_iota(jnp.int32, (rows, rows), 0)
    place = lax.broadcasted_iota(jnp.int32, (rows, rows), 1)
    turn = jnp.where((tap + place == 0) | (tap + place == rows), 1.0, 0.0).astype(jnp.bfloat16)
    lines[...] = jnp.dot(filters_ref[...], turn, preferred_element_type=jnp.float32).reshape(lines.shape)

    @pl.loop(0, tiles)
    def _(c):
        some = lines[c]
        for g in range(groups):
            line = jnp.broadcast_to(some[g : g + 1], (rows, rows))
            ring = pltpu.roll(line, 0, 1, stride=1, stride_axis=0).astype(jnp.bfloat16)
            cols = slice(g * rows, (g + 1) * rows)
            far_ref[c, :, cols] = ring * keep[:, :rows]
            near_ref[c, :, cols] = ring * keep[:, rows:]


def share_kernel(facts_ref, qb_ref, q_ref, kn_ref, ko_ref, vn_ref, vo_ref, b0_ref, b1_ref, c_ref, bias, stat_ref):
    rows = q_ref.shape[0]
    before = facts_ref[NEXT_BEFORE]
    past = facts_ref[NEXT_AFTER]
    odd = facts_ref[ODD] == 1
    half = b0_ref.shape[0] - 1

    @pl.when(odd & (before <= rows))
    def _():
        c_ref[...] = q_ref[...]
        for part, b_ref in enumerate((b0_ref, b1_ref)):

            @pl.loop(0, half)
            def _(h):
                b_ref[h] = vo_ref[:, columns(part * half + h)]

    @pl.when(odd & (before > rows))
    def _():
        bias[:rows] = bias_of(rows, 2 * rows, rows, -rows, rows - before)
        bias[rows:] = bias_of(rows, 2 * rows, 0, -rows, rows - before)
        lane = lax.broadcasted_iota(jnp.int32, (rows, LANES), 1)
        ours = lax.broadcasted_iota(jnp.int32, (rows, LANES), 0) < past
        for part, b_ref in enumerate((b0_ref, b1_ref)):
            stat_ref[...] = jnp.zeros_like(stat_ref)

            def heads(first):
                at = lambda h: columns(part * half + first + h)
                stat = [stat_ref[...]]

                def use(h, o, l, top):
                    o = (o / l).astype(jnp.bfloat16)
                    b_ref[first + h] = o[:rows]
                    c_ref[:, at(h)] = o[rows:]
                    lse = jnp.where(ours, top[:rows] * FACTOR + jnp.log2(l[:rows]), NEG)
                    stat[0] = jnp.where(lane == first + h, lse, stat[0])

                attend(
                    UNROLL,
                    lambda h: jnp.concatenate([qb_ref[:, at(h)], q_ref[:, at(h)]], axis=0),
                    lambda h: jnp.concatenate([kn_ref[:, at(h)], ko_ref[:, at(h)]], axis=0),
                    lambda h: jnp.concatenate([vn_ref[:, at(h)], vo_ref[:, at(h)]], axis=0),
                    bias[...],
                    use,
                )
                stat_ref[...] = stat[0]

            each(half, heads)
            total = stat_ref[...]
            high = total.astype(jnp.bfloat16).astype(jnp.float32)
            middle = (total - high).astype(jnp.bfloat16).astype(jnp.float32)
            low = total - high - middle
            packed = high + pltpu.roll(middle, half, 1) + pltpu.roll(low, 2 * half, 1)
            b_ref[half] = packed.astype(jnp.bfloat16)


def scale_of(squares, width):
    total = jnp.sum(squares, axis=1, keepdims=True)
    return jnp.broadcast_to(lax.rsqrt(total * (1.0 / width) + 1e-06), squares.shape)


def spread(x, groups):
    size = LANES // groups
    lane_group = lax.broadcasted_iota(jnp.int32, x.shape, 1) // size
    return jnp.concatenate([jnp.where(lane_group == g, x, jnp.zeros_like(x)) for g in range(groups)], axis=0)


def convolve_own(att, squares, scale, taps_ref, gain_ref, bypass_ref, out_ref):
    count, rows, _ = att.shape
    scale[...] = scale_of(squares, count * LANES)

    def tiles(first):
        for c in range(UNROLL):
            cols = columns(first + c)
            x = (att[first + c].astype(jnp.float32) * scale[...] * gain_ref[:, cols]).astype(jnp.bfloat16)
            y = jnp.dot(taps_ref[first + c], spread(x, taps_ref.shape[2] // rows), preferred_element_type=jnp.float32)
            out_ref[:, cols] = y + bypass_ref[:, cols] * x.astype(jnp.float32)

    each(count, tiles)


def even_kernel(facts_ref, st_ref, q_ref, ko_ref, vo_ref, kp_ref, vp0_ref, vp1_ref, qn_ref, kn_ref, kf_ref, taps_ref, gain_ref, bypass_ref, three_ref, two_ref, out_ref, att, squares, scale, bias_own, bias_prev):
    rows = q_ref.shape[0]
    odd = facts_ref[ODD] == 1
    half = vp0_ref.shape[0] - 1
    low = jnp.where((facts_ref[ODD] == 0) & (facts_ref[BEFORE] > rows), 0, -(2**20))
    bias_own[...] = bias_of(rows, 3 * rows, 0, -2 * rows, jnp.maximum(st_ref[...], low))

    @pl.when(odd)
    def _():
        bias_prev[...] = bias_of(rows, 2 * rows, -rows, -2 * rows, st_ref[0:1, :])

        def heads(first):
            def scores(h):
                at = columns(first + h)
                key = jnp.concatenate([kf_ref[:, at], kn_ref[:, at], ko_ref[:, at]], axis=0)
                return scores_of(q_ref[:, at], key), scores_of(qn_ref[:, at], key[: 2 * rows])

            ahead = scores(0)
            for h in range(UNROLL):
                now = ahead
                if h + 1 < UNROLL:
                    ahead = scores(h + 1)
                three_ref[first + h] = raised(now[0], bias_own[...])[0]
                two_ref[first + h] = raised(now[1], bias_prev[...])[0]

        each(2 * half, heads)

    @pl.when(jnp.logical_not(odd))
    def _():
        lane = lax.broadcasted_iota(jnp.int32, (rows, LANES), 1)
        squares[...] = jnp.zeros_like(squares)
        for part, vp_ref in enumerate((vp0_ref, vp1_ref)):

            def heads(first):
                at = lambda h: columns(part * half + first + h)
                packed = vp_ref[half].astype(jnp.float32)
                stat = packed + pltpu.roll(packed, LANES - half, 1) + pltpu.roll(packed, LANES - 2 * half, 1)
                stat = jnp.where(facts_ref[BEFORE] > rows, stat, NEG)
                total = [squares[...]]

                def use(h, o, l, top):
                    lse = jnp.sum(jnp.where(lane == first + h, stat, 0.0), axis=1, keepdims=True)
                    top = top * FACTOR
                    high = jnp.maximum(top, lse)
                    here = jnp.exp2(top - high)
                    there = jnp.exp2(lse - high)
                    o = o * here + vp_ref[first + h].astype(jnp.float32) * there
                    a = (o / (l * here + there)).astype(jnp.bfloat16)
                    att[part * half + first + h] = a
                    a = a.astype(jnp.float32)
                    total[0] += a * a

                attend(
                    UNROLL,
                    lambda h: q_ref[:, at(h)],
                    lambda h: jnp.concatenate([kp_ref[:, at(h)], ko_ref[:, at(h)]], axis=0),
                    lambda h: jnp.concatenate([vp_ref[first + h], vo_ref[:, at(h)]], axis=0),
                    bias_own[:, rows:],
                    use,
                )
                squares[...] = total[0]

            each(half, heads)
        convolve_own(att, squares[...], scale, taps_ref, gain_ref, bypass_ref, out_ref)


def odd_kernel(facts_ref, three_ref, two_ref, vo_ref, vn_ref, vf0_ref, vf1_ref, taps_ref, gain_ref, bypass_ref, near_ref, sq_near_ref, out_ref, att, squares, scale):
    rows = vo_ref.shape[0]
    half = vf0_ref.shape[0] - 1

    @pl.when(facts_ref[ODD] == 1)
    def _():
        squares[...] = jnp.zeros_like(squares)
        sq_near_ref[...] = jnp.zeros_like(sq_near_ref)
        for part, vf_ref in enumerate((vf0_ref, vf1_ref)):

            def heads(first):
                total, total_near = squares[...], sq_near_ref[...]
                for h in range(UNROLL):
                    head = part * half + first + h
                    at = columns(head)
                    value = jnp.concatenate([vf_ref[first + h], vn_ref[:, at], vo_ref[:, at]], axis=0)
                    o, l = summed(three_ref[head], value)
                    a = (o / l).astype(jnp.bfloat16)
                    att[head] = a
                    a = a.astype(jnp.float32)
                    total += a * a
                    o, l = summed(two_ref[head], value[: 2 * rows])
                    a = (o / l).astype(jnp.bfloat16)
                    near_ref[head] = a
                    a = a.astype(jnp.float32)
                    total_near += a * a
                squares[...] = total
                sq_near_ref[...] = total_near

            each(half, heads)
        convolve_own(att, squares[...], scale, taps_ref, gain_ref, bypass_ref, out_ref)


def finish_kernel(facts_ref, st_ref, kp_ref, vp0_ref, vp1_ref, c_ref, near_ref, sq_ref, even_ref, odd_ref, taps_ref, gain_ref, out_ref, prev, squares, scale, bias):
    rows = st_ref.shape[0]
    half = vp0_ref.shape[0] - 1
    width = prev.shape[0] * LANES
    odd = facts_ref[ODD] == 1
    shared = facts_ref[BEFORE] > rows

    @pl.when(odd)
    def _():
        squares[...] = sq_ref[...]

        @pl.loop(0, 2 * half)
        def _(h):
            prev[h] = near_ref[h]

    @pl.when(jnp.logical_not(odd) & shared)
    def _():
        squares[...] = jnp.zeros_like(squares)

        def heads(first):
            total = squares[...]
            for h in range(UNROLL):
                a = c_ref[:, columns(first + h)]
                prev[first + h] = a
                a = a.astype(jnp.float32)
                total += a * a
            squares[...] = total

        each(2 * half, heads)

    @pl.when(jnp.logical_not(odd) & jnp.logical_not(shared))
    def _():
        squares[...] = jnp.zeros_like(squares)
        bias[...] = bias_of(rows, rows, -rows, -rows, st_ref[0:1, :])
        for part, vp_ref in enumerate((vp0_ref, vp1_ref)):

            def heads(first):
                at = lambda h: columns(part * half + first + h)
                total = [squares[...]]

                def use(h, o, l, top):
                    a = (o / l).astype(jnp.bfloat16)
                    prev[part * half + first + h] = a
                    a = a.astype(jnp.float32)
                    total[0] += a * a

                attend(UNROLL, lambda h: c_ref[:, at(h)], lambda h: kp_ref[:, at(h)], lambda h: vp_ref[first + h], bias[...], use)
                squares[...] = total[0]

            each(half, heads)

    scale[...] = scale_of(squares[...], width)

    def tiles(first):
        for c in range(UNROLL):
            cols = columns(first + c)
            x = (prev[first + c].astype(jnp.float32) * scale[...] * gain_ref[:, cols]).astype(jnp.bfloat16)
            y = jnp.dot(taps_ref[first + c], spread(x, taps_ref.shape[2] // rows), preferred_element_type=jnp.float32)
            out_ref[:, cols] = (y + jnp.where(odd, odd_ref[:, cols], even_ref[:, cols])).astype(jnp.bfloat16)

    each(2 * half, tiles)


def run(kernel, name, facts, out_shape, scratch, args):
    many = isinstance(out_shape, tuple)
    vmem = pl.BlockSpec(memory_space=pltpu.VMEM)
    return pl.pallas_call(
        kernel,
        out_shape=out_shape,
        in_specs=[pl.BlockSpec(memory_space=pltpu.SMEM)] + [vmem] * len(args),
        out_specs=(vmem,) * len(out_shape) if many else vmem,
        scratch_shapes=scratch,
        compiler_params=pltpu.CompilerParams(vmem_limit_bytes=VMEM_BYTES),
        cost_estimate=pl.CostEstimate(flops=2**20, bytes_accessed=2**16, transcendentals=0),
        name=name,
    )(facts, *args)


def shards(queries, key_rows, value_rows, lengths, norm_gain, filters, bypass):
    rows, width = queries.shape
    heads = width // HEAD_DIM
    half = heads // 2
    groups, taps = filters.shape
    n = lax.axis_size("ctx")
    st, facts = places(lengths, lax.axis_index("ctx") * rows, rows)

    back = [(i, i - 1) for i in range(2, n, 2)]
    within = [(i, i + 1) for i in range(0, n - 1, 2)]
    across = [(i, i + 1) for i in range(1, n - 1, 2)]

    bf16 = lambda *shape: jax.ShapeDtypeStruct(shape, jnp.bfloat16)
    f32 = lambda *shape: jax.ShapeDtypeStruct(shape, jnp.float32)

    query_back = permuted(queries, back)
    key_near = permuted(key_rows, within)
    value_near = permuted(value_rows, within)
    query_near = permuted(queries, within)

    taps_far, taps_near = run(
        taps_kernel,
        "taps",
        facts,
        (bf16(heads, rows, groups // heads * rows),) * 2,
        [pltpu.VMEM((rows, 2 * rows), jnp.bfloat16), pltpu.VMEM((heads, groups // heads, taps), jnp.float32)],
        (st, filters),
    )
    key_across = permuted(after(key_rows, facts), across)

    slot_b0, slot_b1, slot_c = run(
        share_kernel,
        "share",
        after(facts, taps_far, query_near),
        (bf16(half + 1, rows, HEAD_DIM), bf16(half + 1, rows, HEAD_DIM), bf16(rows, width)),
        [pltpu.VMEM((2 * rows, 2 * rows), jnp.float32), pltpu.VMEM((rows, LANES), jnp.float32)],
        (query_back, queries, key_near, key_rows, value_near, value_rows),
    )
    b_across = [permuted(x, across) for x in (slot_b0, slot_b1)]
    c_across = permuted(slot_c, across)
    key_far = permuted(after(key_across, slot_c), within)
    value_far = [permuted(x, within) for x in b_across]

    gain = norm_gain.reshape(1, width)
    skip = bypass.reshape(1, width)
    own_scratch = [
        pltpu.VMEM((heads, rows, HEAD_DIM), jnp.bfloat16),
        pltpu.VMEM((rows, LANES), jnp.float32),
        pltpu.VMEM((rows, LANES), jnp.float32),
    ]
    three, two, even_part = run(
        even_kernel,
        "even",
        facts,
        (bf16(heads, rows, 3 * rows), bf16(heads, rows, 2 * rows), f32(rows, width)),
        own_scratch + [pltpu.VMEM((rows, 3 * rows), jnp.float32), pltpu.VMEM((rows, 2 * rows), jnp.float32)],
        (st, queries, key_rows, value_rows, key_across, *b_across, query_near, key_near, key_far, taps_near, gain, skip),
    )
    near, near_squares, odd_part = run(
        odd_kernel,
        "odd",
        facts,
        (bf16(heads, rows, HEAD_DIM), f32(rows, LANES), f32(rows, width)),
        own_scratch,
        (three, two, value_rows, value_near, *value_far, taps_near, gain, skip),
    )
    return run(
        finish_kernel,
        "finish",
        facts,
        bf16(rows, width),
        [
            pltpu.VMEM((heads, rows, LANES), jnp.bfloat16),
            pltpu.VMEM((rows, LANES), jnp.float32),
            pltpu.VMEM((rows, LANES), jnp.float32),
            pltpu.VMEM((rows, rows), jnp.float32),
        ],
        (st, key_across, *b_across, c_across, near, near_squares, even_part, odd_part, taps_far, gain),
    )


def solution(mesh):
    rows = P(("dp", "ctx"), None)
    in_specs = (rows, rows, rows, P("dp"), P(), P(), P())
    return jax.shard_map(shards, mesh=mesh, in_specs=in_specs, out_specs=rows, check_vma=False)
```

```python
import math

import jax
import jax.numpy as jnp
from jax import lax
from jax.experimental import pallas as pl
from jax.experimental.pallas import tpu as pltpu
from jax.sharding import PartitionSpec as P

HEAD_DIM = 128
LANES = 128
NEG = -1e30
FACTOR = 1.0 / math.sqrt(HEAD_DIM) * math.log2(math.e)
CONTRACT_LAST = (((1,), (1,)), ((), ()))
VMEM_BYTES = 16 * 2**20
UNROLL = 8

ODD, BEFORE, NEXT_BEFORE, NEXT_AFTER = range(4)


def permuted(x, pairs):
    return lax.ppermute(x, "ctx", pairs)


def after(x, *others):
    return lax.optimization_barrier((x, *others))[0]


def places(lengths, first_row, count):
    ends = jnp.cumsum(lengths)
    position = first_row + jnp.arange(count + 1, dtype=jnp.int32)
    passed = ends[None, :] <= position[:, None]
    starts = jnp.sum(jnp.where(passed, lengths[None, :], 0), axis=1) - first_row
    past = jnp.min(jnp.where(passed[count], jnp.int32(2**30), ends)) - first_row - count
    odd = (first_row // count) % 2
    facts = jnp.stack([odd, -starts[0], count - starts[count], past]).astype(jnp.int32)
    return starts[:count].astype(jnp.int32).reshape(count, 1), facts, ends


def bias_of(rows, columns, row_first, key_first, start):
    row = lax.broadcasted_iota(jnp.int32, (rows, columns), 0) + row_first
    key = lax.broadcasted_iota(jnp.int32, (rows, columns), 1) + key_first
    return jnp.where((key >= start) & (key <= row), 0.0, NEG)


def scores_of(query, key):
    return lax.dot_general(query, key, CONTRACT_LAST, preferred_element_type=jnp.float32)


def raised(scores, bias):
    s = scores + bias
    top = jnp.max(s, axis=1, keepdims=True)
    return jnp.exp2((s - top) * FACTOR).astype(jnp.bfloat16), top


def summed(weights, value):
    ones = jnp.ones(value.shape, jnp.bfloat16)
    o = jnp.dot(weights, jnp.concatenate([value, ones], axis=1), preferred_element_type=jnp.float32)
    return o[:, :LANES], o[:, LANES:]


def columns(head):
    if isinstance(head, int):
        return slice(head * HEAD_DIM, (head + 1) * HEAD_DIM)
    return pl.ds(pl.multiple_of(head * HEAD_DIM, HEAD_DIM), HEAD_DIM)


def attend(heads, query, key, value, bias, use):
    ahead = scores_of(query(0), key(0))
    held = None
    for h in range(heads):
        now = ahead
        if h + 1 < heads:
            ahead = scores_of(query(h + 1), key(h + 1))
        weights, top = raised(now, bias)
        if held is not None:
            use(h - 1, *summed(held[0], value(h - 1)), held[1])
        held = weights, top
    use(heads - 1, *summed(held[0], value(heads - 1)), held[1])


def each(count, body):
    @pl.loop(0, count // UNROLL)
    def _(step):
        body(step * UNROLL)


def ring_kernel(place_ref, filters_ref, ring_ref, lines):
    tiles, rows, _ = ring_ref.shape
    groups = filters_ref.shape[0] // tiles
    tap = lax.broadcasted_iota(jnp.int32, (rows, rows), 0)
    place = lax.broadcasted_iota(jnp.int32, (rows, rows), 1)
    turn = jnp.where((tap + place == 0) | (tap + place == rows), 1.0, 0.0).astype(jnp.bfloat16)
    lines[...] = jnp.dot(filters_ref[...], turn, preferred_element_type=jnp.float32).reshape(lines.shape)

    @pl.loop(0, tiles)
    def _(c):
        some = lines[c]
        for g in range(groups):
            line = jnp.broadcast_to(some[g : g + 1], (rows, rows))
            ring = pltpu.roll(line, 0, 1, stride=1, stride_axis=0)
            ring_ref[c, :, g * rows : (g + 1) * rows] = ring.astype(jnp.bfloat16)


def kept(st, width, far):
    rows = st.shape[0]
    row = lax.broadcasted_iota(jnp.int32, (rows, rows), 0)
    key = lax.broadcasted_iota(jnp.int32, (rows, rows), 1)
    keep = ((key - rows >= st) & (key > row)) if far else ((key >= st) & (key <= row))
    return jnp.concatenate([jnp.where(keep, 1.0, 0.0).astype(jnp.bfloat16)] * (width // rows), axis=1)


def share_kernel(facts_ref, qb_ref, q_ref, kn_ref, ko_ref, vn_ref, vo_ref, b0_ref, b1_ref, c_ref, bias, stat_ref):
    rows = q_ref.shape[0]
    before = facts_ref[NEXT_BEFORE]
    past = facts_ref[NEXT_AFTER]
    odd = facts_ref[ODD] == 1
    half = b0_ref.shape[0] - 1

    @pl.when(odd & (before <= rows))
    def _():
        c_ref[...] = q_ref[...]
        for part, b_ref in enumerate((b0_ref, b1_ref)):

            @pl.loop(0, half)
            def _(h):
                b_ref[h] = vo_ref[:, columns(part * half + h)]

    @pl.when(odd & (before > rows))
    def _():
        bias[:rows] = bias_of(rows, 2 * rows, rows, -rows, rows - before)
        bias[rows:] = bias_of(rows, 2 * rows, 0, -rows, rows - before)
        lane = lax.broadcasted_iota(jnp.int32, (rows, LANES), 1)
        ours = lax.broadcasted_iota(jnp.int32, (rows, LANES), 0) < past
        for part, b_ref in enumerate((b0_ref, b1_ref)):
            stat_ref[...] = jnp.zeros_like(stat_ref)

            def heads(first):
                at = lambda h: columns(part * half + first + h)
                stat = [stat_ref[...]]

                def use(h, o, l, top):
                    o = (o / l).astype(jnp.bfloat16)
                    b_ref[first + h] = o[:rows]
                    c_ref[:, at(h)] = o[rows:]
                    lse = jnp.where(ours, top[:rows] * FACTOR + jnp.log2(l[:rows]), NEG)
                    stat[0] = jnp.where(lane == first + h, lse, stat[0])

                attend(
                    UNROLL,
                    lambda h: jnp.concatenate([qb_ref[:, at(h)], q_ref[:, at(h)]], axis=0),
                    lambda h: jnp.concatenate([kn_ref[:, at(h)], ko_ref[:, at(h)]], axis=0),
                    lambda h: jnp.concatenate([vn_ref[:, at(h)], vo_ref[:, at(h)]], axis=0),
                    bias[...],
                    use,
                )
                stat_ref[...] = stat[0]

            each(half, heads)
            total = stat_ref[...]
            high = total.astype(jnp.bfloat16).astype(jnp.float32)
            middle = (total - high).astype(jnp.bfloat16).astype(jnp.float32)
            low = total - high - middle
            packed = high + pltpu.roll(middle, half, 1) + pltpu.roll(low, 2 * half, 1)
            b_ref[half] = packed.astype(jnp.bfloat16)


def scale_of(squares, width):
    total = jnp.sum(squares, axis=1, keepdims=True)
    return jnp.broadcast_to(lax.rsqrt(total * (1.0 / width) + 1e-06), squares.shape)


def spread(x, groups):
    size = LANES // groups
    lane_group = lax.broadcasted_iota(jnp.int32, x.shape, 1) // size
    return jnp.concatenate([jnp.where(lane_group == g, x, jnp.zeros_like(x)) for g in range(groups)], axis=0)


def convolve_own(att, st, squares, scale, ring_ref, gain_ref, bypass_ref, out_ref):
    count, rows, _ = att.shape
    keep = kept(st, ring_ref.shape[2], False)
    scale[...] = scale_of(squares, count * LANES)

    def tiles(first):
        for c in range(UNROLL):
            cols = columns(first + c)
            x = (att[first + c].astype(jnp.float32) * scale[...] * gain_ref[:, cols]).astype(jnp.bfloat16)
            y = jnp.dot(ring_ref[first + c] * keep, spread(x, ring_ref.shape[2] // rows), preferred_element_type=jnp.float32)
            out_ref[:, cols] = y + bypass_ref[:, cols] * x.astype(jnp.float32)

    each(count, tiles)


def even_kernel(facts_ref, st_ref, q_ref, ko_ref, vo_ref, kp_ref, vp0_ref, vp1_ref, qn_ref, kn_ref, kf_ref, ring_ref, gain_ref, bypass_ref, three_ref, two_ref, out_ref, att, squares, scale, bias_own, bias_prev):
    rows = q_ref.shape[0]
    odd = facts_ref[ODD] == 1
    half = vp0_ref.shape[0] - 1
    low = jnp.where((facts_ref[ODD] == 0) & (facts_ref[BEFORE] > rows), 0, -(2**20))
    bias_own[...] = bias_of(rows, 3 * rows, 0, -2 * rows, jnp.maximum(st_ref[...], low))

    @pl.when(odd)
    def _():
        bias_prev[...] = bias_of(rows, 2 * rows, -rows, -2 * rows, st_ref[0:1, :])

        def heads(first):
            def scores(h):
                at = columns(first + h)
                key = jnp.concatenate([kf_ref[:, at], kn_ref[:, at], ko_ref[:, at]], axis=0)
                return scores_of(q_ref[:, at], key), scores_of(qn_ref[:, at], key[: 2 * rows])

            ahead = scores(0)
            for h in range(UNROLL):
                now = ahead
                if h + 1 < UNROLL:
                    ahead = scores(h + 1)
                three_ref[first + h] = raised(now[0], bias_own[...])[0]
                two_ref[first + h] = raised(now[1], bias_prev[...])[0]

        each(2 * half, heads)

    @pl.when(jnp.logical_not(odd))
    def _():
        lane = lax.broadcasted_iota(jnp.int32, (rows, LANES), 1)
        squares[...] = jnp.zeros_like(squares)
        for part, vp_ref in enumerate((vp0_ref, vp1_ref)):

            def heads(first):
                at = lambda h: columns(part * half + first + h)
                packed = vp_ref[half].astype(jnp.float32)
                stat = packed + pltpu.roll(packed, LANES - half, 1) + pltpu.roll(packed, LANES - 2 * half, 1)
                stat = jnp.where(facts_ref[BEFORE] > rows, stat, NEG)
                total = [squares[...]]

                def use(h, o, l, top):
                    lse = jnp.sum(jnp.where(lane == first + h, stat, 0.0), axis=1, keepdims=True)
                    top = top * FACTOR
                    high = jnp.maximum(top, lse)
                    here = jnp.exp2(top - high)
                    there = jnp.exp2(lse - high)
                    o = o * here + vp_ref[first + h].astype(jnp.float32) * there
                    a = (o / (l * here + there)).astype(jnp.bfloat16)
                    att[part * half + first + h] = a
                    a = a.astype(jnp.float32)
                    total[0] += a * a

                attend(
                    UNROLL,
                    lambda h: q_ref[:, at(h)],
                    lambda h: jnp.concatenate([kp_ref[:, at(h)], ko_ref[:, at(h)]], axis=0),
                    lambda h: jnp.concatenate([vp_ref[first + h], vo_ref[:, at(h)]], axis=0),
                    bias_own[:, rows:],
                    use,
                )
                squares[...] = total[0]

            each(half, heads)
        convolve_own(att, st_ref[...], squares[...], scale, ring_ref, gain_ref, bypass_ref, out_ref)


def odd_kernel(facts_ref, st_ref, three_ref, two_ref, vo_ref, vn_ref, vf0_ref, vf1_ref, ring_ref, gain_ref, bypass_ref, near_ref, sq_near_ref, out_ref, att, squares, scale):
    rows = vo_ref.shape[0]
    half = vf0_ref.shape[0] - 1

    @pl.when(facts_ref[ODD] == 1)
    def _():
        squares[...] = jnp.zeros_like(squares)
        sq_near_ref[...] = jnp.zeros_like(sq_near_ref)
        for part, vf_ref in enumerate((vf0_ref, vf1_ref)):

            def heads(first):
                total, total_near = squares[...], sq_near_ref[...]
                for h in range(UNROLL):
                    head = part * half + first + h
                    at = columns(head)
                    value = jnp.concatenate([vf_ref[first + h], vn_ref[:, at], vo_ref[:, at]], axis=0)
                    o, l = summed(three_ref[head], value)
                    a = (o / l).astype(jnp.bfloat16)
                    att[head] = a
                    a = a.astype(jnp.float32)
                    total += a * a
                    o, l = summed(two_ref[head], value[: 2 * rows])
                    a = (o / l).astype(jnp.bfloat16)
                    near_ref[head] = a
                    a = a.astype(jnp.float32)
                    total_near += a * a
                squares[...] = total
                sq_near_ref[...] = total_near

            each(half, heads)
        convolve_own(att, st_ref[...], squares[...], scale, ring_ref, gain_ref, bypass_ref, out_ref)


def finish_kernel(facts_ref, st_ref, kp_ref, vp0_ref, vp1_ref, c_ref, near_ref, sq_ref, even_ref, odd_ref, ring_ref, gain_ref, out_ref, prev, squares, scale, bias):
    rows = st_ref.shape[0]
    half = vp0_ref.shape[0] - 1
    width = prev.shape[0] * LANES
    odd = facts_ref[ODD] == 1
    shared = facts_ref[BEFORE] > rows

    @pl.when(odd)
    def _():
        squares[...] = sq_ref[...]

        @pl.loop(0, 2 * half)
        def _(h):
            prev[h] = near_ref[h]

    @pl.when(jnp.logical_not(odd) & shared)
    def _():
        squares[...] = jnp.zeros_like(squares)

        def heads(first):
            total = squares[...]
            for h in range(UNROLL):
                a = c_ref[:, columns(first + h)]
                prev[first + h] = a
                a = a.astype(jnp.float32)
                total += a * a
            squares[...] = total

        each(2 * half, heads)

    @pl.when(jnp.logical_not(odd) & jnp.logical_not(shared))
    def _():
        squares[...] = jnp.zeros_like(squares)
        bias[...] = bias_of(rows, rows, -rows, -rows, st_ref[0:1, :])
        for part, vp_ref in enumerate((vp0_ref, vp1_ref)):

            def heads(first):
                at = lambda h: columns(part * half + first + h)
                total = [squares[...]]

                def use(h, o, l, top):
                    a = (o / l).astype(jnp.bfloat16)
                    prev[part * half + first + h] = a
                    a = a.astype(jnp.float32)
                    total[0] += a * a

                attend(UNROLL, lambda h: c_ref[:, at(h)], lambda h: kp_ref[:, at(h)], lambda h: vp_ref[first + h], bias[...], use)
                squares[...] = total[0]

            each(half, heads)

    scale[...] = scale_of(squares[...], width)
    keep = kept(st_ref[...], ring_ref.shape[2], True)

    def tiles(first):
        for c in range(UNROLL):
            cols = columns(first + c)
            x = (prev[first + c].astype(jnp.float32) * scale[...] * gain_ref[:, cols]).astype(jnp.bfloat16)
            y = jnp.dot(ring_ref[first + c] * keep, spread(x, ring_ref.shape[2] // rows), preferred_element_type=jnp.float32)
            out_ref[:, cols] = (y + jnp.where(odd, odd_ref[:, cols], even_ref[:, cols])).astype(jnp.bfloat16)

    each(2 * half, tiles)


def run(kernel, name, facts, out_shape, scratch, args):
    many = isinstance(out_shape, tuple)
    vmem = pl.BlockSpec(memory_space=pltpu.VMEM)
    return pl.pallas_call(
        kernel,
        out_shape=out_shape,
        in_specs=[pl.BlockSpec(memory_space=pltpu.SMEM)] + [vmem] * len(args),
        out_specs=(vmem,) * len(out_shape) if many else vmem,
        scratch_shapes=scratch,
        compiler_params=pltpu.CompilerParams(vmem_limit_bytes=VMEM_BYTES),
        cost_estimate=pl.CostEstimate(flops=2**20, bytes_accessed=2**16, transcendentals=0),
        name=name,
    )(facts, *args)


def shards(queries, key_rows, value_rows, lengths, norm_gain, filters, bypass):
    rows, width = queries.shape
    heads = width // HEAD_DIM
    half = heads // 2
    groups, taps = filters.shape
    n = lax.axis_size("ctx")
    st, facts, ends = places(lengths, lax.axis_index("ctx") * rows, rows)

    back = [(i, i - 1) for i in range(2, n, 2)]
    within = [(i, i + 1) for i in range(0, n - 1, 2)]
    across = [(i, i + 1) for i in range(1, n - 1, 2)]

    bf16 = lambda *shape: jax.ShapeDtypeStruct(shape, jnp.bfloat16)
    f32 = lambda *shape: jax.ShapeDtypeStruct(shape, jnp.float32)

    query_back = permuted(queries, back)
    key_near = permuted(key_rows, within)
    value_near = permuted(value_rows, within)
    query_near = permuted(queries, within)

    ring = run(
        ring_kernel,
        "ring",
        facts,
        bf16(heads, rows, groups // heads * rows),
        [pltpu.VMEM((heads, groups // heads, taps), jnp.float32)],
        (filters,),
    )
    key_across = permuted(after(key_rows, ends), across)

    slot_b0, slot_b1, slot_c = run(
        share_kernel,
        "share",
        after(facts, ring, query_near),
        (bf16(half + 1, rows, HEAD_DIM), bf16(half + 1, rows, HEAD_DIM), bf16(rows, width)),
        [pltpu.VMEM((2 * rows, 2 * rows), jnp.float32), pltpu.VMEM((rows, LANES), jnp.float32)],
        (query_back, queries, key_near, key_rows, value_near, value_rows),
    )
    b_across = [permuted(x, across) for x in (slot_b0, slot_b1)]
    c_across = permuted(slot_c, across)
    key_far = permuted(after(key_across, slot_c), within)
    value_far = [permuted(x, within) for x in b_across]

    gain = norm_gain.reshape(1, width)
    skip = bypass.reshape(1, width)
    own_scratch = [
        pltpu.VMEM((heads, rows, HEAD_DIM), jnp.bfloat16),
        pltpu.VMEM((rows, LANES), jnp.float32),
        pltpu.VMEM((rows, LANES), jnp.float32),
    ]
    three, two, even_part = run(
        even_kernel,
        "even",
        facts,
        (bf16(heads, rows, 3 * rows), bf16(heads, rows, 2 * rows), f32(rows, width)),
        own_scratch + [pltpu.VMEM((rows, 3 * rows), jnp.float32), pltpu.VMEM((rows, 2 * rows), jnp.float32)],
        (st, queries, key_rows, value_rows, key_across, *b_across, query_near, key_near, key_far, ring, gain, skip),
    )
    near, near_squares, odd_part = run(
        odd_kernel,
        "odd",
        facts,
        (bf16(heads, rows, HEAD_DIM), f32(rows, LANES), f32(rows, width)),
        own_scratch,
        (st, three, two, value_rows, value_near, *value_far, ring, gain, skip),
    )
    return run(
        finish_kernel,
        "finish",
        facts,
        bf16(rows, width),
        [
            pltpu.VMEM((heads, rows, LANES), jnp.bfloat16),
            pltpu.VMEM((rows, LANES), jnp.float32),
            pltpu.VMEM((rows, LANES), jnp.float32),
            pltpu.VMEM((rows, rows), jnp.float32),
        ],
        (st, key_across, *b_across, c_across, near, near_squares, even_part, odd_part, ring, gain),
    )


def solution(mesh):
    rows = P(("dp", "ctx"), None)
    in_specs = (rows, rows, rows, P("dp"), P(), P(), P())
    return jax.shard_map(shards, mesh=mesh, in_specs=in_specs, out_specs=rows, check_vma=False)
```

```python
import math

import jax
import jax.numpy as jnp
from jax import lax
from jax.experimental import pallas as pl
from jax.experimental.pallas import tpu as pltpu
from jax.sharding import PartitionSpec as P

HEAD_DIM = 128
LANES = 128
NEG = -1e30
FACTOR = 1.0 / math.sqrt(HEAD_DIM) * math.log2(math.e)
CONTRACT_LAST = (((1,), (1,)), ((), ()))
VMEM_BYTES = 16 * 2**20
UNROLL = 8

ODD, BEFORE, NEXT_BEFORE, NEXT_AFTER = range(4)


def permuted(x, pairs):
    return lax.ppermute(x, "ctx", pairs)


def after(x, *others):
    return lax.optimization_barrier((x, *others))[0]


def places(lengths, first_row, count):
    ends = jnp.cumsum(lengths)
    position = first_row + jnp.arange(count + 1, dtype=jnp.int32)
    passed = ends[None, :] <= position[:, None]
    starts = jnp.sum(jnp.where(passed, lengths[None, :], 0), axis=1) - first_row
    past = jnp.min(jnp.where(passed[count], jnp.int32(2**30), ends)) - first_row - count
    odd = (first_row // count) % 2
    facts = jnp.stack([odd, -starts[0], count - starts[count], past]).astype(jnp.int32)
    return starts[:count].astype(jnp.int32).reshape(count, 1), facts


def bias_of(rows, columns, row_first, key_first, start):
    row = lax.broadcasted_iota(jnp.int32, (rows, columns), 0) + row_first
    key = lax.broadcasted_iota(jnp.int32, (rows, columns), 1) + key_first
    return jnp.where((key >= start) & (key <= row), 0.0, NEG)


def scores_of(query, key):
    return lax.dot_general(query, key, CONTRACT_LAST, preferred_element_type=jnp.float32)


def raised(scores, bias):
    s = scores + bias
    top = jnp.max(s, axis=1, keepdims=True)
    return jnp.exp2((s - top) * FACTOR).astype(jnp.bfloat16), top


def summed(weights, value):
    ones = jnp.ones(value.shape, jnp.bfloat16)
    o = jnp.dot(weights, jnp.concatenate([value, ones], axis=1), preferred_element_type=jnp.float32)
    return o[:, :LANES], o[:, LANES:]


def columns(head):
    if isinstance(head, int):
        return slice(head * HEAD_DIM, (head + 1) * HEAD_DIM)
    return pl.ds(pl.multiple_of(head * HEAD_DIM, HEAD_DIM), HEAD_DIM)


def attend(heads, query, key, value, bias, use):
    ahead = scores_of(query(0), key(0))
    held = None
    for h in range(heads):
        now = ahead
        if h + 1 < heads:
            ahead = scores_of(query(h + 1), key(h + 1))
        weights, top = raised(now, bias)
        if held is not None:
            use(h - 1, *summed(held[0], value(h - 1)), held[1])
        held = weights, top
    use(heads - 1, *summed(held[0], value(heads - 1)), held[1])


def each(count, body):
    @pl.loop(0, count // UNROLL)
    def _(step):
        body(step * UNROLL)


def taps_kernel(facts_ref, st_ref, filters_ref, far_ref, near_ref, keep, lines):
    rows = st_ref.shape[0]
    tiles = far_ref.shape[0]
    groups = filters_ref.shape[0] // tiles
    st = st_ref[...]
    row = lax.broadcasted_iota(jnp.int32, (rows, 2 * rows), 0)
    key = lax.broadcasted_iota(jnp.int32, (rows, 2 * rows), 1) - rows
    keep[...] = jnp.where((key >= st) & (key <= row) & (key > row - rows), 1.0, 0.0).astype(jnp.bfloat16)
    tap = lax.broadcasted_iota(jnp.int32, (rows, rows), 0)
    place = lax.broadcasted_iota(jnp.int32, (rows, rows), 1)
    turn = jnp.where((tap + place == 0) | (tap + place == rows), 1.0, 0.0).astype(jnp.bfloat16)
    lines[...] = jnp.dot(filters_ref[...], turn, preferred_element_type=jnp.float32).reshape(lines.shape)

    @pl.loop(0, tiles)
    def _(c):
        some = lines[c]
        for g in range(groups):
            line = jnp.broadcast_to(some[g : g + 1], (rows, rows))
            ring = pltpu.roll(line, 0, 1, stride=1, stride_axis=0).astype(jnp.bfloat16)
            cols = slice(g * rows, (g + 1) * rows)
            far_ref[c, :, cols] = ring * keep[:, :rows]
            near_ref[c, :, cols] = ring * keep[:, rows:]


def share_kernel(facts_ref, qb_ref, q_ref, kn_ref, ko_ref, vn_ref, vo_ref, b0_ref, b1_ref, c_ref, bias, stat_ref):
    rows = q_ref.shape[0]
    before = facts_ref[NEXT_BEFORE]
    past = facts_ref[NEXT_AFTER]
    odd = facts_ref[ODD] == 1
    half = b0_ref.shape[0] - 1

    @pl.when(odd & (before <= rows))
    def _():
        c_ref[...] = q_ref[...]
        for part, b_ref in enumerate((b0_ref, b1_ref)):

            @pl.loop(0, half)
            def _(h):
                b_ref[h] = vo_ref[:, columns(part * half + h)]

    @pl.when(odd & (before > rows))
    def _():
        bias[:rows] = bias_of(rows, 2 * rows, rows, -rows, rows - before)
        bias[rows:] = bias_of(rows, 2 * rows, 0, -rows, rows - before)
        lane = lax.broadcasted_iota(jnp.int32, (rows, LANES), 1)
        ours = lax.broadcasted_iota(jnp.int32, (rows, LANES), 0) < past
        for part, b_ref in enumerate((b0_ref, b1_ref)):
            stat_ref[...] = jnp.zeros_like(stat_ref)

            def heads(first):
                at = lambda h: columns(part * half + first + h)
                stat = [stat_ref[...]]

                def use(h, o, l, top):
                    o = (o / l).astype(jnp.bfloat16)
                    b_ref[first + h] = o[:rows]
                    c_ref[:, at(h)] = o[rows:]
                    lse = jnp.where(ours, top[:rows] * FACTOR + jnp.log2(l[:rows]), NEG)
                    stat[0] = jnp.where(lane == first + h, lse, stat[0])

                attend(
                    UNROLL,
                    lambda h: jnp.concatenate([qb_ref[:, at(h)], q_ref[:, at(h)]], axis=0),
                    lambda h: jnp.concatenate([kn_ref[:, at(h)], ko_ref[:, at(h)]], axis=0),
                    lambda h: jnp.concatenate([vn_ref[:, at(h)], vo_ref[:, at(h)]], axis=0),
                    bias[...],
                    use,
                )
                stat_ref[...] = stat[0]

            each(half, heads)
            total = stat_ref[...]
            high = total.astype(jnp.bfloat16).astype(jnp.float32)
            middle = (total - high).astype(jnp.bfloat16).astype(jnp.float32)
            low = total - high - middle
            packed = high + pltpu.roll(middle, half, 1) + pltpu.roll(low, 2 * half, 1)
            b_ref[half] = packed.astype(jnp.bfloat16)


def scale_of(squares, width):
    total = jnp.sum(squares, axis=1, keepdims=True)
    return jnp.broadcast_to(lax.rsqrt(total * (1.0 / width) + 1e-06), squares.shape)


def spread(x, groups):
    size = LANES // groups
    lane_group = lax.broadcasted_iota(jnp.int32, x.shape, 1) // size
    return jnp.concatenate([jnp.where(lane_group == g, x, jnp.zeros_like(x)) for g in range(groups)], axis=0)


def convolve_own(att, squares, scale, taps_ref, gain_ref, bypass_ref, out_ref):
    count, rows, _ = att.shape
    scale[...] = scale_of(squares, count * LANES)

    def tiles(first):
        for c in range(UNROLL):
            cols = columns(first + c)
            x = (att[first + c].astype(jnp.float32) * scale[...] * gain_ref[:, cols]).astype(jnp.bfloat16)
            y = jnp.dot(taps_ref[first + c], spread(x, taps_ref.shape[2] // rows), preferred_element_type=jnp.float32)
            out_ref[:, cols] = y + bypass_ref[:, cols] * x.astype(jnp.float32)

    each(count, tiles)


def even_kernel(facts_ref, st_ref, q_ref, ko_ref, vo_ref, kp_ref, vp0_ref, vp1_ref, qn_ref, kn_ref, kf_ref, taps_ref, gain_ref, bypass_ref, three_ref, two_ref, out_ref, att, squares, scale, bias_own, bias_prev):
    rows = q_ref.shape[0]
    odd = facts_ref[ODD] == 1
    half = vp0_ref.shape[0] - 1
    low = jnp.where((facts_ref[ODD] == 0) & (facts_ref[BEFORE] > rows), 0, -(2**20))
    bias_own[...] = bias_of(rows, 3 * rows, 0, -2 * rows, jnp.maximum(st_ref[...], low))

    @pl.when(odd)
    def _():
        bias_prev[...] = bias_of(rows, 2 * rows, -rows, -2 * rows, st_ref[0:1, :])

        def heads(first):
            def scores(h):
                at = columns(first + h)
                key = jnp.concatenate([kf_ref[:, at], kn_ref[:, at], ko_ref[:, at]], axis=0)
                return scores_of(q_ref[:, at], key), scores_of(qn_ref[:, at], key[: 2 * rows])

            ahead = scores(0)
            for h in range(UNROLL):
                now = ahead
                if h + 1 < UNROLL:
                    ahead = scores(h + 1)
                three_ref[first + h] = raised(now[0], bias_own[...])[0]
                two_ref[first + h] = raised(now[1], bias_prev[...])[0]

        each(2 * half, heads)

    @pl.when(jnp.logical_not(odd))
    def _():
        lane = lax.broadcasted_iota(jnp.int32, (rows, LANES), 1)
        squares[...] = jnp.zeros_like(squares)
        for part, vp_ref in enumerate((vp0_ref, vp1_ref)):

            def heads(first):
                at = lambda h: columns(part * half + first + h)
                packed = vp_ref[half].astype(jnp.float32)
                stat = packed + pltpu.roll(packed, LANES - half, 1) + pltpu.roll(packed, LANES - 2 * half, 1)
                stat = jnp.where(facts_ref[BEFORE] > rows, stat, NEG)
                total = [squares[...]]

                def use(h, o, l, top):
                    lse = jnp.sum(jnp.where(lane == first + h, stat, 0.0), axis=1, keepdims=True)
                    top = top * FACTOR
                    high = jnp.maximum(top, lse)
                    here = jnp.exp2(top - high)
                    there = jnp.exp2(lse - high)
                    o = o * here + vp_ref[first + h].astype(jnp.float32) * there
                    a = (o / (l * here + there)).astype(jnp.bfloat16)
                    att[part * half + first + h] = a
                    a = a.astype(jnp.float32)
                    total[0] += a * a

                attend(
                    UNROLL,
                    lambda h: q_ref[:, at(h)],
                    lambda h: jnp.concatenate([kp_ref[:, at(h)], ko_ref[:, at(h)]], axis=0),
                    lambda h: jnp.concatenate([vp_ref[first + h], vo_ref[:, at(h)]], axis=0),
                    bias_own[:, rows:],
                    use,
                )
                squares[...] = total[0]

            each(half, heads)
        convolve_own(att, squares[...], scale, taps_ref, gain_ref, bypass_ref, out_ref)


def odd_kernel(facts_ref, three_ref, two_ref, vo_ref, vn_ref, vf0_ref, vf1_ref, taps_ref, gain_ref, bypass_ref, near_ref, sq_near_ref, out_ref, att, squares, scale):
    rows = vo_ref.shape[0]
    half = vf0_ref.shape[0] - 1

    @pl.when(facts_ref[ODD] == 1)
    def _():
        squares[...] = jnp.zeros_like(squares)
        sq_near_ref[...] = jnp.zeros_like(sq_near_ref)
        for part, vf_ref in enumerate((vf0_ref, vf1_ref)):

            def heads(first):
                total, total_near = squares[...], sq_near_ref[...]
                for h in range(UNROLL):
                    head = part * half + first + h
                    at = columns(head)
                    value = jnp.concatenate([vf_ref[first + h], vn_ref[:, at], vo_ref[:, at]], axis=0)
                    o, l = summed(three_ref[head], value)
                    a = (o / l).astype(jnp.bfloat16)
                    att[head] = a
                    a = a.astype(jnp.float32)
                    total += a * a
                    o, l = summed(two_ref[head], value[: 2 * rows])
                    a = (o / l).astype(jnp.bfloat16)
                    near_ref[head] = a
                    a = a.astype(jnp.float32)
                    total_near += a * a
                squares[...] = total
                sq_near_ref[...] = total_near

            each(half, heads)
        convolve_own(att, squares[...], scale, taps_ref, gain_ref, bypass_ref, out_ref)


def finish_kernel(facts_ref, st_ref, kp_ref, vp0_ref, vp1_ref, c_ref, near_ref, sq_ref, even_ref, odd_ref, taps_ref, gain_ref, out_hbm, prev, squares, scale, bias, out_ref, sems):
    rows = st_ref.shape[0]
    half = vp0_ref.shape[0] - 1
    width = prev.shape[0] * LANES
    odd = facts_ref[ODD] == 1
    shared = facts_ref[BEFORE] > rows

    @pl.when(odd)
    def _():
        squares[...] = sq_ref[...]

        @pl.loop(0, 2 * half)
        def _(h):
            prev[h] = near_ref[h]

    @pl.when(jnp.logical_not(odd) & shared)
    def _():
        squares[...] = jnp.zeros_like(squares)

        def heads(first):
            total = squares[...]
            for h in range(UNROLL):
                a = c_ref[:, columns(first + h)]
                prev[first + h] = a
                a = a.astype(jnp.float32)
                total += a * a
            squares[...] = total

        each(2 * half, heads)

    @pl.when(jnp.logical_not(odd) & jnp.logical_not(shared))
    def _():
        squares[...] = jnp.zeros_like(squares)
        bias[...] = bias_of(rows, rows, -rows, -rows, st_ref[0:1, :])
        for part, vp_ref in enumerate((vp0_ref, vp1_ref)):

            def heads(first):
                at = lambda h: columns(part * half + first + h)
                total = [squares[...]]

                def use(h, o, l, top):
                    a = (o / l).astype(jnp.bfloat16)
                    prev[part * half + first + h] = a
                    a = a.astype(jnp.float32)
                    total[0] += a * a

                attend(UNROLL, lambda h: c_ref[:, at(h)], lambda h: kp_ref[:, at(h)], lambda h: vp_ref[first + h], bias[...], use)
                squares[...] = total[0]

            each(half, heads)

    scale[...] = scale_of(squares[...], width)

    def chunk(first):
        cols = pl.ds(pl.multiple_of(first * LANES, UNROLL * LANES), UNROLL * LANES)
        return pltpu.make_async_copy(out_ref.at[:, cols], out_hbm.at[:, cols], sems.at[first // UNROLL])

    def tiles(first):
        for c in range(UNROLL):
            cols = columns(first + c)
            x = (prev[first + c].astype(jnp.float32) * scale[...] * gain_ref[:, cols]).astype(jnp.bfloat16)
            y = jnp.dot(taps_ref[first + c], spread(x, taps_ref.shape[2] // rows), preferred_element_type=jnp.float32)
            out_ref[:, cols] = (y + jnp.where(odd, odd_ref[:, cols], even_ref[:, cols])).astype(jnp.bfloat16)

        chunk(first).start()

    each(2 * half, tiles)
    each(2 * half, lambda first: chunk(first).wait())


def run(kernel, name, facts, out_shape, scratch, args, out_space=pltpu.VMEM):
    many = isinstance(out_shape, tuple)
    vmem = pl.BlockSpec(memory_space=pltpu.VMEM)
    return pl.pallas_call(
        kernel,
        out_shape=out_shape,
        in_specs=[pl.BlockSpec(memory_space=pltpu.SMEM)] + [vmem] * len(args),
        out_specs=(vmem,) * len(out_shape) if many else pl.BlockSpec(memory_space=out_space),
        scratch_shapes=scratch,
        compiler_params=pltpu.CompilerParams(vmem_limit_bytes=VMEM_BYTES),
        cost_estimate=pl.CostEstimate(flops=2**20, bytes_accessed=2**16, transcendentals=0),
        name=name,
    )(facts, *args)


def shards(queries, key_rows, value_rows, lengths, norm_gain, filters, bypass):
    rows, width = queries.shape
    heads = width // HEAD_DIM
    half = heads // 2
    groups, taps = filters.shape
    n = lax.axis_size("ctx")
    st, facts = places(lengths, lax.axis_index("ctx") * rows, rows)

    back = [(i, i - 1) for i in range(2, n, 2)]
    within = [(i, i + 1) for i in range(0, n - 1, 2)]
    across = [(i, i + 1) for i in range(1, n - 1, 2)]

    bf16 = lambda *shape: jax.ShapeDtypeStruct(shape, jnp.bfloat16)
    f32 = lambda *shape: jax.ShapeDtypeStruct(shape, jnp.float32)

    query_back = permuted(queries, back)
    key_near = permuted(key_rows, within)
    value_near = permuted(value_rows, within)
    query_near = permuted(queries, within)

    taps_far, taps_near = run(
        taps_kernel,
        "taps",
        facts,
        (bf16(heads, rows, groups // heads * rows),) * 2,
        [pltpu.VMEM((rows, 2 * rows), jnp.bfloat16), pltpu.VMEM((heads, groups // heads, taps), jnp.float32)],
        (st, filters),
    )
    key_across = permuted(after(key_rows, facts), across)

    slot_b0, slot_b1, slot_c = run(
        share_kernel,
        "share",
        after(facts, taps_far, query_near),
        (bf16(half + 1, rows, HEAD_DIM), bf16(half + 1, rows, HEAD_DIM), bf16(rows, width)),
        [pltpu.VMEM((2 * rows, 2 * rows), jnp.float32), pltpu.VMEM((rows, LANES), jnp.float32)],
        (query_back, queries, key_near, key_rows, value_near, value_rows),
    )
    b_across = [permuted(x, across) for x in (slot_b0, slot_b1)]
    c_across = permuted(slot_c, across)
    key_far = permuted(after(key_across, slot_c), within)
    value_far = [permuted(x, within) for x in b_across]

    gain = norm_gain.reshape(1, width)
    skip = bypass.reshape(1, width)
    own_scratch = [
        pltpu.VMEM((heads, rows, HEAD_DIM), jnp.bfloat16),
        pltpu.VMEM((rows, LANES), jnp.float32),
        pltpu.VMEM((rows, LANES), jnp.float32),
    ]
    three, two, even_part = run(
        even_kernel,
        "even",
        facts,
        (bf16(heads, rows, 3 * rows), bf16(heads, rows, 2 * rows), f32(rows, width)),
        own_scratch + [pltpu.VMEM((rows, 3 * rows), jnp.float32), pltpu.VMEM((rows, 2 * rows), jnp.float32)],
        (st, queries, key_rows, value_rows, key_across, *b_across, query_near, key_near, key_far, taps_near, gain, skip),
    )
    near, near_squares, odd_part = run(
        odd_kernel,
        "odd",
        facts,
        (bf16(heads, rows, HEAD_DIM), f32(rows, LANES), f32(rows, width)),
        own_scratch,
        (three, two, value_rows, value_near, *value_far, taps_near, gain, skip),
    )
    return run(
        finish_kernel,
        "finish",
        facts,
        bf16(rows, width),
        [
            pltpu.VMEM((heads, rows, LANES), jnp.bfloat16),
            pltpu.VMEM((rows, LANES), jnp.float32),
            pltpu.VMEM((rows, LANES), jnp.float32),
            pltpu.VMEM((rows, rows), jnp.float32),
            pltpu.VMEM((rows, width), jnp.bfloat16),
            pltpu.SemaphoreType.DMA((heads // UNROLL,)),
        ],
        (st, key_across, *b_across, c_across, near, near_squares, even_part, odd_part, taps_far, gain),
        pl.ANY,
    )


def solution(mesh):
    rows = P(("dp", "ctx"), None)
    in_specs = (rows, rows, rows, P("dp"), P(), P(), P())
    return jax.shard_map(shards, mesh=mesh, in_specs=in_specs, out_specs=rows, check_vma=False)
```

```python
import math

import jax
import jax.numpy as jnp
from jax import lax
from jax.experimental import pallas as pl
from jax.experimental.pallas import tpu as pltpu
from jax.sharding import PartitionSpec as P

HEAD_DIM = 128
LANES = 128
NEG = -1e30
FACTOR = 1.0 / math.sqrt(HEAD_DIM) * math.log2(math.e)
CONTRACT_LAST = (((1,), (1,)), ((), ()))
VMEM_BYTES = 16 * 2**20
UNROLL = 8

ODD, BEFORE, NEXT_BEFORE, NEXT_AFTER = range(4)


def permuted(x, pairs):
    return lax.ppermute(x, "ctx", pairs)


def after(x, *others):
    return lax.optimization_barrier((x, *others))[0]


def places(lengths, first_row, count):
    ends = jnp.cumsum(lengths)
    position = first_row + jnp.arange(count + 1, dtype=jnp.int32)
    passed = ends[None, :] <= position[:, None]
    starts = jnp.sum(jnp.where(passed, lengths[None, :], 0), axis=1) - first_row
    past = jnp.min(jnp.where(passed[count], jnp.int32(2**30), ends)) - first_row - count
    odd = (first_row // count) % 2
    facts = jnp.stack([odd, -starts[0], count - starts[count], past]).astype(jnp.int32)
    return starts[:count].astype(jnp.int32).reshape(count, 1), facts


def bias_of(rows, columns, row_first, key_first, start):
    row = lax.broadcasted_iota(jnp.int32, (rows, columns), 0) + row_first
    key = lax.broadcasted_iota(jnp.int32, (rows, columns), 1) + key_first
    return jnp.where((key >= start) & (key <= row), 0.0, NEG)


def scores_of(query, key):
    return lax.dot_general(query, key, CONTRACT_LAST, preferred_element_type=jnp.float32)


def raised(scores, bias):
    s = scores + bias
    top = jnp.max(s, axis=1, keepdims=True)
    return jnp.exp2((s - top) * FACTOR).astype(jnp.bfloat16), top


def summed(weights, value):
    ones = jnp.ones(value.shape, jnp.bfloat16)
    o = jnp.dot(weights, jnp.concatenate([value, ones], axis=1), preferred_element_type=jnp.float32)
    return o[:, :LANES], o[:, LANES:]


def columns(head):
    if isinstance(head, int):
        return slice(head * HEAD_DIM, (head + 1) * HEAD_DIM)
    return pl.ds(pl.multiple_of(head * HEAD_DIM, HEAD_DIM), HEAD_DIM)


def attend(heads, query, key, value, bias, use):
    ahead = scores_of(query(0), key(0))
    held = None
    for h in range(heads):
        now = ahead
        if h + 1 < heads:
            ahead = scores_of(query(h + 1), key(h + 1))
        weights, top = raised(now, bias)
        if held is not None:
            use(h - 1, *summed(held[0], value(h - 1)), held[1])
        held = weights, top
    use(heads - 1, *summed(held[0], value(heads - 1)), held[1])


def each(count, body):
    @pl.loop(0, count // UNROLL)
    def _(step):
        body(step * UNROLL)


def taps_kernel(facts_ref, st_ref, filters_ref, far_ref, near_ref, keep, lines):
    rows = st_ref.shape[0]
    tiles = far_ref.shape[0]
    groups = filters_ref.shape[0] // tiles
    st = st_ref[...]
    row = lax.broadcasted_iota(jnp.int32, (rows, 2 * rows), 0)
    key = lax.broadcasted_iota(jnp.int32, (rows, 2 * rows), 1) - rows
    keep[...] = jnp.where((key >= st) & (key <= row) & (key > row - rows), 1.0, 0.0).astype(jnp.bfloat16)
    tap = lax.broadcasted_iota(jnp.int32, (rows, rows), 0)
    place = lax.broadcasted_iota(jnp.int32, (rows, rows), 1)
    turn = jnp.where((tap + place == 0) | (tap + place == rows), 1.0, 0.0).astype(jnp.bfloat16)
    lines[...] = jnp.dot(filters_ref[...], turn, preferred_element_type=jnp.float32).reshape(lines.shape)

    @pl.loop(0, tiles)
    def _(c):
        some = lines[c]
        for g in range(groups):
            line = jnp.broadcast_to(some[g : g + 1], (rows, rows))
            ring = pltpu.roll(line, 0, 1, stride=1, stride_axis=0).astype(jnp.bfloat16)
            cols = slice(g * rows, (g + 1) * rows)
            far_ref[c, :, cols] = ring * keep[:, :rows]
            near_ref[c, :, cols] = ring * keep[:, rows:]


def slot_b_kernel(facts_ref, qb_ref, kn_ref, ko_ref, vn_ref, vo_ref, b0_ref, b1_ref, bias, stat_ref):
    rows = qb_ref.shape[0]
    before = facts_ref[NEXT_BEFORE]
    past = facts_ref[NEXT_AFTER]
    odd = facts_ref[ODD] == 1
    half = b0_ref.shape[0] - 1

    @pl.when(odd & (before <= rows))
    def _():
        for part, b_ref in enumerate((b0_ref, b1_ref)):

            @pl.loop(0, half)
            def _(h):
                b_ref[h] = vo_ref[:, columns(part * half + h)]

    @pl.when(odd & (before > rows))
    def _():
        bias[...] = bias_of(rows, 2 * rows, rows, -rows, rows - before)
        lane = lax.broadcasted_iota(jnp.int32, (rows, LANES), 1)
        ours = lax.broadcasted_iota(jnp.int32, (rows, LANES), 0) < past
        for part, b_ref in enumerate((b0_ref, b1_ref)):
            stat_ref[...] = jnp.zeros_like(stat_ref)

            def heads(first):
                at = lambda h: columns(part * half + first + h)
                stat = [stat_ref[...]]

                def use(h, o, l, top):
                    b_ref[first + h] = (o / l).astype(jnp.bfloat16)
                    lse = jnp.where(ours, top * FACTOR + jnp.log2(l), NEG)
                    stat[0] = jnp.where(lane == first + h, lse, stat[0])

                attend(
                    UNROLL,
                    lambda h: qb_ref[:, at(h)],
                    lambda h: jnp.concatenate([kn_ref[:, at(h)], ko_ref[:, at(h)]], axis=0),
                    lambda h: jnp.concatenate([vn_ref[:, at(h)], vo_ref[:, at(h)]], axis=0),
                    bias[...],
                    use,
                )
                stat_ref[...] = stat[0]

            each(half, heads)
            total = stat_ref[...]
            high = total.astype(jnp.bfloat16).astype(jnp.float32)
            middle = (total - high).astype(jnp.bfloat16).astype(jnp.float32)
            low = total - high - middle
            packed = high + pltpu.roll(middle, half, 1) + pltpu.roll(low, 2 * half, 1)
            b_ref[half] = packed.astype(jnp.bfloat16)


def slot_c_kernel(facts_ref, q_ref, kn_ref, ko_ref, vn_ref, vo_ref, c_ref, bias):
    rows, width = q_ref.shape
    before = facts_ref[NEXT_BEFORE]
    odd = facts_ref[ODD] == 1

    @pl.when(odd & (before <= rows))
    def _():
        c_ref[...] = q_ref[...]

    @pl.when(odd & (before > rows))
    def _():
        bias[...] = bias_of(rows, 2 * rows, 0, -rows, rows - before)

        def heads(first):
            at = lambda h: columns(first + h)

            def use(h, o, l, top):
                c_ref[:, at(h)] = (o / l).astype(jnp.bfloat16)

            attend(
                UNROLL,
                lambda h: q_ref[:, at(h)],
                lambda h: jnp.concatenate([kn_ref[:, at(h)], ko_ref[:, at(h)]], axis=0),
                lambda h: jnp.concatenate([vn_ref[:, at(h)], vo_ref[:, at(h)]], axis=0),
                bias[...],
                use,
            )

        each(width // HEAD_DIM, heads)


def scale_of(squares, width):
    total = jnp.sum(squares, axis=1, keepdims=True)
    return jnp.broadcast_to(lax.rsqrt(total * (1.0 / width) + 1e-06), squares.shape)


def spread(x, groups):
    size = LANES // groups
    lane_group = lax.broadcasted_iota(jnp.int32, x.shape, 1) // size
    return jnp.concatenate([jnp.where(lane_group == g, x, jnp.zeros_like(x)) for g in range(groups)], axis=0)


def convolve_own(att, squares, scale, taps_ref, gain_ref, bypass_ref, out_ref):
    count, rows, _ = att.shape
    scale[...] = scale_of(squares, count * LANES)

    def tiles(first):
        for c in range(UNROLL):
            cols = columns(first + c)
            x = (att[first + c].astype(jnp.float32) * scale[...] * gain_ref[:, cols]).astype(jnp.bfloat16)
            y = jnp.dot(taps_ref[first + c], spread(x, taps_ref.shape[2] // rows), preferred_element_type=jnp.float32)
            out_ref[:, cols] = y + bypass_ref[:, cols] * x.astype(jnp.float32)

    each(count, tiles)


def even_kernel(facts_ref, st_ref, q_ref, ko_ref, vo_ref, kp_ref, vp0_ref, vp1_ref, qn_ref, kn_ref, kf_ref, taps_ref, gain_ref, bypass_ref, three_ref, two_ref, out_ref, att, squares, scale, bias_own, bias_prev):
    rows = q_ref.shape[0]
    odd = facts_ref[ODD] == 1
    half = vp0_ref.shape[0] - 1
    low = jnp.where((facts_ref[ODD] == 0) & (facts_ref[BEFORE] > rows), 0, -(2**20))
    bias_own[...] = bias_of(rows, 3 * rows, 0, -2 * rows, jnp.maximum(st_ref[...], low))

    @pl.when(odd)
    def _():
        bias_prev[...] = bias_of(rows, 2 * rows, -rows, -2 * rows, st_ref[0:1, :])

        def heads(first):
            def scores(h):
                at = columns(first + h)
                key = jnp.concatenate([kf_ref[:, at], kn_ref[:, at], ko_ref[:, at]], axis=0)
                return scores_of(q_ref[:, at], key), scores_of(qn_ref[:, at], key[: 2 * rows])

            ahead = scores(0)
            for h in range(UNROLL):
                now = ahead
                if h + 1 < UNROLL:
                    ahead = scores(h + 1)
                three_ref[first + h] = raised(now[0], bias_own[...])[0]
                two_ref[first + h] = raised(now[1], bias_prev[...])[0]

        each(2 * half, heads)

    @pl.when(jnp.logical_not(odd))
    def _():
        lane = lax.broadcasted_iota(jnp.int32, (rows, LANES), 1)
        squares[...] = jnp.zeros_like(squares)
        for part, vp_ref in enumerate((vp0_ref, vp1_ref)):

            def heads(first):
                at = lambda h: columns(part * half + first + h)
                packed = vp_ref[half].astype(jnp.float32)
                stat = packed + pltpu.roll(packed, LANES - half, 1) + pltpu.roll(packed, LANES - 2 * half, 1)
                stat = jnp.where(facts_ref[BEFORE] > rows, stat, NEG)
                total = [squares[...]]

                def use(h, o, l, top):
                    lse = jnp.sum(jnp.where(lane == first + h, stat, 0.0), axis=1, keepdims=True)
                    top = top * FACTOR
                    high = jnp.maximum(top, lse)
                    here = jnp.exp2(top - high)
                    there = jnp.exp2(lse - high)
                    o = o * here + vp_ref[first + h].astype(jnp.float32) * there
                    a = (o / (l * here + there)).astype(jnp.bfloat16)
                    att[part * half + first + h] = a
                    a = a.astype(jnp.float32)
                    total[0] += a * a

                attend(
                    UNROLL,
                    lambda h: q_ref[:, at(h)],
                    lambda h: jnp.concatenate([kp_ref[:, at(h)], ko_ref[:, at(h)]], axis=0),
                    lambda h: jnp.concatenate([vp_ref[first + h], vo_ref[:, at(h)]], axis=0),
                    bias_own[:, rows:],
                    use,
                )
                squares[...] = total[0]

            each(half, heads)
        convolve_own(att, squares[...], scale, taps_ref, gain_ref, bypass_ref, out_ref)


def odd_kernel(facts_ref, three_ref, two_ref, vo_ref, vn_ref, vf0_ref, vf1_ref, taps_ref, gain_ref, bypass_ref, near_ref, sq_near_ref, out_ref, att, squares, scale):
    rows = vo_ref.shape[0]
    half = vf0_ref.shape[0] - 1

    @pl.when(facts_ref[ODD] == 1)
    def _():
        squares[...] = jnp.zeros_like(squares)
        sq_near_ref[...] = jnp.zeros_like(sq_near_ref)
        for part, vf_ref in enumerate((vf0_ref, vf1_ref)):

            def heads(first):
                total, total_near = squares[...], sq_near_ref[...]
                for h in range(UNROLL):
                    head = part * half + first + h
                    at = columns(head)
                    value = jnp.concatenate([vf_ref[first + h], vn_ref[:, at], vo_ref[:, at]], axis=0)
                    o, l = summed(three_ref[head], value)
                    a = (o / l).astype(jnp.bfloat16)
                    att[head] = a
                    a = a.astype(jnp.float32)
                    total += a * a
                    o, l = summed(two_ref[head], value[: 2 * rows])
                    a = (o / l).astype(jnp.bfloat16)
                    near_ref[head] = a
                    a = a.astype(jnp.float32)
                    total_near += a * a
                squares[...] = total
                sq_near_ref[...] = total_near

            each(half, heads)
        convolve_own(att, squares[...], scale, taps_ref, gain_ref, bypass_ref, out_ref)


def finish_kernel(facts_ref, st_ref, kp_ref, vp0_ref, vp1_ref, c_ref, near_ref, sq_ref, even_ref, odd_ref, taps_ref, gain_ref, out_hbm, prev, squares, scale, bias, out_ref, sems):
    rows = st_ref.shape[0]
    half = vp0_ref.shape[0] - 1
    width = prev.shape[0] * LANES
    odd = facts_ref[ODD] == 1
    shared = facts_ref[BEFORE] > rows

    @pl.when(odd)
    def _():
        squares[...] = sq_ref[...]

        @pl.loop(0, 2 * half)
        def _(h):
            prev[h] = near_ref[h]

    @pl.when(jnp.logical_not(odd) & shared)
    def _():
        squares[...] = jnp.zeros_like(squares)

        def heads(first):
            total = squares[...]
            for h in range(UNROLL):
                a = c_ref[:, columns(first + h)]
                prev[first + h] = a
                a = a.astype(jnp.float32)
                total += a * a
            squares[...] = total

        each(2 * half, heads)

    @pl.when(jnp.logical_not(odd) & jnp.logical_not(shared))
    def _():
        squares[...] = jnp.zeros_like(squares)
        bias[...] = bias_of(rows, rows, -rows, -rows, st_ref[0:1, :])
        for part, vp_ref in enumerate((vp0_ref, vp1_ref)):

            def heads(first):
                at = lambda h: columns(part * half + first + h)
                total = [squares[...]]

                def use(h, o, l, top):
                    a = (o / l).astype(jnp.bfloat16)
                    prev[part * half + first + h] = a
                    a = a.astype(jnp.float32)
                    total[0] += a * a

                attend(UNROLL, lambda h: c_ref[:, at(h)], lambda h: kp_ref[:, at(h)], lambda h: vp_ref[first + h], bias[...], use)
                squares[...] = total[0]

            each(half, heads)

    scale[...] = scale_of(squares[...], width)

    def chunk(first):
        cols = pl.ds(pl.multiple_of(first * LANES, UNROLL * LANES), UNROLL * LANES)
        return pltpu.make_async_copy(out_ref.at[:, cols], out_hbm.at[:, cols], sems.at[first // UNROLL])

    def tiles(first):
        for c in range(UNROLL):
            cols = columns(first + c)
            x = (prev[first + c].astype(jnp.float32) * scale[...] * gain_ref[:, cols]).astype(jnp.bfloat16)
            y = jnp.dot(taps_ref[first + c], spread(x, taps_ref.shape[2] // rows), preferred_element_type=jnp.float32)
            out_ref[:, cols] = (y + jnp.where(odd, odd_ref[:, cols], even_ref[:, cols])).astype(jnp.bfloat16)

        chunk(first).start()

    each(2 * half, tiles)
    each(2 * half, lambda first: chunk(first).wait())


def run(kernel, name, facts, out_shape, scratch, args, out_space=pltpu.VMEM):
    many = isinstance(out_shape, tuple)
    vmem = pl.BlockSpec(memory_space=pltpu.VMEM)
    return pl.pallas_call(
        kernel,
        out_shape=out_shape,
        in_specs=[pl.BlockSpec(memory_space=pltpu.SMEM)] + [vmem] * len(args),
        out_specs=(vmem,) * len(out_shape) if many else pl.BlockSpec(memory_space=out_space),
        scratch_shapes=scratch,
        compiler_params=pltpu.CompilerParams(vmem_limit_bytes=VMEM_BYTES),
        cost_estimate=pl.CostEstimate(flops=2**20, bytes_accessed=2**16, transcendentals=0),
        name=name,
    )(facts, *args)


def shards(queries, key_rows, value_rows, lengths, norm_gain, filters, bypass):
    rows, width = queries.shape
    heads = width // HEAD_DIM
    half = heads // 2
    groups, taps = filters.shape
    n = lax.axis_size("ctx")
    st, facts = places(lengths, lax.axis_index("ctx") * rows, rows)

    back = [(i, i - 1) for i in range(2, n, 2)]
    within = [(i, i + 1) for i in range(0, n - 1, 2)]
    across = [(i, i + 1) for i in range(1, n - 1, 2)]

    bf16 = lambda *shape: jax.ShapeDtypeStruct(shape, jnp.bfloat16)
    f32 = lambda *shape: jax.ShapeDtypeStruct(shape, jnp.float32)

    query_back = permuted(queries, back)
    key_near = permuted(key_rows, within)
    value_near = permuted(value_rows, within)
    query_near = permuted(queries, within)

    taps_far, taps_near = run(
        taps_kernel,
        "taps",
        facts,
        (bf16(heads, rows, groups // heads * rows),) * 2,
        [pltpu.VMEM((rows, 2 * rows), jnp.bfloat16), pltpu.VMEM((heads, groups // heads, taps), jnp.float32)],
        (st, filters),
    )
    key_across = permuted(after(key_rows, facts), across)

    slot_b0, slot_b1 = run(
        slot_b_kernel,
        "slot_b",
        after(facts, taps_far, query_near),
        (bf16(half + 1, rows, HEAD_DIM), bf16(half + 1, rows, HEAD_DIM)),
        [pltpu.VMEM((rows, 2 * rows), jnp.float32), pltpu.VMEM((rows, LANES), jnp.float32)],
        (query_back, key_near, key_rows, value_near, value_rows),
    )
    slot_c = run(
        slot_c_kernel,
        "slot_c",
        after(facts, slot_b1),
        bf16(rows, width),
        [pltpu.VMEM((rows, 2 * rows), jnp.float32)],
        (queries, key_near, key_rows, value_near, value_rows),
    )
    b_across = [permuted(x, across) for x in (slot_b0, slot_b1)]
    c_across = permuted(slot_c, across)
    key_far = permuted(after(key_across, slot_c), within)
    value_far = [permuted(x, within) for x in b_across]

    gain = norm_gain.reshape(1, width)
    skip = bypass.reshape(1, width)
    own_scratch = [
        pltpu.VMEM((heads, rows, HEAD_DIM), jnp.bfloat16),
        pltpu.VMEM((rows, LANES), jnp.float32),
        pltpu.VMEM((rows, LANES), jnp.float32),
    ]
    three, two, even_part = run(
        even_kernel,
        "even",
        facts,
        (bf16(heads, rows, 3 * rows), bf16(heads, rows, 2 * rows), f32(rows, width)),
        own_scratch + [pltpu.VMEM((rows, 3 * rows), jnp.float32), pltpu.VMEM((rows, 2 * rows), jnp.float32)],
        (st, queries, key_rows, value_rows, key_across, *b_across, query_near, key_near, key_far, taps_near, gain, skip),
    )
    near, near_squares, odd_part = run(
        odd_kernel,
        "odd",
        facts,
        (bf16(heads, rows, HEAD_DIM), f32(rows, LANES), f32(rows, width)),
        own_scratch,
        (three, two, value_rows, value_near, *value_far, taps_near, gain, skip),
    )
    return run(
        finish_kernel,
        "finish",
        facts,
        bf16(rows, width),
        [
            pltpu.VMEM((heads, rows, LANES), jnp.bfloat16),
            pltpu.VMEM((rows, LANES), jnp.float32),
            pltpu.VMEM((rows, LANES), jnp.float32),
            pltpu.VMEM((rows, rows), jnp.float32),
            pltpu.VMEM((rows, width), jnp.bfloat16),
            pltpu.SemaphoreType.DMA((heads // UNROLL,)),
        ],
        (st, key_across, *b_across, c_across, near, near_squares, even_part, odd_part, taps_far, gain),
        pl.ANY,
    )


def solution(mesh):
    rows = P(("dp", "ctx"), None)
    in_specs = (rows, rows, rows, P("dp"), P(), P(), P())
    return jax.shard_map(shards, mesh=mesh, in_specs=in_specs, out_specs=rows, check_vma=False)
```
